32 devices in a mesh: ctx: 16 (over z, y, core), ch: 2 (over x).
Axes of the slice: x: 2, y: 2, z: 4, core: 2. Of those that a mesh axis runs over, the one named last changes fastest.
Arguments:
- streams: bfloat16 [8192, 3, 2048], P('ctx', None, 'ch'), may hold values from -6 to 6
- short_taps: float32 [3, 3, 2048], P(None, None, 'ch'), may hold values from -3 to 3
- filters: bfloat16 [8192, 2048], P('ctx', 'ch'), may hold values from -1 to 1, as said below
- skip_gain: float32 [2048], P('ch'), may hold values from 0.2 to 0.6
- out_weight: bfloat16 [2048, 4096], P('ch'), may hold values from -0.1875 to 0.1875
Outputs:
- output: bfloat16 [8192, 4096], P('ctx', 'ch')
The draws below stay inside these ranges and needn't reach their ends.
Inputs may be any that keep to these rules, and one draw needn't show every extreme that they name: `filters`: filter taps of every channel and lag.
All inputs are finite; a program needn't handle non-finite values.
Results may differ from the reference program's by a relative error of at most 0.017.
Values may be sent and summed in bfloat16 or wider, within the bound.
No kernel may reach another device: no remote copies, remote signals or barrier semaphores. Data moves between devices by JAX's collectives and lax.ppermute only.
A program may use at most 192 MiB of HBM per device.

```python
import math
import jax
import jax.numpy as jnp
from jax import lax

D = 4096
CHAN = 2048
SEG = 512
TOKEN_LENGTH = 8192
N_CTX = 16
N_CH = 2


def draw_filters(key, part):
    base_key = jax.random.fold_in(key, 7)
    random_subkeys = jax.random.split(base_key, 6)
    delay_offsets = jnp.arange(TOKEN_LENGTH, dtype=jnp.float32)[:, None]
    random_noise = jnp.clip(jax.random.normal(random_subkeys[0], (TOKEN_LENGTH, CHAN), jnp.float32), -6.0, 6.0)
    fast_share = 0.25
    fast_mask = jax.random.uniform(random_subkeys[1], (1, CHAN), jnp.float32) < fast_share
    fast_rate = jnp.exp(jax.random.uniform(random_subkeys[2], (1, CHAN), jnp.float32, math.log(math.log(10.0) / 50.0), math.log(math.log(10.0) / 30.0)))
    slow_rate = jnp.exp(jax.random.uniform(random_subkeys[3], (1, CHAN), jnp.float32, math.log(0.02), math.log(0.2))) / TOKEN_LENGTH
    falloff_speed = jnp.where(fast_mask, fast_rate, slow_rate)
    signal_power = jnp.expm1(-2.0 * falloff_speed * TOKEN_LENGTH) / jnp.expm1(-2.0 * falloff_speed)
    spike_position = jax.random.randint(random_subkeys[4], (2,), 0, TOKEN_LENGTH)
    spike_retained = jax.random.uniform(random_subkeys[5], (2,), jnp.float32, 0.65, 0.8)
    spike_multiplier = jnp.ones((TOKEN_LENGTH, 1), jnp.float32)
    for index_vector in range(2):
        spike_multiplier = spike_multiplier * jnp.where(delay_offsets >= spike_position[index_vector].astype(jnp.float32), spike_retained[index_vector], 1.0)
    value_entries = random_noise * jnp.exp(-falloff_speed * delay_offsets) * spike_multiplier / jnp.sqrt(signal_power)
    return jnp.clip(value_entries, -1.0, 1.0).astype(jnp.bfloat16)


def with_spikes(entries, rng, source, target, blocks, factor):
    def block_of(position):
        return (jnp.arange(entries.shape[position]) // (entries.shape[position] // blocks)).reshape((-1,) + (1,) * (entries.ndim - 1 - position))

    one_side = jax.random.permutation(rng, blocks)[block_of(target)]
    far = (block_of(target) + blocks // 2) % blocks
    return jnp.where((block_of(source) == one_side) | (block_of(source) == far), factor * entries, entries)


def levels(rng, dims, pieces, low, high):
    gain = 1.0
    for position, shards_of in pieces:
        heights = jax.random.uniform(jax.random.fold_in(jax.random.fold_in(rng, 6), position), (shards_of,), jnp.float32, low / len(pieces), high / len(pieces))
        gain = gain * jnp.repeat(jnp.exp(heights), dims[position] // shards_of).reshape((-1,) + (1,) * (len(dims) - 1 - position))
    return gain


def scatter_about(rng, extent, scale, most, pieces=(), kind=jnp.bfloat16):
    loudness = levels(rng, extent, pieces, -0.22, 0.18) if pieces else 1.0
    drawn = jax.random.normal(rng, extent, jnp.float32) * scale * loudness
    return jnp.minimum(jnp.maximum(drawn, -most), most).astype(kind)


def heavy_noise(key, dims, scale, most, shards, heavy, kind=jnp.bfloat16):
    entries = scale * jax.random.normal(key, dims, jnp.float32)
    if shards:
        entries = entries * levels(key, dims, shards, -0.22, 0.18)
    return jnp.clip(with_spikes(entries, jax.random.fold_in(key, 3), *heavy), -most, most).astype(kind)


def setup_inputs(seed: int = 0) -> dict:
    key_of = jax.random.split(jax.random.key(seed), 6)
    return {
        "streams": scatter_about(key_of[0], (TOKEN_LENGTH, 3, CHAN), 1.0, 6.0, ((0, 16), (2, 2))),
        "short_taps": scatter_about(key_of[1], (3, 3, CHAN), 0.6, 3.0, ((2, 2),), jnp.float32),
        "filters": draw_filters(jax.random.fold_in(key_of[5], 71), 0),
        "skip_gain": jnp.clip(0.2 + 0.400000021 * jax.random.uniform(key_of[3], (CHAN,), jnp.float32) ** levels(key_of[3], (CHAN,), ((0, 2),), -0.2, 0.2), 0.2, 0.6),
        "out_weight": heavy_noise(key_of[4], (CHAN, D), CHAN ** -0.5, 0.1875, ((0, 2),), (0, 1, 2, 2.0)),
    }


def forward_table(size):
    half = size // 2
    rows = jnp.arange(size, dtype=jnp.int32)[:, None]
    cols = jnp.arange(size, dtype=jnp.int32)[None, :]
    freq = jnp.where(cols < half, cols, cols - half)
    phase = (rows * freq) % size
    angle = phase.astype(jnp.float32) * (2.0 * math.pi / size)
    cosine = jnp.cos(angle)
    sine = -jnp.sin(angle)
    nyquist = jnp.where(rows % 2 == 0, 1.0, -1.0).astype(jnp.float32)
    table = jnp.where(cols < half, cosine, jnp.where(cols == half, nyquist, sine))
    return table.astype(jnp.bfloat16)


def inverse_table(size):
    half = size // 2
    rows = jnp.arange(size, dtype=jnp.int32)[:, None]
    places = half + jnp.arange(half, dtype=jnp.int32)[None, :]
    freq = jnp.where(rows < half, rows, rows - half)
    phase = (places * freq) % size
    angle = phase.astype(jnp.float32) * (2.0 * math.pi / size)
    weight = jnp.where(freq == 0, 1.0, 2.0).astype(jnp.float32) / size
    cosine = weight * jnp.cos(angle)
    sine = -weight * jnp.sin(angle)
    nyquist = jnp.where(places % 2 == 0, 1.0, -1.0).astype(jnp.float32) / size
    table = jnp.where(rows < half, cosine, jnp.where(rows == half, nyquist, sine))
    return table.astype(jnp.bfloat16)


def spectrum_product(left, right):
    half = left.shape[-1] // 2
    right = right.astype(jnp.float32)
    left_re, left_im = left[..., :half], left[..., half:]
    right_re, right_im = right[..., :half], right[..., half:]
    inside = jnp.arange(half, dtype=jnp.int32) > 0
    real_part = left_re * right_re - jnp.where(inside, left_im * right_im, 0.0)
    imag_part = jnp.where(inside, left_re * right_im + left_im * right_re, left_im * right_im)
    return jnp.concatenate([real_part, imag_part], axis=-1)


def reference(streams, short_taps, filters, skip_gain, out_weight):
    seq_len = streams.shape[0]
    width = 2 * SEG
    padded = jnp.concatenate([jnp.zeros((2, 3, CHAN), streams.dtype), streams], axis=0)
    mixed = short_taps[0][None] * padded[2:].astype(jnp.float32)
    mixed = mixed + short_taps[1][None] * padded[1:seq_len + 1].astype(jnp.float32)
    mixed = mixed + short_taps[2][None] * padded[:seq_len].astype(jnp.float32)
    inner = (mixed[:, 0, :] * mixed[:, 1, :]).astype(jnp.bfloat16)
    forward = forward_table(width)
    backward = inverse_table(width)
    filt_blocks = filters.reshape(N_CTX, SEG, CHAN)
    earlier = jnp.concatenate([jnp.zeros((1, SEG, CHAN), filters.dtype), filt_blocks[:-1]], axis=0)
    windows = jnp.concatenate([earlier, filt_blocks], axis=1)
    filter_spectrum = jnp.einsum("nmc,mf->ncf", windows.astype(jnp.float32), forward.astype(jnp.float32)).astype(jnp.bfloat16)
    in_blocks = inner.reshape(N_CTX, SEG, CHAN)
    input_spectrum = jnp.einsum("nbc,bf->ncf", in_blocks.astype(jnp.float32), forward[:SEG].astype(jnp.float32))

    def one_block(target):
        def add_tile(source, total):
            return total + spectrum_product(input_spectrum[source], filter_spectrum[target - source])
        accumulated = lax.fori_loop(0, target + 1, add_tile, jnp.zeros((CHAN, width), jnp.float32))
        spectrum_low = accumulated.astype(jnp.bfloat16)
        return jnp.dot(spectrum_low, backward, preferred_element_type=jnp.float32).astype(jnp.bfloat16)

    long_blocks = lax.map(one_block, jnp.arange(N_CTX, dtype=jnp.int32))
    long_conv = jnp.transpose(long_blocks, (0, 2, 1)).reshape(seq_len, CHAN)
    gated = (mixed[:, 2, :] * (long_conv.astype(jnp.float32) + skip_gain[None, :] * inner.astype(jnp.float32))).astype(jnp.bfloat16)
    group = CHAN // N_CH
    summed = jnp.zeros((seq_len, D), jnp.float32)
    for index_vector in range(N_CH):
        partial_term = jnp.dot(gated[:, index_vector * group:(index_vector + 1) * group], out_weight[index_vector * group:(index_vector + 1) * group], preferred_element_type=jnp.float32)
        summed = summed + partial_term.astype(jnp.bfloat16).astype(jnp.float32)
    return summed.astype(jnp.bfloat16)
```

```python
import functools

import jax
import jax.numpy as jnp
import ml_dtypes
import numpy as np
from jax import lax
from jax.experimental import pallas as pl
from jax.experimental.pallas import tpu as pltpu
from jax.sharding import PartitionSpec as P

LANES = 128
VMEM_BYTES = 48 * 1024 * 1024


def passed_along(value, axis, steps):
    count = lax.axis_size(axis)
    initial, last = (max(0, -steps), min(count, count - steps))
    return lax.ppermute(value, axis, [(source, source + steps) for source in range(initial, last)])


def paired_columns(half):
    order = np.arange(2 * half).reshape(2, half // LANES, LANES)
    return order.transpose(1, 0, 2).reshape(-1)


def head_table(size):
    half = size // 2
    rows = np.arange(half)[:, None]
    cols = np.arange(size)[None, :]
    freq = np.where(cols < half, cols, cols - half)
    angle = (rows * freq % size) * (2.0 * np.pi / size)
    nyquist = np.where(rows % 2 == 0, 1.0, -1.0)
    table = np.where(cols < half, np.cos(angle), np.where(cols == half, nyquist, -np.sin(angle)))
    return table[:, paired_columns(half)].astype(ml_dtypes.bfloat16)


def inverse_table(size):
    half = size // 2
    rows = np.arange(size)[:, None]
    places = half + np.arange(half)[None, :]
    freq = np.where(rows < half, rows, rows - half)
    angle = (places * freq % size) * (2.0 * np.pi / size)
    weight = np.where(freq == 0, 1.0, 2.0) / size
    nyquist = np.where(places % 2 == 0, 1.0, -1.0) / size
    table = np.where(
        rows < half, weight * np.cos(angle), np.where(rows == half, nyquist, -weight * np.sin(angle))
    )
    return table[paired_columns(half)].astype(ml_dtypes.bfloat16)


def call(kernel, grid, in_specs, out_specs, out_shape, scratch=(), flops=0, moved=0):
    return pl.pallas_call(
        kernel,
        grid=grid,
        in_specs=in_specs,
        out_specs=out_specs,
        out_shape=out_shape,
        scratch_shapes=list(scratch),
        compiler_params=pltpu.CompilerParams(vmem_limit_bytes=VMEM_BYTES),
        cost_estimate=pl.CostEstimate(flops=flops, bytes_accessed=moved, transcendentals=0),
    )


def turn_kernel(x_ref, o_ref):
    o_ref[...] = x_ref[...].astype(jnp.float32).T.astype(o_ref.dtype)


def turned(x, tile):
    rows, chan = x.shape
    return call(
        turn_kernel,
        (chan // tile,),
        [pl.BlockSpec((rows, tile), lambda c: (0, c))],
        pl.BlockSpec((tile, rows), lambda c: (c, 0)),
        jax.ShapeDtypeStruct((chan, rows), x.dtype),
        moved=4 * rows * chan,
    )(x)


def mix_kernel(s_ref, e_ref, t_ref, inner_ref, turned_ref, outer_ref):
    rows, width = s_ref.shape[1:]
    place = lax.broadcasted_iota(jnp.int32, (rows, width), 0)

    def mixed(q):
        now = s_ref[q].astype(jnp.float32)
        edge = e_ref[q].astype(jnp.float32)
        one = jnp.where(place == 0, edge[1:2], pltpu.roll(now, 1, 0))
        two = jnp.where(
            place == 0, edge[0:1], jnp.where(place == 1, edge[1:2], pltpu.roll(now, 2, 0))
        )
        return t_ref[0, q : q + 1] * now + t_ref[1, q : q + 1] * one + t_ref[2, q : q + 1] * two

    inner = mixed(0) * mixed(1)
    inner_ref[...] = inner.astype(inner_ref.dtype)
    turned_ref[...] = inner.T.astype(turned_ref.dtype)
    outer_ref[...] = mixed(2)


def mix(streams, edges, taps, tile):
    _, rows, chan = streams.shape
    return call(
        mix_kernel,
        (chan // tile,),
        [
            pl.BlockSpec((3, rows, tile), lambda c: (0, 0, c)),
            pl.BlockSpec((3, 2, tile), lambda c: (0, 0, c)),
            pl.BlockSpec((3, 3, tile), lambda c: (0, 0, c)),
        ],
        [
            pl.BlockSpec((rows, tile), lambda c: (0, c)),
            pl.BlockSpec((tile, rows), lambda c: (c, 0)),
            pl.BlockSpec((rows, tile), lambda c: (0, c)),
        ],
        [
            jax.ShapeDtypeStruct((rows, chan), jnp.bfloat16),
            jax.ShapeDtypeStruct((chan, rows), jnp.bfloat16),
            jax.ShapeDtypeStruct((rows, chan), jnp.float32),
        ],
        moved=14 * rows * chan,
    )(streams, edges, taps)


def filter_kernel(own, f_ref, table_ref, one_ref, two_ref, three_ref):
    spectrum = jnp.dot(f_ref[...], table_ref[...], preferred_element_type=jnp.float32)
    lane = lax.broadcasted_iota(jnp.int32, spectrum.shape, 1)
    signed = jnp.where(lane % 2 == 0, spectrum, -spectrum)
    nyquist = (pl.program_id(0) == 0) & (lane == LANES)
    signed = jnp.where(nyquist, spectrum, signed)
    earlier = jnp.concatenate([jnp.zeros((own, 2 * LANES), jnp.float32), spectrum[:-own]], axis=0)
    window = (earlier + signed).astype(jnp.bfloat16).astype(jnp.float32)
    real, imag = (window[:, :LANES], window[:, LANES:])
    first = (pl.program_id(0) == 0) & (lax.broadcasted_iota(jnp.int32, real.shape, 1) == 0)
    one_ref[...] = real
    two_ref[...] = jnp.where(first, real, imag - real)
    three_ref[...] = jnp.where(first, imag, real + imag)


def filter_factors(blocks, table, own):
    height, rows = blocks.shape
    tiles = rows // LANES
    factor = jax.ShapeDtypeStruct((height, rows), jnp.float32)
    spec = pl.BlockSpec((height, LANES), lambda f: (0, f))
    return call(
        functools.partial(filter_kernel, own),
        (tiles,),
        [
            pl.BlockSpec((height, rows), lambda f: (0, 0)),
            pl.BlockSpec((rows, 2 * LANES), lambda f: (0, f)),
        ],
        [spec, spec, spec],
        [factor, factor, factor],
        flops=4 * height * rows * rows,
        moved=height * rows * 14,
    )(blocks, table)


def conv_kernel(count, own, x_ref, head_ref, one_ref, two_ref, three_ref, back_ref, o_ref, spec_ref, low_ref, sum_ref):
    step = pl.program_id(0)
    spec_ref[...] = jnp.dot(x_ref[...], head_ref[...], preferred_element_type=jnp.float32)
    high = 8
    group = 4
    first = (step == 0) & (lax.broadcasted_iota(jnp.int32, (high, LANES), 1) == 0)

    def one_slab(slab, carry):
        base = pl.multiple_of(slab * high, high)

        def at(ref, block, col=0):
            return ref[pl.ds(base + block * own, high), col : col + LANES]

        for low in range(0, count, group):
            sums = [[None] * 3 for _ in range(group)]
            for source in range(low + group):
                real = at(spec_ref, source)
                imag = at(spec_ref, source, LANES)
                both = real + imag
                for g in range(group):
                    lag = low + g - source
                    if lag < 0:
                        continue
                    terms = (
                        both * at(one_ref, lag),
                        real * at(two_ref, lag),
                        imag * at(three_ref, lag),
                    )
                    for k in range(3):
                        sums[g][k] = terms[k] if sums[g][k] is None else sums[g][k] + terms[k]
            for g in range(group):
                a, b, c = sums[g]
                place = pl.ds(base + (low + g) * own, high)
                low_ref[place, :LANES] = jnp.where(first, b, a - c)
                low_ref[place, LANES:] = jnp.where(first, c, a + b)
        return carry

    lax.fori_loop(0, own // high, one_slab, 0)
    term = jnp.dot(
        low_ref[...].astype(jnp.bfloat16), back_ref[...], preferred_element_type=jnp.float32
    )

    @pl.when(step == 0)
    def _():
        sum_ref[...] = term

    @pl.when(step > 0)
    def _():
        sum_ref[...] += term

    @pl.when(step == pl.num_programs(0) - 1)
    def _():
        o_ref[...] = sum_ref[...].astype(o_ref.dtype)


def long_conv(blocks, head, factors, back, count, own):
    height, rows = blocks.shape
    spec = pl.BlockSpec((height, LANES), lambda f: (0, f))
    return call(
        functools.partial(conv_kernel, count, own),
        (rows // LANES,),
        [
            pl.BlockSpec((height, rows), lambda f: (0, 0)),
            pl.BlockSpec((rows, 2 * LANES), lambda f: (0, f)),
            spec,
            spec,
            spec,
            pl.BlockSpec((2 * LANES, rows), lambda f: (f, 0)),
        ],
        pl.BlockSpec((height, rows), lambda f: (0, 0)),
        jax.ShapeDtypeStruct((height, rows), jnp.bfloat16),
        scratch=[
            pltpu.VMEM((height, 2 * LANES), jnp.float32),
            pltpu.VMEM((height, 2 * LANES), jnp.float32),
            pltpu.VMEM((height, rows), jnp.float32),
        ],
        flops=8 * height * rows * rows,
        moved=height * rows * 16,
    )(blocks, head, *factors, back)


def gate_kernel(long_ref, inner_ref, outer_ref, skip_ref, o_ref):
    value = long_ref[...].astype(jnp.float32).T
    value = value + skip_ref[...] * inner_ref[...].astype(jnp.float32)
    o_ref[...] = (outer_ref[...] * value).astype(o_ref.dtype)


def gate(turned_long, inner, outer, skip, tile):
    chan, rows = turned_long.shape
    spec = pl.BlockSpec((rows, tile), lambda c: (0, c))
    return call(
        gate_kernel,
        (chan // tile,),
        [pl.BlockSpec((tile, rows), lambda c: (c, 0)), spec, spec, pl.BlockSpec((1, tile), lambda c: (0, c))],
        spec,
        jax.ShapeDtypeStruct((rows, chan), jnp.bfloat16),
        moved=10 * rows * chan,
    )(turned_long, inner, outer, skip)


def exchanged(value):
    return lax.all_to_all(value, "ctx", 0, 0, tiled=True)


def weights_of(out_weight):
    chan, width = out_weight.shape
    groups = lax.axis_size("ch")
    count = lax.axis_size("ctx")
    here = lax.axis_index("ch")
    core = lax.axis_index("ctx") % 2
    cols = width // groups
    half = chan // 2
    pieces = [lax.dynamic_slice(out_weight, (0, here * cols), (chan, cols))]
    for step in range(1, groups):
        target = (here + step) % groups
        part = lax.dynamic_slice(out_weight, (core * half, target * cols), (half, cols))
        mine = lax.ppermute(part, "ch", [(g, (g + step) % groups) for g in range(groups)])
        other = lax.ppermute(mine, "ctx", [(i, i ^ 1) for i in range(count)])
        low = jnp.where(core == 0, mine, other)
        high = jnp.where(core == 0, other, mine)
        pieces.append(jnp.concatenate([low, high], axis=0))
    return pieces


def local(streams, short_taps, filters, skip_gain, out_weight):
    rows, _, chan = streams.shape
    count = lax.axis_size("ctx")
    groups = lax.axis_size("ch")
    own = chan // count
    tile = min(chan, 256)
    head = jnp.asarray(head_table(2 * rows))
    back = jnp.asarray(inverse_table(2 * rows))
    edges = passed_along(streams[rows - 2 :], "ctx", 1)
    filter_blocks = exchanged(turned(filters, tile))
    inner, turned_inner, outer = mix(
        streams.transpose(1, 0, 2), edges.transpose(1, 0, 2), short_taps, tile
    )
    inner_blocks = exchanged(turned_inner)
    factors = filter_factors(filter_blocks, head, own)
    weights = weights_of(out_weight)
    turned_long = exchanged(long_conv(inner_blocks, head, factors, back, count, own))
    gated = gate(turned_long, inner, outer, skip_gain[None], tile)
    total = jnp.dot(gated, weights[0], preferred_element_type=jnp.float32)
    for step in range(1, groups):
        arrived = lax.ppermute(gated, "ch", [(g, (g + step) % groups) for g in range(groups)])
        total = total + jnp.dot(arrived, weights[step], preferred_element_type=jnp.float32)
    return total.astype(jnp.bfloat16)


def solution(mesh):
    return jax.shard_map(
        local,
        mesh=mesh,
        in_specs=(
            P("ctx", None, "ch"),
            P(None, None, "ch"),
            P("ctx", "ch"),
            P("ch"),
            P("ch", None),
        ),
        out_specs=P("ctx", "ch"),
        check_vma=False,
    )
```

```python
import functools

import jax
import jax.numpy as jnp
import ml_dtypes
import numpy as np
from jax import lax
from jax.experimental import pallas as pl
from jax.experimental.pallas import tpu as pltpu
from jax.sharding import PartitionSpec as P

LANES = 128


def passed_along(value, axis, steps):
    count = lax.axis_size(axis)
    initial, last = (max(0, -steps), min(count, count - steps))
    return lax.ppermute(value, axis, [(source, source + steps) for source in range(initial, last)])


def paired_columns(half):
    order = np.arange(2 * half).reshape(2, half // LANES, LANES)
    return order.transpose(1, 0, 2).reshape(-1)


def head_table(size):
    half = size // 2
    rows = np.arange(half)[:, None]
    cols = np.arange(size)[None, :]
    freq = np.where(cols < half, cols, cols - half)
    angle = (rows * freq % size) * (2.0 * np.pi / size)
    nyquist = np.where(rows % 2 == 0, 1.0, -1.0)
    table = np.where(cols < half, np.cos(angle), np.where(cols == half, nyquist, -np.sin(angle)))
    return table[:, paired_columns(half)].astype(ml_dtypes.bfloat16)


def inverse_table(size):
    half = size // 2
    rows = np.arange(size)[:, None]
    places = half + np.arange(half)[None, :]
    freq = np.where(rows < half, rows, rows - half)
    angle = (places * freq % size) * (2.0 * np.pi / size)
    weight = np.where(freq == 0, 1.0, 2.0) / size
    nyquist = np.where(places % 2 == 0, 1.0, -1.0) / size
    table = np.where(
        rows < half, weight * np.cos(angle), np.where(rows == half, nyquist, -weight * np.sin(angle))
    )
    return table[paired_columns(half)].astype(ml_dtypes.bfloat16)


def call(kernel, in_specs, out_specs, outs, grid=(), scratch=(), megabytes=16, flops=0, moved=0, scalars=0):
    inner = pl.pallas_call(
        kernel,
        grid_spec=pltpu.PrefetchScalarGridSpec(
            num_scalar_prefetch=scalars,
            grid=grid,
            in_specs=in_specs,
            out_specs=out_specs,
            scratch_shapes=list(scratch),
        ),
        out_shape=[pltpu.HBM(shape, dtype) for shape, dtype in outs],
        compiler_params=pltpu.CompilerParams(vmem_limit_bytes=megabytes * 1024 * 1024),
        cost_estimate=pl.CostEstimate(flops=flops, bytes_accessed=moved, transcendentals=0),
    )

    def run(*args, free=()):
        pinned = [
            a if k < scalars or k in free else pltpu.with_memory_space_constraint(a, pltpu.HBM)
            for k, a in enumerate(args)
        ]
        return inner(*pinned)

    return run


def store_turned(value, o_ref, parts):
    count, held, rows = o_ref.shape
    step = held // parts
    tile = value.shape[1] // parts
    value = value.T
    for p in range(parts):
        piece = value[p * tile : (p + 1) * tile].reshape(count, step, rows)
        o_ref[:, p * step : (p + 1) * step] = piece.astype(o_ref.dtype)


def turn_kernel(parts, x_ref, s_ref, o_ref, tail_ref):
    tail_ref[...] = s_ref[:, s_ref.shape[1] - 2 :]
    store_turned(x_ref[...].astype(jnp.float32), o_ref, parts)


def turned(x, streams, count, parts):
    rows, chan = x.shape
    own = chan // count
    grid = min(parts, 2)
    last = min(rows, 16)
    tile = chan // grid
    return call(
        functools.partial(turn_kernel, parts // grid),
        [
            pl.BlockSpec((rows, tile), lambda p: (0, p)),
            pl.BlockSpec((3, last, tile), lambda p: (0, rows // last - 1, p)),
        ],
        [
            pl.BlockSpec((count, own // grid, rows), lambda p: (0, p, 0)),
            pl.BlockSpec((3, 2, tile), lambda p: (0, 0, p)),
        ],
        [((count, own, rows), x.dtype), ((3, 2, chan), streams.dtype)],
        grid=(grid,),
        moved=4 * rows * chan,
    )(x, streams)


def mix_kernel(parts, s_ref, e_ref, t_ref, turned_ref, outer_ref):
    rows, width = s_ref.shape[1:]
    place = lax.broadcasted_iota(jnp.int32, (rows, width), 0)

    def mixed(q):
        now = s_ref[q].astype(jnp.float32)
        edge = e_ref[q].astype(jnp.float32)
        one = jnp.where(place == 0, edge[1:2], pltpu.roll(now, 1, 0))
        two = jnp.where(
            place == 0, edge[0:1], jnp.where(place == 1, edge[1:2], pltpu.roll(now, 2, 0))
        )
        return t_ref[0, q : q + 1] * now + t_ref[1, q : q + 1] * one + t_ref[2, q : q + 1] * two

    outer_ref[...] = mixed(2).astype(outer_ref.dtype)
    store_turned(mixed(0) * mixed(1), turned_ref, parts)


def mix(streams, edges, taps, count, parts):
    _, rows, chan = streams.shape
    own = chan // count
    grid = min(parts, 2)
    tile = chan // grid
    return call(
        functools.partial(mix_kernel, parts // grid),
        [
            pl.BlockSpec((3, rows, tile), lambda p: (0, 0, p)),
            pl.BlockSpec((3, 2, tile), lambda p: (0, 0, p)),
            pl.BlockSpec((3, 3, tile), lambda p: (0, 0, p)),
        ],
        [
            pl.BlockSpec((count, own // grid, rows), lambda p: (0, p, 0)),
            pl.BlockSpec((rows, tile), lambda p: (0, p)),
        ],
        [((count, own, rows), jnp.bfloat16), ((rows, chan), jnp.bfloat16)],
        grid=(grid,),
        megabytes=32,
        moved=10 * rows * chan,
    )(streams, edges, taps)


def filter_kernel(own, f_ref, table_ref, real_ref, imag_ref):
    spectrum = jnp.dot(f_ref[...], table_ref[...], preferred_element_type=jnp.float32)
    lane = lax.broadcasted_iota(jnp.int32, spectrum.shape, 1)
    nyquist = (pl.program_id(0) == 0) & (lane == LANES)
    signed = jnp.where((lane % 2 == 0) | nyquist, spectrum, -spectrum)
    earlier = jnp.concatenate([jnp.zeros((own, 2 * LANES), jnp.float32), spectrum[:-own]], axis=0)
    window = (earlier + signed).astype(jnp.bfloat16).astype(jnp.float32)
    real_ref[...] = window[:, :LANES]
    imag_ref[...] = window[:, LANES:]


def filter_spectra(blocks, table):
    count, own, rows = blocks.shape
    height = count * own
    plane = ((height, rows), jnp.float32)
    spec = pl.BlockSpec((height, LANES), lambda f: (0, f))
    return call(
        functools.partial(filter_kernel, own),
        [
            pl.BlockSpec((height, rows), lambda f: (0, 0)),
            pl.BlockSpec((rows, 2 * LANES), lambda f: (0, f)),
        ],
        [spec, spec],
        [plane, plane],
        grid=(rows // LANES,),
        flops=4 * height * rows * rows,
        moved=height * rows * 10,
    )(blocks.reshape(height, rows), table)


def conv_kernel(low, x_ref, head_ref, real_ref, imag_ref, back_ref, skip_ref, o_ref, *scratch):
    head_buf, real_buf, imag_buf, back_buf, spec_ref, low_ref, sems = scratch
    count, _, part, rows = o_ref.shape
    high = min(part, 16)
    group = 2
    some = pl.ds(low, part)
    pairs = [
        (head_ref, head_buf),
        (real_ref.at[:, some], real_buf),
        (imag_ref.at[:, some], imag_buf),
        (back_ref, back_buf),
    ]
    copies = [pltpu.make_async_copy(a, b, sems.at[i]) for i, (a, b) in enumerate(pairs)]
    for copy in copies:
        copy.start()
    copies[0].wait()
    x = x_ref[:, low : low + part]
    blocks = x.reshape(count * part, rows)
    spec_ref[...] = jnp.dot(blocks, head_buf[...], preferred_element_type=jnp.float32)
    for copy in copies[1:]:
        copy.wait()
    lane = lax.broadcasted_iota(jnp.int32, (high, LANES), 1)
    slabs = part // high

    def one_slab(turn, carry):
        tile = turn // slabs
        base = pl.multiple_of((turn % slabs) * high, high)
        column = pl.ds(pl.multiple_of(tile * LANES, LANES), LANES)
        reals = pl.ds(pl.multiple_of(tile * 2 * LANES, LANES), LANES)
        imags = pl.ds(pl.multiple_of(tile * 2 * LANES + LANES, LANES), LANES)
        first = (lane == 0) & (tile == 0)
        for start in range(0, count, group):
            sums = [[None] * 3 for _ in range(group)]
            factors = {}
            for source in range(start + group):
                place = pl.ds(base + source * part, high)
                real, imag = (spec_ref[place, reals], spec_ref[place, imags])
                for g in range(group):
                    lag = start + g - source
                    if lag < 0:
                        continue
                    if lag not in factors:
                        place = pl.ds(base, high)
                        factors[lag] = (real_buf[lag, place, column], imag_buf[lag, place, column])
                    a, b = factors[lag]
                    terms = (real * a, imag * b, real * b + imag * a)
                    before = sums[g]
                    sums[g] = [t if p is None else p + t for p, t in zip(before, terms)]
            for g in range(group):
                rr, ii, ri = sums[g]
                place = pl.ds(base + (start + g) * part, high)
                low_ref[place, reals] = jnp.where(first, rr, rr - ii).astype(low_ref.dtype)
                low_ref[place, imags] = jnp.where(first, ii, ri).astype(low_ref.dtype)
        return carry

    lax.fori_loop(0, slabs * (rows // LANES), one_slab, 0)
    back = jnp.dot(
        low_ref[...].astype(jnp.bfloat16), back_buf[...], preferred_element_type=jnp.float32
    )
    value = back.reshape(count, part, rows)
    value = value + skip_ref[low : low + part, :1][None] * x_ref[:, low : low + part].astype(jnp.float32)
    for copy in range(o_ref.shape[1]):
        o_ref[:, copy] = value.astype(o_ref.dtype)


def long_conv(blocks, head, planes, back, skip, low, part, copies=1):
    count, own, rows = blocks.shape
    height = count * part
    return call(
        functools.partial(conv_kernel, low),
        [pl.BlockSpec(memory_space=pltpu.VMEM)]
        + [pl.BlockSpec(memory_space=pl.ANY)] * 4
        + [pl.BlockSpec(memory_space=pltpu.VMEM)],
        [pl.BlockSpec(memory_space=pltpu.VMEM)],
        [((count, copies, part, rows), jnp.bfloat16)],
        scratch=[
            pltpu.VMEM(head.shape, jnp.bfloat16),
            pltpu.VMEM((count, part, rows), jnp.float32),
            pltpu.VMEM((count, part, rows), jnp.float32),
            pltpu.VMEM(back.shape, jnp.bfloat16),
            pltpu.VMEM((height, 2 * rows), jnp.float32),
            pltpu.VMEM((height, 2 * rows), jnp.float32 if part % 16 else jnp.bfloat16),
            pltpu.SemaphoreType.DMA((4,)),
        ],
        megabytes=28,
        flops=8 * height * rows * rows,
        moved=height * rows * 16,
    )(blocks, head, *[p.reshape(count, own, rows) for p in planes], back, skip, free=(0,))[0]


def gated_part(long, outer, p):
    count, step, rows = long.shape
    value = long.reshape(count * step, rows).T.astype(jnp.float32)
    tile = count * step
    return (outer[:, p * tile : (p + 1) * tile].astype(jnp.float32) * value).astype(jnp.bfloat16)


def gate_kernel(long_ref, outer_ref, o_ref):
    step = long_ref.shape[1] // 2
    tile = o_ref.shape[1] // 2
    for p in range(2):
        long = long_ref[:, p * step : (p + 1) * step]
        o_ref[:, p * tile : (p + 1) * tile] = gated_part(long, outer_ref, p)


def gate(long, outer):
    rows = outer.shape[0]
    width = long.shape[0] * long.shape[1]
    return call(
        gate_kernel,
        [
            pl.BlockSpec(long.shape, lambda n: (0, 0, 0)),
            pl.BlockSpec((rows, width), lambda n: (0, 0)),
        ],
        [pl.BlockSpec((rows, width), lambda n: (0, 0))],
        [((rows, width), jnp.bfloat16)],
        grid=(1,),
        moved=6 * rows * width,
    )(long, outer, free=(0,))[0]


def own_kernel(here_ref, gated_ref, weight_ref, o_ref):
    value = jnp.dot(gated_ref[...], weight_ref[...], preferred_element_type=jnp.float32)
    o_ref[...] = value.astype(o_ref.dtype)


def own_term(here, gated, out_weight, cols):
    rows, used = gated.shape
    wide = cols // 2
    return call(
        own_kernel,
        [
            pl.BlockSpec((rows, used), lambda n, h: (0, 0)),
            pl.BlockSpec((used, wide), lambda n, h: (0, h[0] * 2 + n)),
        ],
        [pl.BlockSpec((rows, wide), lambda n, h: (0, n))],
        [((rows, cols), jnp.bfloat16)],
        grid=(2,),
        flops=2 * rows * used * cols,
        moved=rows * cols * 2 + used * cols * 2,
        scalars=1,
    )(here, gated, out_weight)[0]


def last_kernel(
    place_ref, sent_ref, dealt_ref, sum_ref, mine_ref, theirs_ref, near_ref, far_ref, weight_ref, o_ref, *scratch
):
    outer_buf, weight_buf, block_buf, sum_buf, out_buf, gated_ref, sems = scratch
    here, core = (place_ref[0], place_ref[1])
    rows, used = outer_buf.shape[1:]
    wide = out_buf.shape[2]
    cols = 4 * wide
    pairs = [(mine_ref.at[:, pl.ds(used, used)], outer_buf.at[0]), (theirs_ref, outer_buf.at[1])]
    gates = [pltpu.make_async_copy(a, b, sems.at[g]) for g, (a, b) in enumerate(pairs)]
    for copy in gates:
        copy.start()
    places, inputs = ([], [])
    for k in range(4):
        source, side = ((near_ref, core), (far_ref, 1 - core))[k // 2]
        inside = k % 2 * wide
        column = pl.multiple_of(side * 2 * wide + inside, wide)
        places.append(pl.ds(column, wide))
        ours = pl.multiple_of(here * cols + column, wide)
        pairs = [
            (source.at[:, pl.ds(inside, wide)], block_buf.at[k]),
            (weight_ref.at[pl.ds(used, used), pl.ds(ours, wide)], weight_buf.at[k]),
            (sum_ref.at[:, places[k]], sum_buf.at[k]),
        ]
        inputs.append(
            [pltpu.make_async_copy(a, b, sems.at[2 + 3 * k + i]) for i, (a, b) in enumerate(pairs)]
        )
        for copy in inputs[k]:
            copy.start()
    tile = used // 2
    step = dealt_ref.shape[2] // 2
    for g in range(2):
        gates[g].wait()
        long = dealt_ref[:, here if g == 0 else 1 - here]
        for p in range(2):
            gated_ref[g, :, p * tile : (p + 1) * tile] = gated_part(
                long[:, p * step : (p + 1) * step], outer_buf.at[g], p
            )
    outputs = []
    for k in range(4):
        for copy in inputs[k]:
            copy.wait()
        value = sum_buf[k].astype(jnp.float32)
        for left, right in (
            (sent_ref[...], block_buf[k, :used]),
            (gated_ref[1], block_buf[k, used:]),
            (gated_ref[0], weight_buf[k]),
        ):
            value = value + jnp.dot(left, right, preferred_element_type=jnp.float32)
        out_buf[k] = value.astype(out_buf.dtype)
        outputs.append(pltpu.make_async_copy(out_buf.at[k], o_ref.at[:, places[k]], sems.at[14 + k]))
        outputs[k].start()
    for copy in outputs:
        copy.wait()


def last_term(place, sent, dealt, total, mine, theirs, near, far, out_weight):
    rows, cols = total.shape
    chan = near.shape[0]
    wide = cols // 4
    used = chan // 2
    vmem, anywhere = (pl.BlockSpec(memory_space=pltpu.VMEM), pl.BlockSpec(memory_space=pl.ANY))
    bf16 = jnp.bfloat16
    return call(
        last_kernel,
        [pl.BlockSpec(memory_space=pltpu.SMEM), vmem, vmem] + [anywhere] * 6,
        [anywhere],
        [((rows, cols), bf16)],
        scratch=[
            pltpu.VMEM((2, rows, used), bf16),
            pltpu.VMEM((4, used, wide), bf16),
            pltpu.VMEM((4, chan, wide), bf16),
            pltpu.VMEM((4, rows, wide), bf16),
            pltpu.VMEM((4, rows, wide), bf16),
            pltpu.VMEM((2, rows, used), bf16),
            pltpu.SemaphoreType.DMA((18,)),
        ],
        megabytes=32,
        flops=24 * rows * used * wide,
        moved=rows * wide * 16 + used * wide * 24,
    )(place, sent, dealt, total, mine, theirs, near, far, out_weight, free=(0, 1, 2))[0]


def exchanged(value):
    return lax.all_to_all(value, "ctx", 0, 0, tiled=True)


def to_groups(values):
    groups = lax.axis_size("ch")
    return [
        lax.ppermute(value, "ch", [(g, (g + s) % groups) for g in range(groups)])
        for s, value in enumerate(values, 1)
    ]


def any_groups(long, outer, out_weight):
    rows, chan = outer.shape
    groups = lax.axis_size("ch")
    here = lax.axis_index("ch")
    cols = out_weight.shape[1] // groups
    gated = gated_part(long, outer, 0)
    total = jnp.zeros((rows, cols), jnp.float32)
    weights = [
        lax.dynamic_slice(out_weight, (0, (here + s) % groups * cols), (chan, cols))
        for s in range(groups)
    ]
    values = [gated] + to_groups([gated] * (groups - 1))
    for value, weight in zip(values, weights[:1] + to_groups(weights[1:])):
        total = total + jnp.dot(value, weight, preferred_element_type=jnp.float32)
    return total.astype(jnp.bfloat16)


def local(streams, short_taps, filters, skip_gain, out_weight):
    rows, _, chan = streams.shape
    count = lax.axis_size("ctx")
    groups = lax.axis_size("ch")
    own = chan // count
    fast = groups == 2 and count % 2 == 0 and own % 64 == 0
    parts = 4 if fast else 1
    step = own // parts
    after = lax.optimization_barrier
    position, here = (lax.axis_index("ctx"), lax.axis_index("ch"))
    head = jnp.asarray(head_table(2 * rows))
    back = jnp.asarray(inverse_table(2 * rows))
    skip = lax.dynamic_index_in_dim(skip_gain.reshape(parts, count, step), position, 1, False)
    skip = jnp.broadcast_to(skip.reshape(own, 1), (own, LANES))
    streams = streams.transpose(1, 0, 2)
    turned_filters, tail = turned(filters, streams, count, parts)
    edges = passed_along(tail, "ctx", 1)
    turned_filters, edges = after((turned_filters, edges))
    filter_blocks = exchanged(turned_filters)
    cols = out_weight.shape[1] // groups
    if fast:
        half = cols // 2
        columns = (1 - here) * cols + position % 2 * half
        near = lax.dynamic_slice(out_weight, (0, columns), (chan, half))
        near, edges = after((near, edges))
    edges, skip = after((edges, skip))
    turned_inner, outer = mix(streams, edges, short_taps, count, parts)
    turned_inner, filter_blocks = after((turned_inner, filter_blocks))
    inner_blocks = exchanged(turned_inner)
    planes = filter_spectra(filter_blocks, head)
    if not fast:
        long = exchanged(long_conv(inner_blocks, head, planes, back, skip, 0, own)[:, 0])
        return any_groups(long, outer, out_weight)
    near, theirs = to_groups([near])[0], to_groups([outer[:, chan // 2 :]])[0]
    planes, near = after((planes, near))
    inner_blocks, near = after((inner_blocks, near))
    far = lax.ppermute(near, "ctx", [(i, i ^ 1) for i in range(count)])
    early = long_conv(inner_blocks, head, planes, back, skip, 0, 2 * step)[:, 0]
    inner_blocks, early = after((inner_blocks, early))
    late = long_conv(inner_blocks, head, planes, back, skip, 2 * step, 2 * step, copies=groups)
    early, late, far, theirs = after((exchanged(early), late, far, theirs))
    gated = gate(early, outer)
    sent = to_groups([gated])[0]
    dealt = lax.all_to_all(
        late.reshape(count * groups, 2 * step, rows), ("ctx", "ch"), 0, 0, tiled=True
    )
    dealt = dealt.reshape(count, groups, 2 * step, rows)
    total = own_term(here[None], gated, out_weight, cols)
    place = jnp.stack([here, position % 2])
    return last_term(place, sent, dealt, total, outer, theirs, near, far, out_weight)


def solution(mesh):
    return jax.shard_map(
        local,
        mesh=mesh,
        in_specs=(
            P("ctx", None, "ch"),
            P(None, None, "ch"),
            P("ctx", "ch"),
            P("ch"),
            P("ch", None),
        ),
        out_specs=P("ctx", "ch"),
        check_vma=False,
    )
```

```python
import functools

import jax
import jax.numpy as jnp
import ml_dtypes
import numpy as np
from jax import lax
from jax.experimental import pallas as pl
from jax.experimental.pallas import tpu as pltpu
from jax.sharding import PartitionSpec as P

LANES = 128


def passed_along(value, axis, steps):
    count = lax.axis_size(axis)
    initial, last = (max(0, -steps), min(count, count - steps))
    return lax.ppermute(value, axis, [(source, source + steps) for source in range(initial, last)])


def paired_columns(half):
    order = np.arange(2 * half).reshape(2, half // LANES, LANES)
    return order.transpose(1, 0, 2).reshape(-1)


def head_table(size):
    half = size // 2
    rows = np.arange(half)[:, None]
    cols = np.arange(size)[None, :]
    freq = np.where(cols < half, cols, cols - half)
    angle = (rows * freq % size) * (2.0 * np.pi / size)
    nyquist = np.where(rows % 2 == 0, 1.0, -1.0)
    table = np.where(cols < half, np.cos(angle), np.where(cols == half, nyquist, -np.sin(angle)))
    return table[:, paired_columns(half)].astype(ml_dtypes.bfloat16)


def inverse_table(size):
    half = size // 2
    rows = np.arange(size)[:, None]
    places = half + np.arange(half)[None, :]
    freq = np.where(rows < half, rows, rows - half)
    angle = (places * freq % size) * (2.0 * np.pi / size)
    weight = np.where(freq == 0, 1.0, 2.0) / size
    nyquist = np.where(places % 2 == 0, 1.0, -1.0) / size
    table = np.where(
        rows < half, weight * np.cos(angle), np.where(rows == half, nyquist, -weight * np.sin(angle))
    )
    return table[paired_columns(half)].astype(ml_dtypes.bfloat16)


def call(kernel, in_specs, out_specs, outs, grid=(), scratch=(), megabytes=16, flops=0, moved=0, scalars=0, aliases=None):
    inner = pl.pallas_call(
        kernel,
        grid_spec=pltpu.PrefetchScalarGridSpec(
            num_scalar_prefetch=scalars,
            grid=grid,
            in_specs=in_specs,
            out_specs=out_specs,
            scratch_shapes=list(scratch),
        ),
        out_shape=[pltpu.HBM(shape, dtype) for shape, dtype in outs],
        input_output_aliases=aliases or {},
        compiler_params=pltpu.CompilerParams(vmem_limit_bytes=megabytes * 1024 * 1024),
        cost_estimate=pl.CostEstimate(flops=flops, bytes_accessed=moved, transcendentals=0),
    )

    def run(*args, free=()):
        pinned = [
            a if k < scalars or k in free else pltpu.with_memory_space_constraint(a, pltpu.HBM)
            for k, a in enumerate(args)
        ]
        return inner(*pinned)

    return run


def store_turned(value, o_ref):
    o_ref[...] = value.T.reshape(o_ref.shape).astype(o_ref.dtype)


def turn_kernel(x_ref, s_ref, o_ref, tail_ref):
    tail_ref[...] = s_ref[:, s_ref.shape[1] - 2 :]
    store_turned(x_ref[...].astype(jnp.float32), o_ref)


def turned(x, streams, count, parts):
    rows, chan = x.shape
    own = chan // count
    last = min(rows, 16)
    tile = chan // parts
    return call(
        turn_kernel,
        [
            pl.BlockSpec((rows, tile), lambda p: (0, p)),
            pl.BlockSpec((3, last, tile), lambda p: (0, rows // last - 1, p)),
        ],
        [
            pl.BlockSpec((count, 1, own // parts, rows), lambda p: (0, 0, p, 0)),
            pl.BlockSpec((3, 2, tile), lambda p: (0, 0, p)),
        ],
        [((count, 2, own, rows), x.dtype), ((3, 2, chan), streams.dtype)],
        grid=(parts,),
        moved=4 * rows * chan,
    )(x, streams)


def mixed(s_ref, e_ref, t_ref, q):
    rows, width = s_ref.shape[1:]
    place = lax.broadcasted_iota(jnp.int32, (8, width), 0)
    now = s_ref[q].astype(jnp.float32)
    edge = e_ref[q].astype(jnp.float32)
    one, two = (pltpu.roll(now, 1, 0), pltpu.roll(now, 2, 0))
    one_top = jnp.where(place == 0, edge[1:2], one[:8])
    two_top = jnp.where(place == 0, edge[0:1], jnp.where(place == 1, edge[1:2], two[:8]))
    one = jnp.concatenate([one_top, one[8:]], axis=0)
    two = jnp.concatenate([two_top, two[8:]], axis=0)
    return t_ref[0, q : q + 1] * now + t_ref[1, q : q + 1] * one + t_ref[2, q : q + 1] * two


def inner_kernel(s_ref, e_ref, t_ref, _, o_ref):
    store_turned(mixed(s_ref, e_ref, t_ref, 0) * mixed(s_ref, e_ref, t_ref, 1), o_ref)


def with_inner(both, streams, edges, taps, parts):
    count, _, own, rows = both.shape
    chan = count * own
    tile = chan // parts
    return call(
        inner_kernel,
        [
            pl.BlockSpec((2, rows, tile), lambda p: (0, 0, p)),
            pl.BlockSpec((3, 2, tile), lambda p: (0, 0, p)),
            pl.BlockSpec((3, 3, tile), lambda p: (0, 0, p)),
            pl.BlockSpec(memory_space=pl.ANY),
        ],
        [pl.BlockSpec((count, 1, own // parts, rows), lambda p: (0, 1, p, 0))],
        [(both.shape, both.dtype)],
        grid=(parts,),
        megabytes=32,
        moved=6 * rows * chan,
        aliases={3: 0},
    )(streams, edges, taps, both)[0]


def outer_kernel(s_ref, e_ref, t_ref, o_ref):
    o_ref[...] = mixed(s_ref, e_ref, t_ref, 0).astype(o_ref.dtype)


def outer_gate(streams, which, edges, taps, parts):
    _, rows, chan = streams.shape
    tile = chan // parts
    return call(
        outer_kernel,
        [
            pl.BlockSpec((1, rows, tile), lambda p: (which, 0, p)),
            pl.BlockSpec((1, 2, tile), lambda p: (0, 0, p)),
            pl.BlockSpec((3, 1, tile), lambda p: (0, 0, p)),
        ],
        [pl.BlockSpec((rows, tile), lambda p: (0, p))],
        [((rows, chan), jnp.bfloat16)],
        grid=(parts,),
        megabytes=32,
        moved=4 * rows * chan,
    )(streams, edges, taps)[0]


def deal_kernel(f_ref, s_ref, t_ref, o_ref, f_buf, s_buf, tail_buf, sems):
    count, height, rows = o_ref.shape
    step = (height - 8) // 4
    chan = f_ref.shape[1]
    tile = chan // 2
    last = tail_buf.shape[0]
    per = LANES // step
    copies = [
        pltpu.make_async_copy(f_ref.at[:, pl.ds(p * tile, tile)], f_buf.at[p], sems.at[2 * p])
        for p in range(2)
    ] + [
        pltpu.make_async_copy(
            s_ref.at[pl.ds(0, 2), :, pl.ds(p * tile, tile)], s_buf.at[p], sems.at[2 * p + 1]
        )
        for p in range(2)
    ]
    copies.append(
        pltpu.make_async_copy(s_ref.at[2, pl.ds(rows - last, last)], tail_buf, sems.at[4])
    )
    for k in (0, 2, 1, 3, 4):
        copies[k].start()
    for p in range(2):
        start = p * 2 * step
        lanes = slice(p * tile, (p + 1) * tile)
        copies[p].wait()
        value = f_buf[p].astype(jnp.float32).T.reshape(count, step, rows)
        o_ref[:, start : start + step] = value.astype(o_ref.dtype)
        copies[2 + p].wait()
        both = []
        for q in range(2):
            now = s_buf[p, q].astype(jnp.float32)
            value = t_ref[0, q : q + 1, lanes] * now
            value = value + t_ref[1, q : q + 1, lanes] * pltpu.roll(now, 1, 0)
            both.append(value + t_ref[2, q : q + 1, lanes] * pltpu.roll(now, 2, 0))
        value = (both[0] * both[1]).T.reshape(count, step, rows)
        o_ref[:, start + step : start + 2 * step] = value.astype(o_ref.dtype)
        ends = [s_buf[p, q, a : a + 2].astype(jnp.float32) for a in (0, rows - 2) for q in range(2)]
        ends = jnp.concatenate(ends, axis=0).astype(o_ref.dtype)
        for g in range(tile // LANES):
            value = ends[:, g * LANES : (g + 1) * LANES]
            o_ref[g * per : (g + 1) * per, 4 * step :, p * LANES : (p + 1) * LANES] = (
                jnp.broadcast_to(value[None], (per, 8, LANES))
            )
    copies[4].wait()
    tail = tail_buf[last - 2 :].astype(jnp.float32)
    wide = chan // 4
    tail = jnp.concatenate(
        [tail[t : t + 1, q * wide : (q + 1) * wide] for t in range(2) for q in range(4)], axis=0
    ).astype(o_ref.dtype)
    o_ref[:, 4 * step :, 2 * LANES : 2 * LANES + wide] = jnp.broadcast_to(
        tail[None], (count, 8, wide)
    )


def deal(filters, streams, taps, count):
    rows, chan = filters.shape
    height = 2 * chan // count + 8
    anywhere, vmem = (pl.BlockSpec(memory_space=pl.ANY), pl.BlockSpec(memory_space=pltpu.VMEM))
    bf16 = jnp.bfloat16
    return call(
        deal_kernel,
        [anywhere, anywhere, vmem],
        [vmem],
        [((count, height, rows), bf16)],
        scratch=[
            pltpu.VMEM((2, rows, chan // 2), bf16),
            pltpu.VMEM((2, 2, rows, chan // 2), bf16),
            pltpu.VMEM((16, chan), bf16),
            pltpu.SemaphoreType.DMA((5,)),
        ],
        megabytes=32,
        moved=10 * rows * chan,
    )(filters, streams, taps)[0]


def first_tokens(ends, taps, place):
    count = ends.shape[0]

    def at(row):
        return ends[:, row].astype(jnp.float32)

    block = lax.broadcasted_iota(jnp.int32, (count, LANES), 0)

    def before(row):
        return jnp.where(block == 0, 0.0, pltpu.roll(at(row), 1, 0))

    values = [1.0, 1.0]
    for q in range(2):
        t0, t1, t2 = (taps[2 * m + q : 2 * m + q + 1] for m in range(3))
        one, two = (at(2 * q), at(2 * q + 1))
        far, near = (before(4 + 2 * q), before(5 + 2 * q))
        values[0] = values[0] * (t0 * one + t1 * near + t2 * far)
        values[1] = values[1] * (t0 * two + t1 * one + t2 * near)
    rest = jnp.zeros((LANES - 2 * count, LANES), jnp.float32)
    return jnp.concatenate(values + [rest], axis=0).T


def conv_kernel(split, place_ref, both_ref, head_ref, back_ref, skip_ref, taps_ref, o_ref, *scratch):
    head_buf, back_buf, spec_ref, factor_ref, low_ref, x_buf, fix_ref, sems = scratch
    count, _, part, rows = o_ref.shape
    high = min(part, 16)
    group = 2
    low = 2 * part * (split or 0)
    pairs = [(head_ref, head_buf), (back_ref, back_buf)]
    copies = [pltpu.make_async_copy(a, b, sems.at[i]) for i, (a, b) in enumerate(pairs)]
    for copy in copies:
        copy.start()
    x_buf[...] = both_ref[:, low + part : low + 2 * part]
    if split is not None:
        ends = both_ref[:, 4 * part :, split * LANES : (split + 1) * LANES]
        fix_ref[...] = first_tokens(ends, taps_ref[split], place_ref[0])
        mine = fix_ref[pl.ds(pl.multiple_of(place_ref[0] * part, part), part), :]
        lane = lax.broadcasted_iota(jnp.int32, (part, LANES), 1)
        for block in range(count):
            one = pltpu.roll(mine, (LANES - block) % LANES, 1)
            two = pltpu.roll(mine, (LANES - block - count + 1) % LANES, 1)
            value = x_buf[block, :, :LANES].astype(jnp.float32)
            value = jnp.where(lane == 0, one, jnp.where(lane == 1, two, value))
            x_buf[block, :, :LANES] = value.astype(x_buf.dtype)
    copies[0].wait()
    for ref, blocks in ((factor_ref, both_ref[:, low : low + part]), (spec_ref, x_buf[...])):
        blocks = blocks.reshape(count * part, rows)
        ref[...] = jnp.dot(blocks, head_buf[...], preferred_element_type=jnp.float32)
    column = lax.broadcasted_iota(jnp.int32, (part, 2 * rows), 1)
    sign = jnp.where(column % 2 == 0, 1.0, -1.0)

    def one_window(turn, carry):
        block = count - 1 - turn
        place = pl.ds(pl.multiple_of(block * part, part), part)
        before = pl.ds(pl.multiple_of(jnp.maximum(block - 1, 0) * part, part), part)
        earlier = jnp.where(block > 0, factor_ref[before, :], 0.0)
        factor_ref[place, :] = earlier + sign * factor_ref[place, :]
        return carry

    lax.fori_loop(0, count, one_window, 0)
    lane = lax.broadcasted_iota(jnp.int32, (high, LANES), 1)
    slabs = part // high

    def one_slab(turn, carry):
        tile = turn // slabs
        base = pl.multiple_of((turn % slabs) * high, high)
        reals = pl.ds(pl.multiple_of(tile * 2 * LANES, LANES), LANES)
        imags = pl.ds(pl.multiple_of(tile * 2 * LANES + LANES, LANES), LANES)
        first = (lane == 0) & (tile == 0)
        for start in range(0, count, group):
            sums = [[None] * 3 for _ in range(group)]
            factors = {}
            for source in range(start + group):
                place = pl.ds(base + source * part, high)
                real, imag = (spec_ref[place, reals], spec_ref[place, imags])
                for g in range(group):
                    lag = start + g - source
                    if lag < 0:
                        continue
                    if lag not in factors:
                        place = pl.ds(base + lag * part, high)
                        factors[lag] = (factor_ref[place, reals], factor_ref[place, imags])
                    a, b = factors[lag]
                    terms = (real * a, imag * b, real * b + imag * a)
                    before = sums[g]
                    sums[g] = [t if p is None else p + t for p, t in zip(before, terms)]
            for g in range(group):
                rr, ii, ri = sums[g]
                place = pl.ds(base + (start + g) * part, high)
                low_ref[place, reals] = jnp.where(first, rr, rr - ii).astype(low_ref.dtype)
                low_ref[place, imags] = jnp.where(first, ii, ri).astype(low_ref.dtype)
        return carry

    lax.fori_loop(0, slabs * (rows // LANES), one_slab, 0)
    copies[1].wait()
    back = jnp.dot(
        low_ref[...].astype(jnp.bfloat16), back_buf[...], preferred_element_type=jnp.float32
    )
    value = back.reshape(count, part, rows)
    skip = skip_ref[low // 2 : low // 2 + part, :1][None]
    value = value + skip * x_buf[...].astype(jnp.float32)
    for copy in range(o_ref.shape[1]):
        o_ref[:, copy] = value.astype(o_ref.dtype)


def long_conv(both, head, back, skip, taps, place, split, copies=1):
    count, _, rows = both.shape
    own = skip.shape[0]
    part = own if split is None else own // 2
    height = count * part
    vmem, anywhere = (pl.BlockSpec(memory_space=pltpu.VMEM), pl.BlockSpec(memory_space=pl.ANY))
    return call(
        functools.partial(conv_kernel, split),
        [pl.BlockSpec(memory_space=pltpu.SMEM), vmem, anywhere, anywhere, vmem, vmem],
        [vmem],
        [((count, copies, part, rows), jnp.bfloat16)],
        scratch=[
            pltpu.VMEM(head.shape, jnp.bfloat16),
            pltpu.VMEM(back.shape, jnp.bfloat16),
            pltpu.VMEM((height, 2 * rows), jnp.float32),
            pltpu.VMEM((height, 2 * rows), jnp.float32),
            pltpu.VMEM((height, 2 * rows), jnp.float32 if part % 16 else jnp.bfloat16),
            pltpu.VMEM((count, part, rows), jnp.bfloat16),
            pltpu.VMEM((LANES, LANES), jnp.float32),
            pltpu.SemaphoreType.DMA((2,)),
        ],
        megabytes=28,
        flops=12 * height * rows * rows,
        moved=height * rows * 8,
    )(place, both, head, back, skip, taps, free=(0, 1))[0]


def gated_part(long, outer, first):
    count, step, rows = long.shape
    value = long.reshape(count * step, rows).T.astype(jnp.float32)
    outer = outer.astype(jnp.float32)
    outer = jnp.concatenate([outer[:8] + first, outer[8:]], axis=0)
    return (outer * value).astype(jnp.bfloat16)


def gate_kernel(long_ref, outer_ref, first_ref, o_ref):
    o_ref[...] = gated_part(long_ref[...], outer_ref[...], first_ref[...])


def gate(long, outer, first):
    rows = outer.shape[0]
    width = long.shape[0] * long.shape[1]
    return call(
        gate_kernel,
        [
            pl.BlockSpec(long.shape, lambda n: (0, 0, 0)),
            pl.BlockSpec((rows, width), lambda n: (0, 0)),
            pl.BlockSpec((8, width), lambda n: (0, 0)),
        ],
        [pl.BlockSpec((rows, width), lambda n: (0, 0))],
        [((rows, width), jnp.bfloat16)],
        grid=(1,),
        moved=6 * rows * width,
    )(long, outer, first, free=(0,))[0]


def own_kernel(here_ref, gated_ref, weight_ref, o_ref):
    value = jnp.dot(gated_ref[...], weight_ref[...], preferred_element_type=jnp.float32)
    o_ref[...] = value.astype(o_ref.dtype)


def own_term(here, gated, out_weight, cols):
    rows, used = gated.shape
    wide = cols // 2
    return call(
        own_kernel,
        [
            pl.BlockSpec((rows, used), lambda n, h: (0, 0)),
            pl.BlockSpec((used, wide), lambda n, h: (0, h[0] * 2 + n)),
        ],
        [pl.BlockSpec((rows, wide), lambda n, h: (0, n))],
        [((rows, cols), jnp.bfloat16)],
        grid=(2,),
        flops=2 * rows * used * cols,
        moved=rows * cols * 2 + used * cols * 2,
        scalars=1,
    )(here, gated, out_weight)[0]


def last_kernel(
    place_ref, sent_ref, dealt_ref, first_ref, sum_ref, mine_ref, theirs_ref, *refs
):
    blocks, (weight_ref, o_ref, *scratch) = (refs[:4], refs[4:])
    outer_buf, weight_buf, block_buf, sum_buf, out_buf, gated_ref, sems = scratch
    here, quarter = (place_ref[0], place_ref[1])
    rows, used = outer_buf.shape[1:]
    wide = out_buf.shape[2]
    cols = 4 * wide
    pairs = [(mine_ref.at[:, pl.ds(used, used)], outer_buf.at[0]), (theirs_ref, outer_buf.at[1])]
    gates = [pltpu.make_async_copy(a, b, sems.at[g]) for g, (a, b) in enumerate(pairs)]
    for copy in gates:
        copy.start()
    places, inputs = ([], [])
    for k in range(4):
        column = pl.multiple_of((quarter ^ k) * wide, wide)
        places.append(pl.ds(column, wide))
        ours = pl.multiple_of(here * cols + column, wide)
        pairs = [
            (blocks[k], block_buf.at[k]),
            (weight_ref.at[pl.ds(used, used), pl.ds(ours, wide)], weight_buf.at[k]),
            (sum_ref.at[:, places[k]], sum_buf.at[k]),
        ]
        inputs.append(
            [pltpu.make_async_copy(a, b, sems.at[2 + 3 * k + i]) for i, (a, b) in enumerate(pairs)]
        )
        for copy in inputs[k]:
            copy.start()
    for g in range(2):
        gates[g].wait()
        long = dealt_ref[:, here if g == 0 else 1 - here]
        gated_ref[g] = gated_part(long, outer_buf[g], first_ref[g])
    outputs = []
    for k in range(4):
        for copy in inputs[k]:
            copy.wait()
        value = sum_buf[k].astype(jnp.float32)
        for left, right in (
            (sent_ref[...], block_buf[k, :used]),
            (gated_ref[1], block_buf[k, used:]),
            (gated_ref[0], weight_buf[k]),
        ):
            value = value + jnp.dot(left, right, preferred_element_type=jnp.float32)
        out_buf[k] = value.astype(out_buf.dtype)
        outputs.append(pltpu.make_async_copy(out_buf.at[k], o_ref.at[:, places[k]], sems.at[14 + k]))
        outputs[k].start()
    for copy in outputs:
        copy.wait()


def last_term(place, sent, dealt, first, total, mine, theirs, blocks, out_weight):
    rows, cols = total.shape
    chan = mine.shape[1]
    wide = cols // 4
    used = chan // 2
    vmem, anywhere = (pl.BlockSpec(memory_space=pltpu.VMEM), pl.BlockSpec(memory_space=pl.ANY))
    bf16 = jnp.bfloat16
    return call(
        last_kernel,
        [pl.BlockSpec(memory_space=pltpu.SMEM), vmem, vmem, vmem] + [anywhere] * 8,
        [anywhere],
        [((rows, cols), bf16)],
        scratch=[
            pltpu.VMEM((2, rows, used), bf16),
            pltpu.VMEM((4, used, wide), bf16),
            pltpu.VMEM((4, chan, wide), bf16),
            pltpu.VMEM((4, rows, wide), bf16),
            pltpu.VMEM((4, rows, wide), bf16),
            pltpu.VMEM((2, rows, used), bf16),
            pltpu.SemaphoreType.DMA((18,)),
        ],
        megabytes=32,
        flops=24 * rows * used * wide,
        moved=rows * wide * 16 + used * wide * 24,
    )(place, sent, dealt, first, total, mine, theirs, *blocks, out_weight, free=(0, 1, 2, 3))[0]


def exchanged(value):
    return lax.all_to_all(value, "ctx", 0, 0, tiled=True)


def to_groups(values):
    groups = lax.axis_size("ch")
    return [
        lax.ppermute(value, "ch", [(g, (g + s) % groups) for g in range(groups)])
        for s, value in enumerate(values, 1)
    ]


def any_groups(long, outer, out_weight):
    rows, chan = outer.shape
    groups = lax.axis_size("ch")
    here = lax.axis_index("ch")
    cols = out_weight.shape[1] // groups
    gated = gated_part(long, outer, jnp.zeros((8, chan), jnp.float32))
    total = jnp.zeros((rows, cols), jnp.float32)
    weights = [
        lax.dynamic_slice(out_weight, (0, (here + s) % groups * cols), (chan, cols))
        for s in range(groups)
    ]
    values = [gated] + to_groups([gated] * (groups - 1))
    for value, weight in zip(values, weights[:1] + to_groups(weights[1:])):
        total = total + jnp.dot(value, weight, preferred_element_type=jnp.float32)
    return total.astype(jnp.bfloat16)


def local(streams, short_taps, filters, skip_gain, out_weight):
    rows, _, chan = streams.shape
    count = lax.axis_size("ctx")
    groups = lax.axis_size("ch")
    own = chan // count
    step = own // 2
    fast = groups == 2 and count % 4 == 0 and own % 32 == 0 and LANES % step == 0
    fast = fast and chan // 4 + 2 * LANES <= rows and 2 * count <= LANES
    after = lax.optimization_barrier
    position, here = (lax.axis_index("ctx"), lax.axis_index("ch"))
    head = jnp.asarray(head_table(2 * rows))
    back = jnp.asarray(inverse_table(2 * rows))
    streams = streams.transpose(1, 0, 2)
    parts = 2 if fast else 1
    skip = skip_gain.reshape(parts, count, own // parts)
    skip = lax.dynamic_index_in_dim(skip, position, 1, False)
    skip = jnp.broadcast_to(skip.reshape(own, 1), (own, LANES))
    if not fast:
        both, tail = turned(filters, streams, count, parts)
        edges = passed_along(tail, "ctx", 1)
        both = exchanged(with_inner(both, streams, edges, short_taps, parts))
        both = both.reshape(count, 2 * own, rows)
        outer = outer_gate(streams, 2, edges[2:], short_taps[:, 2:], parts)
        none = jnp.zeros((2, 8, LANES), jnp.float32)
        long = long_conv(both, head, back, skip, none, jnp.zeros((1,), jnp.int32), None)
        return any_groups(exchanged(long[:, 0]), outer, out_weight)
    per = LANES // step
    place = (position % per)[None]
    taps = short_taps[:, :2].reshape(6, 2, chan // 2)
    taps = lax.dynamic_slice(taps, (0, 0, position // per * LANES), (6, 2, LANES))
    taps = jnp.pad(taps.transpose(1, 0, 2), ((0, 0), (0, 2), (0, 0)))
    both = exchanged(deal(filters, streams, short_taps, count))
    cols = out_weight.shape[1] // groups
    wide = cols // 4
    columns = (1 - here) * cols + position % 4 * wide
    near = lax.dynamic_slice(out_weight, (0, columns), (chan, wide))
    near, skip, taps = after((near, skip, taps))
    near = to_groups([near])[0]
    none = jnp.zeros((1, 2, chan), jnp.float32)
    none, near = after((none, near))
    outer = outer_gate(streams, 2, none, short_taps[:, 2:], 2)
    theirs = to_groups([outer[:, chan // 2 :]])[0]

    def swapped(value, bit):
        return lax.ppermute(value, "ctx", [(i, i ^ bit) for i in range(count)])

    across = swapped(near, 2)
    early = long_conv(both, head, back, skip, taps, place, 0)[:, 0]
    edges = lax.dynamic_slice(
        both, (jnp.maximum(position - 1, 0), 4 * step, 2 * LANES), (1, 8, chan // 4)
    )
    edges = jnp.where(position == 0, 0.0, edges.reshape(2, chan).astype(jnp.float32))
    first = jnp.stack(
        [short_taps[1, 2] * edges[1] + short_taps[2, 2] * edges[0], short_taps[2, 2] * edges[1]]
    )
    first = jnp.pad(first, ((0, 6), (0, 0)))
    other = to_groups([first[:, chan // 2 :]])[0]
    both, across, theirs, _ = after((both, across, theirs, early))
    blocks = [near, swapped(near, 1), across, swapped(across, 1)]
    late = long_conv(both, head, back, skip, taps, place, 1, copies=groups)
    early, late, blocks, other, first = after((exchanged(early), late, blocks, other, first))
    gated = gate(early, outer, first)
    sent = to_groups([gated])[0]
    dealt = lax.all_to_all(
        late.reshape(count * groups, step, rows), ("ctx", "ch"), 0, 0, tiled=True
    )
    dealt = dealt.reshape(count, groups, step, rows)
    total = own_term(here[None], gated, out_weight, cols)
    place = jnp.stack([here, position % 4])
    first = jnp.stack([first[:, chan // 2 :], other])
    return last_term(place, sent, dealt, first, total, outer, theirs, blocks, out_weight)


def solution(mesh):
    return jax.shard_map(
        local,
        mesh=mesh,
        in_specs=(
            P("ctx", None, "ch"),
            P(None, None, "ch"),
            P("ctx", "ch"),
            P("ch"),
            P("ch", None),
        ),
        out_specs=P("ctx", "ch"),
        check_vma=False,
    )
```

```python
import functools

import jax
import jax.numpy as jnp
import ml_dtypes
import numpy as np
from jax import lax
from jax.experimental import pallas as pl
from jax.experimental.pallas import tpu as pltpu
from jax.sharding import PartitionSpec as P

LANES = 128


def passed_along(value, axis, steps):
    count = lax.axis_size(axis)
    initial, last = (max(0, -steps), min(count, count - steps))
    return lax.ppermute(value, axis, [(source, source + steps) for source in range(initial, last)])


def paired_columns(half):
    order = np.arange(2 * half).reshape(2, half // LANES, LANES)
    return order.transpose(1, 0, 2).reshape(-1)


def head_table(size):
    half = size // 2
    rows = np.arange(half)[:, None]
    cols = np.arange(size)[None, :]
    freq = np.where(cols < half, cols, cols - half)
    angle = (rows * freq % size) * (2.0 * np.pi / size)
    nyquist = np.where(rows % 2 == 0, 1.0, -1.0)
    table = np.where(cols < half, np.cos(angle), np.where(cols == half, nyquist, -np.sin(angle)))
    return table[:, paired_columns(half)].astype(ml_dtypes.bfloat16)


def inverse_table(size):
    half = size // 2
    rows = np.arange(size)[:, None]
    places = half + np.arange(half)[None, :]
    freq = np.where(rows < half, rows, rows - half)
    angle = (places * freq % size) * (2.0 * np.pi / size)
    weight = np.where(freq == 0, 1.0, 2.0) / size
    nyquist = np.where(places % 2 == 0, 1.0, -1.0) / size
    table = np.where(
        rows < half, weight * np.cos(angle), np.where(rows == half, nyquist, -weight * np.sin(angle))
    )
    return table[paired_columns(half)].astype(ml_dtypes.bfloat16)


def call(kernel, in_specs, out_specs, outs, grid=(), scratch=(), megabytes=16, flops=0, moved=0, scalars=0, aliases=None):
    inner = pl.pallas_call(
        kernel,
        grid_spec=pltpu.PrefetchScalarGridSpec(
            num_scalar_prefetch=scalars,
            grid=grid,
            in_specs=in_specs,
            out_specs=out_specs,
            scratch_shapes=list(scratch),
        ),
        out_shape=[pltpu.HBM(shape, dtype) for shape, dtype in outs],
        input_output_aliases=aliases or {},
        compiler_params=pltpu.CompilerParams(vmem_limit_bytes=megabytes * 1024 * 1024),
        cost_estimate=pl.CostEstimate(flops=flops, bytes_accessed=moved, transcendentals=0),
    )

    def run(*args, free=()):
        pinned = [
            a if k < scalars or k in free else pltpu.with_memory_space_constraint(a, pltpu.HBM)
            for k, a in enumerate(args)
        ]
        return inner(*pinned)

    return run


def store_turned(value, o_ref):
    o_ref[...] = value.T.reshape(o_ref.shape).astype(o_ref.dtype)


def turn_kernel(x_ref, s_ref, o_ref, tail_ref):
    tail_ref[...] = s_ref[:, s_ref.shape[1] - 2 :]
    store_turned(x_ref[...].astype(jnp.float32), o_ref)


def turned(x, streams, count, parts):
    rows, chan = x.shape
    own = chan // count
    last = min(rows, 16)
    tile = chan // parts
    return call(
        turn_kernel,
        [
            pl.BlockSpec((rows, tile), lambda p: (0, p)),
            pl.BlockSpec((3, last, tile), lambda p: (0, rows // last - 1, p)),
        ],
        [
            pl.BlockSpec((count, 1, own // parts, rows), lambda p: (0, 0, p, 0)),
            pl.BlockSpec((3, 2, tile), lambda p: (0, 0, p)),
        ],
        [((count, 2, own, rows), x.dtype), ((3, 2, chan), streams.dtype)],
        grid=(parts,),
        moved=4 * rows * chan,
    )(x, streams)


def mixed(s_ref, e_ref, t_ref, q):
    rows, width = s_ref.shape[1:]
    place = lax.broadcasted_iota(jnp.int32, (8, width), 0)
    now = s_ref[q].astype(jnp.float32)
    edge = e_ref[q].astype(jnp.float32)
    one, two = (pltpu.roll(now, 1, 0), pltpu.roll(now, 2, 0))
    one_top = jnp.where(place == 0, edge[1:2], one[:8])
    two_top = jnp.where(place == 0, edge[0:1], jnp.where(place == 1, edge[1:2], two[:8]))
    one = jnp.concatenate([one_top, one[8:]], axis=0)
    two = jnp.concatenate([two_top, two[8:]], axis=0)
    return t_ref[0, q : q + 1] * now + t_ref[1, q : q + 1] * one + t_ref[2, q : q + 1] * two


def inner_kernel(s_ref, e_ref, t_ref, _, o_ref):
    store_turned(mixed(s_ref, e_ref, t_ref, 0) * mixed(s_ref, e_ref, t_ref, 1), o_ref)


def with_inner(both, streams, edges, taps, parts):
    count, _, own, rows = both.shape
    chan = count * own
    tile = chan // parts
    return call(
        inner_kernel,
        [
            pl.BlockSpec((2, rows, tile), lambda p: (0, 0, p)),
            pl.BlockSpec((3, 2, tile), lambda p: (0, 0, p)),
            pl.BlockSpec((3, 3, tile), lambda p: (0, 0, p)),
            pl.BlockSpec(memory_space=pl.ANY),
        ],
        [pl.BlockSpec((count, 1, own // parts, rows), lambda p: (0, 1, p, 0))],
        [(both.shape, both.dtype)],
        grid=(parts,),
        megabytes=32,
        moved=6 * rows * chan,
        aliases={3: 0},
    )(streams, edges, taps, both)[0]


def outer_kernel(s_ref, e_ref, t_ref, o_ref):
    o_ref[...] = mixed(s_ref, e_ref, t_ref, 0).astype(o_ref.dtype)


def outer_gate(streams, which, edges, taps, parts):
    _, rows, chan = streams.shape
    tile = chan // parts
    return call(
        outer_kernel,
        [
            pl.BlockSpec((1, rows, tile), lambda p: (which, 0, p)),
            pl.BlockSpec((1, 2, tile), lambda p: (0, 0, p)),
            pl.BlockSpec((3, 1, tile), lambda p: (0, 0, p)),
        ],
        [pl.BlockSpec((rows, tile), lambda p: (0, p))],
        [((rows, chan), jnp.bfloat16)],
        grid=(parts,),
        megabytes=32,
        moved=4 * rows * chan,
    )(streams, edges, taps)[0]


def deal_kernel(f_ref, s_ref, t_ref, o_ref, f_buf, s_buf, tail_buf, sems):
    count, height, rows = o_ref.shape
    step = (height - 8) // 4
    chan = f_ref.shape[1]
    tile = chan // 2
    last = tail_buf.shape[0]
    per = LANES // step
    copies = [
        pltpu.make_async_copy(f_ref.at[:, pl.ds(p * tile, tile)], f_buf.at[p], sems.at[2 * p])
        for p in range(2)
    ] + [
        pltpu.make_async_copy(
            s_ref.at[pl.ds(0, 2), :, pl.ds(p * tile, tile)], s_buf.at[p], sems.at[2 * p + 1]
        )
        for p in range(2)
    ]
    copies.append(
        pltpu.make_async_copy(s_ref.at[2, pl.ds(rows - last, last)], tail_buf, sems.at[4])
    )
    for k in (0, 2, 1, 3, 4):
        copies[k].start()
    for p in range(2):
        start = p * 2 * step
        lanes = slice(p * tile, (p + 1) * tile)
        copies[p].wait()
        value = f_buf[p].astype(jnp.float32).T.reshape(count, step, rows)
        o_ref[:, start : start + step] = value.astype(o_ref.dtype)
        copies[2 + p].wait()
        both = []
        for q in range(2):
            now = s_buf[p, q].astype(jnp.float32)
            value = t_ref[0, q : q + 1, lanes] * now
            value = value + t_ref[1, q : q + 1, lanes] * pltpu.roll(now, 1, 0)
            both.append(value + t_ref[2, q : q + 1, lanes] * pltpu.roll(now, 2, 0))
        value = (both[0] * both[1]).T.reshape(count, step, rows)
        o_ref[:, start + step : start + 2 * step] = value.astype(o_ref.dtype)
        ends = [s_buf[p, q, a : a + 2].astype(jnp.float32) for a in (0, rows - 2) for q in range(2)]
        ends = jnp.concatenate(ends, axis=0).astype(o_ref.dtype)
        for g in range(tile // LANES):
            value = ends[:, g * LANES : (g + 1) * LANES]
            o_ref[g * per : (g + 1) * per, 4 * step :, p * LANES : (p + 1) * LANES] = (
                jnp.broadcast_to(value[None], (per, 8, LANES))
            )
    copies[4].wait()
    tail = tail_buf[last - 2 :].astype(jnp.float32)
    wide = chan // 4
    tail = jnp.concatenate(
        [tail[t : t + 1, q * wide : (q + 1) * wide] for t in range(2) for q in range(4)], axis=0
    ).astype(o_ref.dtype)
    o_ref[:, 4 * step :, 2 * LANES : 2 * LANES + wide] = jnp.broadcast_to(
        tail[None], (count, 8, wide)
    )


def deal(filters, streams, taps, count):
    rows, chan = filters.shape
    height = 2 * chan // count + 8
    anywhere, vmem = (pl.BlockSpec(memory_space=pl.ANY), pl.BlockSpec(memory_space=pltpu.VMEM))
    bf16 = jnp.bfloat16
    return call(
        deal_kernel,
        [anywhere, anywhere, vmem],
        [vmem],
        [((count, height, rows), bf16)],
        scratch=[
            pltpu.VMEM((2, rows, chan // 2), bf16),
            pltpu.VMEM((2, 2, rows, chan // 2), bf16),
            pltpu.VMEM((16, chan), bf16),
            pltpu.SemaphoreType.DMA((5,)),
        ],
        megabytes=32,
        moved=10 * rows * chan,
    )(filters, streams, taps)[0]


def first_tokens(ends, taps, place):
    count = ends.shape[0]

    def at(row):
        return ends[:, row].astype(jnp.float32)

    block = lax.broadcasted_iota(jnp.int32, (count, LANES), 0)

    def before(row):
        return jnp.where(block == 0, 0.0, pltpu.roll(at(row), 1, 0))

    values = [1.0, 1.0]
    for q in range(2):
        t0, t1, t2 = (taps[2 * m + q : 2 * m + q + 1] for m in range(3))
        one, two = (at(2 * q), at(2 * q + 1))
        far, near = (before(4 + 2 * q), before(5 + 2 * q))
        values[0] = values[0] * (t0 * one + t1 * near + t2 * far)
        values[1] = values[1] * (t0 * two + t1 * one + t2 * near)
    rest = jnp.zeros((LANES - 2 * count, LANES), jnp.float32)
    return jnp.concatenate(values + [rest], axis=0).T


def conv_kernel(split, place_ref, both_ref, head_ref, back_ref, skip_ref, taps_ref, o_ref, *scratch):
    head_buf, back_buf, spec_ref, factor_ref, low_ref, x_buf, fix_ref, sems = scratch
    count, _, part, rows = o_ref.shape
    tiles = rows // LANES
    high = min(part, 16)
    group = 2
    low = 2 * part * (split or 0)
    copies = [
        pltpu.make_async_copy(
            head_ref.at[:, pl.ds(t * 2 * LANES, 2 * LANES)], head_buf.at[t], sems.at[t]
        )
        for t in range(tiles)
    ]
    copies.append(pltpu.make_async_copy(back_ref, back_buf, sems.at[tiles]))
    for copy in copies:
        copy.start()
    x_buf[...] = both_ref[:, low + part : low + 2 * part]
    if split is not None:
        ends = both_ref[:, 4 * part :, split * LANES : (split + 1) * LANES]
        fix_ref[...] = first_tokens(ends, taps_ref[split], place_ref[0])
        mine = fix_ref[pl.ds(pl.multiple_of(place_ref[0] * part, part), part), :]
        lane = lax.broadcasted_iota(jnp.int32, (part, LANES), 1)
        for block in range(count):
            one = pltpu.roll(mine, (LANES - block) % LANES, 1)
            two = pltpu.roll(mine, (LANES - block - count + 1) % LANES, 1)
            value = x_buf[block, :, :LANES].astype(jnp.float32)
            value = jnp.where(lane == 0, one, jnp.where(lane == 1, two, value))
            x_buf[block, :, :LANES] = value.astype(x_buf.dtype)
    height = count * part
    filters = both_ref[:, low : low + part].reshape(height, rows)
    odd = lax.broadcasted_iota(jnp.int32, (height, 2 * LANES), 1) % 2 == 1
    lane = lax.broadcasted_iota(jnp.int32, (high, LANES), 1)

    def spectra(t):
        copies[t].wait()
        value = jnp.dot(filters, head_buf[t], preferred_element_type=jnp.float32)
        earlier = jnp.concatenate([jnp.zeros_like(value[:part]), value[:-part]], axis=0)
        factor_ref[t] = earlier + jnp.where(odd, -value, value)
        spec_ref[t] = jnp.dot(
            x_buf[...].reshape(height, rows), head_buf[t], preferred_element_type=jnp.float32
        )

    def products(t, slab):
        base = slab * high
        if not isinstance(base, int):
            base = pl.multiple_of(base, high)
        for start in range(0, count, group):
            sums = [[None] * 3 for _ in range(group)]
            factors = {}
            for source in range(start + group):
                place = pl.ds(base + source * part, high)
                real, imag = (spec_ref[t, place, :LANES], spec_ref[t, place, LANES:])
                for g in range(group):
                    lag = start + g - source
                    if lag < 0:
                        continue
                    if lag not in factors:
                        place = pl.ds(base + lag * part, high)
                        factors[lag] = (factor_ref[t, place, :LANES], factor_ref[t, place, LANES:])
                    a, b = factors[lag]
                    terms = (real * a, imag * b, real * b + imag * a)
                    before = sums[g]
                    sums[g] = [u if p is None else p + u for p, u in zip(before, terms)]
            for g in range(group):
                rr, ii, ri = sums[g]
                place = pl.ds(base + (start + g) * part, high)
                re, im = (rr - ii, ri)
                if t == 0:
                    re, im = (jnp.where(lane == 0, rr, re), jnp.where(lane == 0, ii, im))
                low_ref[place, t * 2 * LANES : t * 2 * LANES + LANES] = re.astype(low_ref.dtype)
                low_ref[place, t * 2 * LANES + LANES : (t + 1) * 2 * LANES] = im.astype(low_ref.dtype)

    for t in range(tiles):
        spectra(t)
        if split is not None:
            for slab in range(part // high):
                products(t, slab)
        else:

            def one_slab(slab, carry, t=t):
                products(t, slab)
                return carry

            lax.fori_loop(0, part // high, one_slab, 0)
    copies[tiles].wait()
    back = jnp.dot(
        low_ref[...].astype(jnp.bfloat16), back_buf[...], preferred_element_type=jnp.float32
    )
    value = back.reshape(count, part, rows)
    skip = skip_ref[low // 2 : low // 2 + part, :1][None]
    value = value + skip * x_buf[...].astype(jnp.float32)
    for copy in range(o_ref.shape[1]):
        o_ref[:, copy] = value.astype(o_ref.dtype)


def long_conv(both, head, back, skip, taps, place, split, copies=1):
    count, _, rows = both.shape
    own = skip.shape[0]
    part = own if split is None else own // 2
    height = count * part
    vmem, anywhere = (pl.BlockSpec(memory_space=pltpu.VMEM), pl.BlockSpec(memory_space=pl.ANY))
    return call(
        functools.partial(conv_kernel, split),
        [pl.BlockSpec(memory_space=pltpu.SMEM), vmem, anywhere, anywhere, vmem, vmem],
        [vmem],
        [((count, copies, part, rows), jnp.bfloat16)],
        scratch=[
            pltpu.VMEM((rows // LANES, rows, 2 * LANES), jnp.bfloat16),
            pltpu.VMEM(back.shape, jnp.bfloat16),
            pltpu.VMEM((rows // LANES, height, 2 * LANES), jnp.float32),
            pltpu.VMEM((rows // LANES, height, 2 * LANES), jnp.float32),
            pltpu.VMEM((height, 2 * rows), jnp.float32 if part % 16 else jnp.bfloat16),
            pltpu.VMEM((count, part, rows), jnp.bfloat16),
            pltpu.VMEM((LANES, LANES), jnp.float32),
            pltpu.SemaphoreType.DMA((rows // LANES + 1,)),
        ],
        megabytes=28,
        flops=12 * height * rows * rows,
        moved=height * rows * 8,
    )(place, both, head, back, skip, taps, free=(0, 1))[0]


def gated_part(long, outer, first):
    count, step, rows = long.shape
    value = long.reshape(count * step, rows).T.astype(jnp.float32)
    outer = outer.astype(jnp.float32)
    outer = jnp.concatenate([outer[:8] + first, outer[8:]], axis=0)
    return (outer * value).astype(jnp.bfloat16)


def gate_kernel(long_ref, outer_ref, first_ref, o_ref):
    o_ref[...] = gated_part(long_ref[...], outer_ref[...], first_ref[...])


def gate(long, outer, first):
    rows = outer.shape[0]
    width = long.shape[0] * long.shape[1]
    return call(
        gate_kernel,
        [
            pl.BlockSpec(long.shape, lambda n: (0, 0, 0)),
            pl.BlockSpec((rows, width), lambda n: (0, 0)),
            pl.BlockSpec((8, width), lambda n: (0, 0)),
        ],
        [pl.BlockSpec((rows, width), lambda n: (0, 0))],
        [((rows, width), jnp.bfloat16)],
        grid=(1,),
        moved=6 * rows * width,
    )(long, outer, first, free=(0,))[0]


def own_kernel(here_ref, gated_ref, weight_ref, o_ref):
    value = jnp.dot(gated_ref[...], weight_ref[...], preferred_element_type=jnp.float32)
    o_ref[...] = value.astype(o_ref.dtype)


def own_term(here, gated, out_weight, cols):
    rows, used = gated.shape
    wide = cols // 2
    return call(
        own_kernel,
        [
            pl.BlockSpec((rows, used), lambda n, h: (0, 0)),
            pl.BlockSpec((used, wide), lambda n, h: (0, h[0] * 2 + n)),
        ],
        [pl.BlockSpec((rows, wide), lambda n, h: (0, n))],
        [((rows, cols), jnp.bfloat16)],
        grid=(2,),
        flops=2 * rows * used * cols,
        moved=rows * cols * 2 + used * cols * 2,
        scalars=1,
    )(here, gated, out_weight)[0]


def last_kernel(
    place_ref, sent_ref, dealt_ref, first_ref, sum_ref, mine_ref, theirs_ref, *refs
):
    blocks, (weight_ref, o_ref, *scratch) = (refs[:4], refs[4:])
    outer_buf, weight_buf, block_buf, sum_buf, out_buf, gated_ref, sems = scratch
    here, quarter = (place_ref[0], place_ref[1])
    rows, used = outer_buf.shape[1:]
    wide = out_buf.shape[2]
    cols = 4 * wide
    pairs = [(mine_ref.at[:, pl.ds(used, used)], outer_buf.at[0]), (theirs_ref, outer_buf.at[1])]
    gates = [pltpu.make_async_copy(a, b, sems.at[g]) for g, (a, b) in enumerate(pairs)]
    for copy in gates:
        copy.start()
    places, inputs = ([], [])
    for k in range(4):
        column = pl.multiple_of((quarter ^ k) * wide, wide)
        places.append(pl.ds(column, wide))
        ours = pl.multiple_of(here * cols + column, wide)
        pairs = [
            (blocks[k], block_buf.at[k]),
            (weight_ref.at[pl.ds(used, used), pl.ds(ours, wide)], weight_buf.at[k]),
            (sum_ref.at[:, places[k]], sum_buf.at[k]),
        ]
        inputs.append(
            [pltpu.make_async_copy(a, b, sems.at[2 + 3 * k + i]) for i, (a, b) in enumerate(pairs)]
        )
        for copy in inputs[k]:
            copy.start()
    for g in range(2):
        gates[g].wait()
        long = dealt_ref[:, here if g == 0 else 1 - here]
        gated_ref[g] = gated_part(long, outer_buf[g], first_ref[g])
    outputs = []
    for k in range(4):
        for copy in inputs[k]:
            copy.wait()
        value = sum_buf[k].astype(jnp.float32)
        for left, right in (
            (sent_ref[...], block_buf[k, :used]),
            (gated_ref[1], block_buf[k, used:]),
            (gated_ref[0], weight_buf[k]),
        ):
            value = value + jnp.dot(left, right, preferred_element_type=jnp.float32)
        out_buf[k] = value.astype(out_buf.dtype)
        outputs.append(pltpu.make_async_copy(out_buf.at[k], o_ref.at[:, places[k]], sems.at[14 + k]))
        outputs[k].start()
    for copy in outputs:
        copy.wait()


def last_term(place, sent, dealt, first, total, mine, theirs, blocks, out_weight):
    rows, cols = total.shape
    chan = mine.shape[1]
    wide = cols // 4
    used = chan // 2
    vmem, anywhere = (pl.BlockSpec(memory_space=pltpu.VMEM), pl.BlockSpec(memory_space=pl.ANY))
    bf16 = jnp.bfloat16
    return call(
        last_kernel,
        [pl.BlockSpec(memory_space=pltpu.SMEM), vmem, vmem, vmem] + [anywhere] * 8,
        [anywhere],
        [((rows, cols), bf16)],
        scratch=[
            pltpu.VMEM((2, rows, used), bf16),
            pltpu.VMEM((4, used, wide), bf16),
            pltpu.VMEM((4, chan, wide), bf16),
            pltpu.VMEM((4, rows, wide), bf16),
            pltpu.VMEM((4, rows, wide), bf16),
            pltpu.VMEM((2, rows, used), bf16),
            pltpu.SemaphoreType.DMA((18,)),
        ],
        megabytes=32,
        flops=24 * rows * used * wide,
        moved=rows * wide * 16 + used * wide * 24,
    )(place, sent, dealt, first, total, mine, theirs, *blocks, out_weight, free=(0, 1, 2, 3))[0]


def exchanged(value):
    return lax.all_to_all(value, "ctx", 0, 0, tiled=True)


def to_groups(values):
    groups = lax.axis_size("ch")
    return [
        lax.ppermute(value, "ch", [(g, (g + s) % groups) for g in range(groups)])
        for s, value in enumerate(values, 1)
    ]


def any_groups(long, outer, out_weight):
    rows, chan = outer.shape
    groups = lax.axis_size("ch")
    here = lax.axis_index("ch")
    cols = out_weight.shape[1] // groups
    gated = gated_part(long, outer, jnp.zeros((8, chan), jnp.float32))
    total = jnp.zeros((rows, cols), jnp.float32)
    weights = [
        lax.dynamic_slice(out_weight, (0, (here + s) % groups * cols), (chan, cols))
        for s in range(groups)
    ]
    values = [gated] + to_groups([gated] * (groups - 1))
    for value, weight in zip(values, weights[:1] + to_groups(weights[1:])):
        total = total + jnp.dot(value, weight, preferred_element_type=jnp.float32)
    return total.astype(jnp.bfloat16)


def local(streams, short_taps, filters, skip_gain, out_weight):
    rows, _, chan = streams.shape
    count = lax.axis_size("ctx")
    groups = lax.axis_size("ch")
    own = chan // count
    step = own // 2
    fast = groups == 2 and count % 4 == 0 and own % 32 == 0 and LANES % step == 0
    fast = fast and chan // 4 + 2 * LANES <= rows and 2 * count <= LANES
    after = lax.optimization_barrier
    position, here = (lax.axis_index("ctx"), lax.axis_index("ch"))
    head = jnp.asarray(head_table(2 * rows))
    back = jnp.asarray(inverse_table(2 * rows))
    streams = streams.transpose(1, 0, 2)
    parts = 2 if fast else 1
    skip = skip_gain.reshape(parts, count, own // parts)
    skip = lax.dynamic_index_in_dim(skip, position, 1, False)
    skip = jnp.broadcast_to(skip.reshape(own, 1), (own, LANES))
    if not fast:
        both, tail = turned(filters, streams, count, parts)
        edges = passed_along(tail, "ctx", 1)
        both = exchanged(with_inner(both, streams, edges, short_taps, parts))
        both = both.reshape(count, 2 * own, rows)
        outer = outer_gate(streams, 2, edges[2:], short_taps[:, 2:], parts)
        none = jnp.zeros((2, 8, LANES), jnp.float32)
        long = long_conv(both, head, back, skip, none, jnp.zeros((1,), jnp.int32), None)
        return any_groups(exchanged(long[:, 0]), outer, out_weight)
    per = LANES // step
    place = (position % per)[None]
    taps = short_taps[:, :2].reshape(6, 2, chan // 2)
    taps = lax.dynamic_slice(taps, (0, 0, position // per * LANES), (6, 2, LANES))
    taps = jnp.pad(taps.transpose(1, 0, 2), ((0, 0), (0, 2), (0, 0)))
    both = exchanged(deal(filters, streams, short_taps, count))
    cols = out_weight.shape[1] // groups
    wide = cols // 4
    columns = (1 - here) * cols + position % 4 * wide
    near = lax.dynamic_slice(out_weight, (0, columns), (chan, wide))
    near, skip, taps = after((near, skip, taps))
    near = to_groups([near])[0]
    none = jnp.zeros((1, 2, chan), jnp.float32)
    none, near = after((none, near))
    outer = outer_gate(streams, 2, none, short_taps[:, 2:], 2)
    theirs = to_groups([outer[:, chan // 2 :]])[0]

    def swapped(value, bit):
        return lax.ppermute(value, "ctx", [(i, i ^ bit) for i in range(count)])

    across = swapped(near, 2)
    both, outer, theirs = after((both, outer, theirs))
    early = long_conv(both, head, back, skip, taps, place, 0)[:, 0]
    edges = lax.dynamic_slice(
        both, (jnp.maximum(position - 1, 0), 4 * step, 2 * LANES), (1, 8, chan // 4)
    )
    edges = jnp.where(position == 0, 0.0, edges.reshape(2, chan).astype(jnp.float32))
    first = jnp.stack(
        [short_taps[1, 2] * edges[1] + short_taps[2, 2] * edges[0], short_taps[2, 2] * edges[1]]
    )
    first = jnp.pad(first, ((0, 6), (0, 0)))
    other = to_groups([first[:, chan // 2 :]])[0]
    both, _ = after((both, early))
    late = long_conv(both, head, back, skip, taps, place, 1, copies=groups)
    late, across = after((late, across))
    blocks = [near, swapped(near, 1), across, swapped(across, 1)]
    early, late, other, first = after((exchanged(early), late, other, first))
    gated = gate(early, outer, first)
    sent = to_groups([gated])[0]
    dealt = lax.all_to_all(
        late.reshape(count * groups, step, rows), ("ctx", "ch"), 0, 0, tiled=True
    )
    dealt = dealt.reshape(count, groups, step, rows)
    total = own_term(here[None], gated, out_weight, cols)
    place = jnp.stack([here, position % 4])
    first = jnp.stack([first[:, chan // 2 :], other])
    return last_term(place, sent, dealt, first, total, outer, theirs, blocks, out_weight)


def solution(mesh):
    return jax.shard_map(
        local,
        mesh=mesh,
        in_specs=(
            P("ctx", None, "ch"),
            P(None, None, "ch"),
            P("ctx", "ch"),
            P("ch"),
            P("ch", None),
        ),
        out_specs=P("ctx", "ch"),
        check_vma=False,
    )
```

```python
import functools

import jax
import jax.numpy as jnp
import ml_dtypes
import numpy as np
from jax import lax
from jax.experimental import pallas as pl
from jax.experimental.pallas import tpu as pltpu
from jax.sharding import PartitionSpec as P

LANES = 128


def passed_along(value, axis, steps):
    count = lax.axis_size(axis)
    initial, last = (max(0, -steps), min(count, count - steps))
    return lax.ppermute(value, axis, [(source, source + steps) for source in range(initial, last)])


def paired_columns(half):
    order = np.arange(2 * half).reshape(2, half // LANES, LANES)
    return order.transpose(1, 0, 2).reshape(-1)


def head_table(size):
    half = size // 2
    rows = np.arange(half)[:, None]
    cols = np.arange(size)[None, :]
    freq = np.where(cols < half, cols, cols - half)
    angle = (rows * freq % size) * (2.0 * np.pi / size)
    nyquist = np.where(rows % 2 == 0, 1.0, -1.0)
    table = np.where(cols < half, np.cos(angle), np.where(cols == half, nyquist, -np.sin(angle)))
    return table[:, paired_columns(half)].astype(ml_dtypes.bfloat16)


def inverse_table(size):
    half = size // 2
    rows = np.arange(size)[:, None]
    places = half + np.arange(half)[None, :]
    freq = np.where(rows < half, rows, rows - half)
    angle = (places * freq % size) * (2.0 * np.pi / size)
    weight = np.where(freq == 0, 1.0, 2.0) / size
    nyquist = np.where(places % 2 == 0, 1.0, -1.0) / size
    table = np.where(
        rows < half, weight * np.cos(angle), np.where(rows == half, nyquist, -weight * np.sin(angle))
    )
    return table[paired_columns(half)].astype(ml_dtypes.bfloat16)


def call(kernel, in_specs, out_specs, outs, grid=(), scratch=(), megabytes=16, flops=0, moved=0, scalars=0, aliases=None):
    inner = pl.pallas_call(
        kernel,
        grid_spec=pltpu.PrefetchScalarGridSpec(
            num_scalar_prefetch=scalars,
            grid=grid,
            in_specs=in_specs,
            out_specs=out_specs,
            scratch_shapes=list(scratch),
        ),
        out_shape=[pltpu.HBM(shape, dtype) for shape, dtype in outs],
        input_output_aliases=aliases or {},
        compiler_params=pltpu.CompilerParams(vmem_limit_bytes=megabytes * 1024 * 1024),
        cost_estimate=pl.CostEstimate(flops=flops, bytes_accessed=moved, transcendentals=0),
    )

    def run(*args, free=()):
        pinned = [
            a if k < scalars or k in free else pltpu.with_memory_space_constraint(a, pltpu.HBM)
            for k, a in enumerate(args)
        ]
        return inner(*pinned)

    return run


def store_turned(value, o_ref):
    o_ref[...] = value.T.reshape(o_ref.shape).astype(o_ref.dtype)


def turn_kernel(x_ref, s_ref, o_ref, tail_ref):
    tail_ref[...] = s_ref[:, s_ref.shape[1] - 2 :]
    store_turned(x_ref[...].astype(jnp.float32), o_ref)


def turned(x, streams, count, parts):
    rows, chan = x.shape
    own = chan // count
    last = min(rows, 16)
    tile = chan // parts
    return call(
        turn_kernel,
        [
            pl.BlockSpec((rows, tile), lambda p: (0, p)),
            pl.BlockSpec((3, last, tile), lambda p: (0, rows // last - 1, p)),
        ],
        [
            pl.BlockSpec((count, 1, own // parts, rows), lambda p: (0, 0, p, 0)),
            pl.BlockSpec((3, 2, tile), lambda p: (0, 0, p)),
        ],
        [((count, 2, own, rows), x.dtype), ((3, 2, chan), streams.dtype)],
        grid=(parts,),
        moved=4 * rows * chan,
    )(x, streams)


def mixed(s_ref, e_ref, t_ref, q):
    rows, width = s_ref.shape[1:]
    place = lax.broadcasted_iota(jnp.int32, (8, width), 0)
    now = s_ref[q].astype(jnp.float32)
    edge = e_ref[q].astype(jnp.float32)
    one, two = (pltpu.roll(now, 1, 0), pltpu.roll(now, 2, 0))
    one_top = jnp.where(place == 0, edge[1:2], one[:8])
    two_top = jnp.where(place == 0, edge[0:1], jnp.where(place == 1, edge[1:2], two[:8]))
    one = jnp.concatenate([one_top, one[8:]], axis=0)
    two = jnp.concatenate([two_top, two[8:]], axis=0)
    return t_ref[0, q : q + 1] * now + t_ref[1, q : q + 1] * one + t_ref[2, q : q + 1] * two


def inner_kernel(s_ref, e_ref, t_ref, _, o_ref):
    store_turned(mixed(s_ref, e_ref, t_ref, 0) * mixed(s_ref, e_ref, t_ref, 1), o_ref)


def with_inner(both, streams, edges, taps, parts):
    count, _, own, rows = both.shape
    chan = count * own
    tile = chan // parts
    return call(
        inner_kernel,
        [
            pl.BlockSpec((2, rows, tile), lambda p: (0, 0, p)),
            pl.BlockSpec((3, 2, tile), lambda p: (0, 0, p)),
            pl.BlockSpec((3, 3, tile), lambda p: (0, 0, p)),
            pl.BlockSpec(memory_space=pl.ANY),
        ],
        [pl.BlockSpec((count, 1, own // parts, rows), lambda p: (0, 1, p, 0))],
        [(both.shape, both.dtype)],
        grid=(parts,),
        megabytes=32,
        moved=6 * rows * chan,
        aliases={3: 0},
    )(streams, edges, taps, both)[0]


def outer_kernel(s_ref, e_ref, t_ref, o_ref):
    o_ref[...] = mixed(s_ref, e_ref, t_ref, 0).astype(o_ref.dtype)


def outer_gate(streams, which, edges, taps, parts):
    _, rows, chan = streams.shape
    tile = chan // parts
    return call(
        outer_kernel,
        [
            pl.BlockSpec((1, rows, tile), lambda p: (which, 0, p)),
            pl.BlockSpec((1, 2, tile), lambda p: (0, 0, p)),
            pl.BlockSpec((3, 1, tile), lambda p: (0, 0, p)),
        ],
        [pl.BlockSpec((rows, tile), lambda p: (0, p))],
        [((rows, chan), jnp.bfloat16)],
        grid=(parts,),
        megabytes=32,
        moved=4 * rows * chan,
    )(streams, edges, taps)[0]


def deal_kernel(f_ref, s_ref, t_ref, o_ref, f_buf, s_buf, out_buf, sems):
    count, height, _, wide = out_buf.shape
    step = height - 1
    rows, chan = f_ref.shape
    tile = chan // 4
    few = count // 2
    per = LANES // step
    ins = []
    for q in range(4):
        lanes = pl.ds(q * tile, tile)
        ins.append(pltpu.make_async_copy(f_ref.at[:, lanes], f_buf.at[q], sems.at[2 * q]))
        ins.append(
            pltpu.make_async_copy(s_ref.at[pl.ds(0, 2), :, lanes], s_buf.at[q], sems.at[2 * q + 1])
        )
    for copy in ins:
        copy.start()
    outs = []
    for q in range(4):
        p, owner = (q // 2, q % 2 * few)
        lanes = slice(q * tile, (q + 1) * tile)
        ins[2 * q].wait()
        values = [f_buf[q].astype(jnp.float32)]
        ins[2 * q + 1].wait()
        both = []
        for stream in range(2):
            now = s_buf[q, stream].astype(jnp.float32)
            value = t_ref[0, stream : stream + 1, lanes] * now
            value = value + t_ref[1, stream : stream + 1, lanes] * pltpu.roll(now, 1, 0)
            both.append(value + t_ref[2, stream : stream + 1, lanes] * pltpu.roll(now, 2, 0))
        values.append(both[0] * both[1])
        for k in range(2):
            value = values[k].T.astype(o_ref.dtype)
            for half in range(2):
                place = (4 * p + 2 * k + half) * step // 8
                out_buf[owner : owner + few, place : place + step // 8] = value[
                    :, half * wide : (half + 1) * wide
                ].reshape(few, step // 8, 8, wide)
        ends = [s_buf[q, k, a : a + 2].astype(jnp.float32) for a in (0, rows - 2) for k in range(2)]
        ends = jnp.concatenate(ends, axis=0).astype(o_ref.dtype)
        for g in range(tile // LANES):
            value = jnp.broadcast_to(ends[:, g * LANES : (g + 1) * LANES][None], (per, 8, LANES))
            first = owner + g * per
            out_buf[first : first + per, height - 1, :, p * LANES : (p + 1) * LANES] = value
        some = (pl.ds(owner, few), pl.ds(p * step // 2, step // 2))
        outs.append(pltpu.make_async_copy(out_buf.at[some], o_ref.at[some], sems.at[8 + q]))
        outs[q].start()
    some = pl.ds(height - 1, 1)
    outs.append(pltpu.make_async_copy(out_buf.at[:, some], o_ref.at[:, some], sems.at[12]))
    outs[4].start()
    for copy in outs:
        copy.wait()


def deal(filters, streams, taps, count):
    rows, chan = filters.shape
    shape = (count, chan // count // 2 + 1, 8, rows // 2)
    anywhere, vmem = (pl.BlockSpec(memory_space=pl.ANY), pl.BlockSpec(memory_space=pltpu.VMEM))
    bf16 = jnp.bfloat16
    return call(
        deal_kernel,
        [anywhere, anywhere, vmem],
        [anywhere],
        [(shape, bf16)],
        scratch=[
            pltpu.VMEM((4, rows, chan // 4), bf16),
            pltpu.VMEM((4, 2, rows, chan // 4), bf16),
            pltpu.VMEM(shape, bf16),
            pltpu.SemaphoreType.DMA((13,)),
        ],
        megabytes=32,
        moved=10 * rows * chan,
    )(filters, streams, taps)[0]


def first_tokens(ends, taps, place):
    count = ends.shape[0]

    def at(row):
        return ends[:, row].astype(jnp.float32)

    block = lax.broadcasted_iota(jnp.int32, (count, LANES), 0)

    def before(row):
        return jnp.where(block == 0, 0.0, pltpu.roll(at(row), 1, 0))

    values = [1.0, 1.0]
    for q in range(2):
        t0, t1, t2 = (taps[2 * m + q : 2 * m + q + 1] for m in range(3))
        one, two = (at(2 * q), at(2 * q + 1))
        far, near = (before(4 + 2 * q), before(5 + 2 * q))
        values[0] = values[0] * (t0 * one + t1 * near + t2 * far)
        values[1] = values[1] * (t0 * two + t1 * one + t2 * near)
    rest = jnp.zeros((LANES - 2 * count, LANES), jnp.float32)
    return jnp.concatenate(values + [rest], axis=0).T


def conv_kernel(split, place_ref, both_ref, head_ref, back_ref, skip_ref, taps_ref, o_ref, *scratch):
    head_buf, back_buf, spec_ref, factor_ref, low_ref, x_buf, fix_ref, sems = scratch
    count, _, part, rows = o_ref.shape
    tiles = rows // LANES
    high = min(part, 16)
    group = 2
    low = part * (split or 0)
    copies = [
        pltpu.make_async_copy(
            head_ref.at[:, pl.ds(t * 2 * LANES, 2 * LANES)], head_buf.at[t], sems.at[t]
        )
        for t in range(tiles)
    ]
    copies.append(pltpu.make_async_copy(back_ref, back_buf, sems.at[tiles]))
    for copy in copies:
        copy.start()
    height = count * part

    def arrived(kind):
        if split is None:
            return both_ref[:, kind * part : (kind + 1) * part].reshape(height, rows)
        first = (4 * split + 2 * kind) * part // 8
        halves = [both_ref[:, a : a + part // 8] for a in (first, first + part // 8)]
        return jnp.concatenate([h.reshape(height, rows // 2) for h in halves], axis=1)

    x_buf[...] = arrived(1).reshape(count, part, rows)
    if split is not None:
        ends = both_ref[:, both_ref.shape[1] - 1, :, split * LANES : (split + 1) * LANES]
        fix_ref[...] = first_tokens(ends, taps_ref[split], place_ref[0])
        mine = fix_ref[pl.ds(pl.multiple_of(place_ref[0] * part, part), part), :]
        lane = lax.broadcasted_iota(jnp.int32, (part, LANES), 1)
        for block in range(count):
            one = pltpu.roll(mine, (LANES - block) % LANES, 1)
            two = pltpu.roll(mine, (LANES - block - count + 1) % LANES, 1)
            value = x_buf[block, :, :LANES].astype(jnp.float32)
            value = jnp.where(lane == 0, one, jnp.where(lane == 1, two, value))
            x_buf[block, :, :LANES] = value.astype(x_buf.dtype)
    filters = arrived(0)
    odd = lax.broadcasted_iota(jnp.int32, (height, 2 * LANES), 1) % 2 == 1
    lane = lax.broadcasted_iota(jnp.int32, (high, LANES), 1)

    lane0 = lax.broadcasted_iota(jnp.int32, (height, LANES), 1) == 0

    def spectra(t):
        value = jnp.dot(filters, head_buf[t], preferred_element_type=jnp.float32)
        earlier = jnp.concatenate([jnp.zeros_like(value[:part]), value[:-part]], axis=0)
        window = earlier + jnp.where(odd, -value, value)
        real, imag = (window[:, :LANES], window[:, LANES:])
        factor_ref[t, :, :LANES] = real
        less, more = (imag - real, real + imag)
        if t == 0:
            less, more = (jnp.where(lane0, real, less), jnp.where(lane0, imag, more))
        factor_ref[t, :, LANES : 2 * LANES] = less
        factor_ref[t, :, 2 * LANES :] = more
        spec_ref[t] = jnp.dot(
            x_buf[...].reshape(height, rows), head_buf[t], preferred_element_type=jnp.float32
        )

    def products(t, slab):
        base = slab * high
        if not isinstance(base, int):
            base = pl.multiple_of(base, high)
        for start in range(0, count, group):
            sums = [[None] * 3 for _ in range(group)]
            factors = {}
            for source in range(start + group):
                place = pl.ds(base + source * part, high)
                real, imag = (spec_ref[t, place, :LANES], spec_ref[t, place, LANES:])
                both = real + imag
                for g in range(group):
                    lag = start + g - source
                    if lag < 0:
                        continue
                    if lag not in factors:
                        place = pl.ds(base + lag * part, high)
                        factors[lag] = [
                            factor_ref[t, place, c * LANES : (c + 1) * LANES] for c in range(3)
                        ]
                    a, b, c = factors[lag]
                    terms = (both * a, real * b, imag * c)
                    before = sums[g]
                    sums[g] = [u if p is None else p + u for p, u in zip(before, terms)]
            for g in range(group):
                a, b, c = sums[g]
                place = pl.ds(base + (start + g) * part, high)
                re, im = (a - c, a + b)
                if t == 0:
                    re, im = (jnp.where(lane == 0, b, re), jnp.where(lane == 0, c, im))
                low_ref[place, t * 2 * LANES : t * 2 * LANES + LANES] = re.astype(low_ref.dtype)
                low_ref[place, t * 2 * LANES + LANES : (t + 1) * 2 * LANES] = im.astype(low_ref.dtype)

    for copy in copies:
        copy.wait()
    for t in range(tiles):
        spectra(t)
        if split is not None:
            for slab in range(part // high):
                products(t, slab)
        else:

            def one_slab(slab, carry, t=t):
                products(t, slab)
                return carry

            lax.fori_loop(0, part // high, one_slab, 0)
    back = jnp.dot(
        low_ref[...].astype(jnp.bfloat16), back_buf[...], preferred_element_type=jnp.float32
    )
    value = back.reshape(count, part, rows)
    skip = skip_ref[low : low + part, :1][None]
    value = value + skip * x_buf[...].astype(jnp.float32)
    for copy in range(o_ref.shape[1]):
        o_ref[:, copy] = value.astype(o_ref.dtype)


def long_conv(both, head, back, skip, taps, place, split, copies=1):
    count, rows = (both.shape[0], head.shape[0])
    own = skip.shape[0]
    part = own if split is None else own // 2
    height = count * part
    vmem, anywhere = (pl.BlockSpec(memory_space=pltpu.VMEM), pl.BlockSpec(memory_space=pl.ANY))
    return call(
        functools.partial(conv_kernel, split),
        [pl.BlockSpec(memory_space=pltpu.SMEM), vmem, anywhere, anywhere, vmem, vmem],
        [vmem],
        [((count, copies, part, rows), jnp.bfloat16)],
        scratch=[
            pltpu.VMEM((rows // LANES, rows, 2 * LANES), jnp.bfloat16),
            pltpu.VMEM(back.shape, jnp.bfloat16),
            pltpu.VMEM((rows // LANES, height, 2 * LANES), jnp.float32),
            pltpu.VMEM((rows // LANES, height, 3 * LANES), jnp.float32),
            pltpu.VMEM((height, 2 * rows), jnp.float32 if part % 16 else jnp.bfloat16),
            pltpu.VMEM((count, part, rows), jnp.bfloat16),
            pltpu.VMEM((LANES, LANES), jnp.float32),
            pltpu.SemaphoreType.DMA((rows // LANES + 1,)),
        ],
        megabytes=28,
        flops=12 * height * rows * rows,
        moved=height * rows * 8,
    )(place, both, head, back, skip, taps, free=(0, 1))[0]


def gated_part(long, outer, first):
    count, step, rows = long.shape
    value = long.reshape(count * step, rows).T.astype(jnp.float32)
    outer = outer.astype(jnp.float32)
    outer = jnp.concatenate([outer[:8] + first, outer[8:]], axis=0)
    return (outer * value).astype(jnp.bfloat16)


def gate_kernel(long_ref, outer_ref, first_ref, o_ref):
    o_ref[...] = gated_part(long_ref[...], outer_ref[...], first_ref[...])


def gate(long, outer, first):
    rows = outer.shape[0]
    width = long.shape[0] * long.shape[1]
    return call(
        gate_kernel,
        [
            pl.BlockSpec(long.shape, lambda n: (0, 0, 0)),
            pl.BlockSpec((rows, width), lambda n: (0, 0)),
            pl.BlockSpec((8, width), lambda n: (0, 0)),
        ],
        [pl.BlockSpec((rows, width), lambda n: (0, 0))],
        [((rows, width), jnp.bfloat16)],
        grid=(1,),
        moved=6 * rows * width,
    )(long, outer, first, free=(0,))[0]


def own_kernel(here_ref, gated_ref, weight_ref, o_ref):
    value = jnp.dot(gated_ref[...], weight_ref[...], preferred_element_type=jnp.float32)
    o_ref[...] = value.astype(o_ref.dtype)


def own_term(here, gated, out_weight, cols):
    rows, used = gated.shape
    wide = cols // 2
    return call(
        own_kernel,
        [
            pl.BlockSpec((rows, used), lambda n, h: (0, 0)),
            pl.BlockSpec((used, wide), lambda n, h: (0, h[0] * 2 + n)),
        ],
        [pl.BlockSpec((rows, wide), lambda n, h: (0, n))],
        [((rows, cols), jnp.bfloat16)],
        grid=(2,),
        flops=2 * rows * used * cols,
        moved=rows * cols * 2 + used * cols * 2,
        scalars=1,
    )(here, gated, out_weight)[0]


def last_kernel(
    place_ref, sent_ref, dealt_ref, first_ref, sum_ref, mine_ref, theirs_ref, *refs
):
    blocks, (weight_ref, o_ref, *scratch) = (refs[:4], refs[4:])
    outer_buf, weight_buf, block_buf, sum_buf, out_buf, gated_ref, sems = scratch
    here, quarter = (place_ref[0], place_ref[1])
    rows, used = outer_buf.shape[1:]
    wide = out_buf.shape[2]
    cols = 4 * wide
    pairs = [(mine_ref.at[:, pl.ds(used, used)], outer_buf.at[0]), (theirs_ref, outer_buf.at[1])]
    gates = [pltpu.make_async_copy(a, b, sems.at[g]) for g, (a, b) in enumerate(pairs)]
    for copy in gates:
        copy.start()
    places, inputs = ([], [])
    for k in range(4):
        column = pl.multiple_of((quarter ^ k) * wide, wide)
        places.append(pl.ds(column, wide))
        ours = pl.multiple_of(here * cols + column, wide)
        pairs = [
            (blocks[k], block_buf.at[k]),
            (weight_ref.at[pl.ds(used, used), pl.ds(ours, wide)], weight_buf.at[k]),
            (sum_ref.at[:, places[k]], sum_buf.at[k]),
        ]
        inputs.append(
            [pltpu.make_async_copy(a, b, sems.at[2 + 3 * k + i]) for i, (a, b) in enumerate(pairs)]
        )
        for copy in inputs[k]:
            copy.start()
    for g in range(2):
        gates[g].wait()
        long = dealt_ref[:, here if g == 0 else 1 - here]
        gated_ref[g] = gated_part(long, outer_buf[g], first_ref[g])
    outputs = []
    for k in range(4):
        for copy in inputs[k]:
            copy.wait()
        value = sum_buf[k].astype(jnp.float32)
        for left, right in (
            (sent_ref[...], block_buf[k, :used]),
            (gated_ref[1], block_buf[k, used:]),
            (gated_ref[0], weight_buf[k]),
        ):
            value = value + jnp.dot(left, right, preferred_element_type=jnp.float32)
        out_buf[k] = value.astype(out_buf.dtype)
        outputs.append(pltpu.make_async_copy(out_buf.at[k], o_ref.at[:, places[k]], sems.at[14 + k]))
        outputs[k].start()
    for copy in outputs:
        copy.wait()


def last_term(place, sent, dealt, first, total, mine, theirs, blocks, out_weight):
    rows, cols = total.shape
    chan = mine.shape[1]
    wide = cols // 4
    used = chan // 2
    vmem, anywhere = (pl.BlockSpec(memory_space=pltpu.VMEM), pl.BlockSpec(memory_space=pl.ANY))
    bf16 = jnp.bfloat16
    return call(
        last_kernel,
        [pl.BlockSpec(memory_space=pltpu.SMEM), vmem, vmem, vmem] + [anywhere] * 8,
        [anywhere],
        [((rows, cols), bf16)],
        scratch=[
            pltpu.VMEM((2, rows, used), bf16),
            pltpu.VMEM((4, used, wide), bf16),
            pltpu.VMEM((4, chan, wide), bf16),
            pltpu.VMEM((4, rows, wide), bf16),
            pltpu.VMEM((4, rows, wide), bf16),
            pltpu.VMEM((2, rows, used), bf16),
            pltpu.SemaphoreType.DMA((18,)),
        ],
        megabytes=32,
        flops=24 * rows * used * wide,
        moved=rows * wide * 16 + used * wide * 24,
    )(place, sent, dealt, first, total, mine, theirs, *blocks, out_weight, free=(0, 1, 2, 3))[0]


def exchanged(value):
    return lax.all_to_all(value, "ctx", 0, 0, tiled=True)


def to_groups(values):
    groups = lax.axis_size("ch")
    return [
        lax.ppermute(value, "ch", [(g, (g + s) % groups) for g in range(groups)])
        for s, value in enumerate(values, 1)
    ]


def any_groups(long, outer, out_weight):
    rows, chan = outer.shape
    groups = lax.axis_size("ch")
    here = lax.axis_index("ch")
    cols = out_weight.shape[1] // groups
    gated = gated_part(long, outer, jnp.zeros((8, chan), jnp.float32))
    total = jnp.zeros((rows, cols), jnp.float32)
    weights = [
        lax.dynamic_slice(out_weight, (0, (here + s) % groups * cols), (chan, cols))
        for s in range(groups)
    ]
    values = [gated] + to_groups([gated] * (groups - 1))
    for value, weight in zip(values, weights[:1] + to_groups(weights[1:])):
        total = total + jnp.dot(value, weight, preferred_element_type=jnp.float32)
    return total.astype(jnp.bfloat16)


def local(streams, short_taps, filters, skip_gain, out_weight):
    rows, _, chan = streams.shape
    count = lax.axis_size("ctx")
    groups = lax.axis_size("ch")
    own = chan // count
    step = own // 2
    fast = groups == 2 and count % 4 == 0 and own % 32 == 0 and count % 2 == 0 and LANES % step == 0
    fast = fast and rows % (4 * LANES) == 0 and 2 * count <= LANES and chan % (4 * LANES) == 0
    after = lax.optimization_barrier
    position, here = (lax.axis_index("ctx"), lax.axis_index("ch"))
    head = jnp.asarray(head_table(2 * rows))
    back = jnp.asarray(inverse_table(2 * rows))
    streams = streams.transpose(1, 0, 2)
    parts = 2 if fast else 1
    skip = skip_gain.reshape(parts, count, own // parts)
    skip = lax.dynamic_index_in_dim(skip, position, 1, False)
    skip = jnp.broadcast_to(skip.reshape(own, 1), (own, LANES))
    if not fast:
        both, tail = turned(filters, streams, count, parts)
        edges = passed_along(tail, "ctx", 1)
        both = exchanged(with_inner(both, streams, edges, short_taps, parts))
        both = both.reshape(count, 2 * own, rows)
        outer = outer_gate(streams, 2, edges[2:], short_taps[:, 2:], parts)
        none = jnp.zeros((2, 8, LANES), jnp.float32)
        long = long_conv(both, head, back, skip, none, jnp.zeros((1,), jnp.int32), None)
        return any_groups(exchanged(long[:, 0]), outer, out_weight)
    per = LANES // step
    place = (position % per)[None]
    taps = short_taps[:, :2].reshape(6, 2, chan // 2)
    taps = lax.dynamic_slice(taps, (0, 0, position // per * LANES), (6, 2, LANES))
    taps = jnp.pad(taps.transpose(1, 0, 2), ((0, 0), (0, 2), (0, 0)))
    both = exchanged(deal(filters, streams, short_taps, count))
    cols = out_weight.shape[1] // groups
    wide = cols // 4
    columns = (1 - here) * cols + position % 4 * wide
    near = lax.dynamic_slice(out_weight, (0, columns), (chan, wide))
    near, skip, taps = after((near, skip, taps))
    near = to_groups([near])[0]
    none = jnp.zeros((1, 2, chan), jnp.float32)
    none, near = after((none, near))
    outer = outer_gate(streams, 2, none, short_taps[:, 2:], 2)
    theirs = to_groups([outer[:, chan // 2 :]])[0]

    def swapped(value, bit):
        return lax.ppermute(value, "ctx", [(i, i ^ bit) for i in range(count)])

    across = swapped(near, 2)
    edges = passed_along(streams[2, rows - 2 :], "ctx", 1).astype(jnp.float32)
    both, outer, theirs, edges = after((both, outer, theirs, edges))
    early = long_conv(both, head, back, skip, taps, place, 0)[:, 0]
    first = jnp.stack(
        [short_taps[1, 2] * edges[1] + short_taps[2, 2] * edges[0], short_taps[2, 2] * edges[1]]
    )
    first = jnp.pad(first, ((0, 6), (0, 0)))
    other = to_groups([first[:, chan // 2 :]])[0]
    both, _ = after((both, early))
    late = long_conv(both, head, back, skip, taps, place, 1, copies=groups)
    late, across = after((late, across))
    blocks = [near, swapped(near, 1), across, swapped(across, 1)]
    early, late, other, first = after((exchanged(early), late, other, first))
    gated = gate(early, outer, first)
    sent = to_groups([gated])[0]
    dealt = lax.all_to_all(
        late.reshape(count * groups, step, rows), ("ctx", "ch"), 0, 0, tiled=True
    )
    dealt = dealt.reshape(count, groups, step, rows)
    total = own_term(here[None], gated, out_weight, cols)
    place = jnp.stack([here, position % 4])
    first = jnp.stack([first[:, chan // 2 :], other])
    return last_term(place, sent, dealt, first, total, outer, theirs, blocks, out_weight)


def solution(mesh):
    return jax.shard_map(
        local,
        mesh=mesh,
        in_specs=(
            P("ctx", None, "ch"),
            P(None, None, "ch"),
            P("ctx", "ch"),
            P("ch"),
            P("ch", None),
        ),
        out_specs=P("ctx", "ch"),
        check_vma=False,
    )
```

```python
import functools

import jax
import jax.numpy as jnp
import ml_dtypes
import numpy as np
from jax import lax
from jax.experimental import pallas as pl
from jax.experimental.pallas import tpu as pltpu
from jax.sharding import PartitionSpec as P

LANES = 128


def passed_along(value, axis, steps):
    count = lax.axis_size(axis)
    initial, last = (max(0, -steps), min(count, count - steps))
    return lax.ppermute(value, axis, [(source, source + steps) for source in range(initial, last)])


def paired_columns(half):
    order = np.arange(2 * half).reshape(2, half // LANES, LANES)
    return order.transpose(1, 0, 2).reshape(-1)


def head_table(size):
    half = size // 2
    rows = np.arange(half)[:, None]
    cols = np.arange(size)[None, :]
    freq = np.where(cols < half, cols, cols - half)
    angle = (rows * freq % size) * (2.0 * np.pi / size)
    nyquist = np.where(rows % 2 == 0, 1.0, -1.0)
    table = np.where(cols < half, np.cos(angle), np.where(cols == half, nyquist, -np.sin(angle)))
    return table[:, paired_columns(half)].astype(ml_dtypes.bfloat16)


def inverse_table(size):
    half = size // 2
    rows = np.arange(size)[:, None]
    places = half + np.arange(half)[None, :]
    freq = np.where(rows < half, rows, rows - half)
    angle = (places * freq % size) * (2.0 * np.pi / size)
    weight = np.where(freq == 0, 1.0, 2.0) / size
    nyquist = np.where(places % 2 == 0, 1.0, -1.0) / size
    table = np.where(
        rows < half, weight * np.cos(angle), np.where(rows == half, nyquist, -weight * np.sin(angle))
    )
    return table[paired_columns(half)].astype(ml_dtypes.bfloat16)


def call(kernel, in_specs, out_specs, outs, grid=(), scratch=(), megabytes=16, flops=0, moved=0, scalars=0, aliases=None):
    inner = pl.pallas_call(
        kernel,
        grid_spec=pltpu.PrefetchScalarGridSpec(
            num_scalar_prefetch=scalars,
            grid=grid,
            in_specs=in_specs,
            out_specs=out_specs,
            scratch_shapes=list(scratch),
        ),
        out_shape=[pltpu.HBM(shape, dtype) for shape, dtype in outs],
        input_output_aliases=aliases or {},
        compiler_params=pltpu.CompilerParams(vmem_limit_bytes=megabytes * 1024 * 1024),
        cost_estimate=pl.CostEstimate(flops=flops, bytes_accessed=moved, transcendentals=0),
    )

    def run(*args, free=()):
        pinned = [
            a if k < scalars or k in free else pltpu.with_memory_space_constraint(a, pltpu.HBM)
            for k, a in enumerate(args)
        ]
        return inner(*pinned)

    return run


def store_turned(value, o_ref):
    o_ref[...] = value.T.reshape(o_ref.shape).astype(o_ref.dtype)


def turn_kernel(x_ref, s_ref, o_ref, tail_ref):
    tail_ref[...] = s_ref[:, s_ref.shape[1] - 2 :]
    store_turned(x_ref[...].astype(jnp.float32), o_ref)


def turned(x, streams, count, parts):
    rows, chan = x.shape
    own = chan // count
    last = min(rows, 16)
    tile = chan // parts
    return call(
        turn_kernel,
        [
            pl.BlockSpec((rows, tile), lambda p: (0, p)),
            pl.BlockSpec((3, last, tile), lambda p: (0, rows // last - 1, p)),
        ],
        [
            pl.BlockSpec((count, 1, own // parts, rows), lambda p: (0, 0, p, 0)),
            pl.BlockSpec((3, 2, tile), lambda p: (0, 0, p)),
        ],
        [((count, 2, own, rows), x.dtype), ((3, 2, chan), streams.dtype)],
        grid=(parts,),
        moved=4 * rows * chan,
    )(x, streams)


def mixed(s_ref, e_ref, t_ref, q):
    rows, width = s_ref.shape[1:]
    place = lax.broadcasted_iota(jnp.int32, (8, width), 0)
    now = s_ref[q].astype(jnp.float32)
    edge = e_ref[q].astype(jnp.float32)
    one, two = (pltpu.roll(now, 1, 0), pltpu.roll(now, 2, 0))
    one_top = jnp.where(place == 0, edge[1:2], one[:8])
    two_top = jnp.where(place == 0, edge[0:1], jnp.where(place == 1, edge[1:2], two[:8]))
    one = jnp.concatenate([one_top, one[8:]], axis=0)
    two = jnp.concatenate([two_top, two[8:]], axis=0)
    return t_ref[0, q : q + 1] * now + t_ref[1, q : q + 1] * one + t_ref[2, q : q + 1] * two


def inner_kernel(s_ref, e_ref, t_ref, _, o_ref):
    store_turned(mixed(s_ref, e_ref, t_ref, 0) * mixed(s_ref, e_ref, t_ref, 1), o_ref)


def with_inner(both, streams, edges, taps, parts):
    count, _, own, rows = both.shape
    chan = count * own
    tile = chan // parts
    return call(
        inner_kernel,
        [
            pl.BlockSpec((2, rows, tile), lambda p: (0, 0, p)),
            pl.BlockSpec((3, 2, tile), lambda p: (0, 0, p)),
            pl.BlockSpec((3, 3, tile), lambda p: (0, 0, p)),
            pl.BlockSpec(memory_space=pl.ANY),
        ],
        [pl.BlockSpec((count, 1, own // parts, rows), lambda p: (0, 1, p, 0))],
        [(both.shape, both.dtype)],
        grid=(parts,),
        megabytes=32,
        moved=6 * rows * chan,
        aliases={3: 0},
    )(streams, edges, taps, both)[0]


def outer_kernel(s_ref, e_ref, t_ref, o_ref):
    o_ref[...] = mixed(s_ref, e_ref, t_ref, 0).astype(o_ref.dtype)


def outer_gate(streams, which, edges, taps, parts):
    _, rows, chan = streams.shape
    tile = chan // parts
    return call(
        outer_kernel,
        [
            pl.BlockSpec((1, rows, tile), lambda p: (which, 0, p)),
            pl.BlockSpec((1, 2, tile), lambda p: (0, 0, p)),
            pl.BlockSpec((3, 1, tile), lambda p: (0, 0, p)),
        ],
        [pl.BlockSpec((rows, tile), lambda p: (0, p))],
        [((rows, chan), jnp.bfloat16)],
        grid=(parts,),
        megabytes=32,
        moved=4 * rows * chan,
    )(streams, edges, taps)[0]


def deal_kernel(f_ref, s_ref, t_ref, o_ref, f_buf, s_buf, out_buf, sems):
    count, height, _, _ = out_buf.shape
    rows, chan = f_ref.shape
    step = chan // count // 2
    tile = chan // 4
    few = count // 2
    per = LANES // step // 2
    ins = []
    for q in range(4):
        lanes = pl.ds(q * tile, tile)
        ins.append(pltpu.make_async_copy(f_ref.at[:, lanes], f_buf.at[q], sems.at[2 * q]))
        ins.append(
            pltpu.make_async_copy(s_ref.at[pl.ds(0, 2), :, lanes], s_buf.at[q], sems.at[2 * q + 1])
        )
    for copy in ins:
        copy.start()
    outs, edges = ([], [])
    for q in range(4):
        p, owner = (q // 2, q % 2 * few)
        lanes = slice(q * tile, (q + 1) * tile)
        ins[2 * q].wait()
        values = [f_buf[q].astype(jnp.float32)]
        ins[2 * q + 1].wait()
        both = []
        for stream in range(2):
            now = s_buf[q, stream].astype(jnp.float32)
            value = t_ref[0, stream : stream + 1, lanes] * now
            value = value + t_ref[1, stream : stream + 1, lanes] * pltpu.roll(now, 1, 0)
            both.append(value + t_ref[2, stream : stream + 1, lanes] * pltpu.roll(now, 2, 0))
        values.append(both[0] * both[1])
        for k in range(2):
            value = values[k].astype(o_ref.dtype).T
            for c in range(rows // LANES):
                place = ((2 * p + k) * rows // LANES + c) * step // 8
                out_buf[owner : owner + few, place : place + step // 8] = value[
                    :, c * LANES : (c + 1) * LANES
                ].reshape(few, step // 8, 8, LANES)
        ends = [s_buf[q, k, a : a + 2].astype(jnp.float32) for a in (0, rows - 2) for k in range(2)]
        ends = jnp.concatenate(ends, axis=0)
        edges.append(ends)
        if p == 1:
            for g in range(few // per):
                lanes = slice(g * LANES // 2, (g + 1) * LANES // 2)
                value = jnp.concatenate([edges[q - 2][:, lanes], edges[q][:, lanes]], axis=1)
                first = owner + g * per
                out_buf[first : first + per, height - 1] = jnp.broadcast_to(
                    value[None].astype(o_ref.dtype), (per, 8, LANES)
                )
        some = (pl.ds(owner, few), pl.ds(p * (height // 2), height // 2))
        outs.append(pltpu.make_async_copy(out_buf.at[some], o_ref.at[some], sems.at[8 + q]))
        outs[q].start()
    some = pl.ds(height - 1, 1)
    outs.append(pltpu.make_async_copy(out_buf.at[:, some], o_ref.at[:, some], sems.at[12]))
    outs[4].start()
    for copy in outs:
        copy.wait()


def deal(filters, streams, taps, count):
    rows, chan = filters.shape
    shape = (count, chan // count * rows // LANES // 4 + 1, 8, LANES)
    anywhere, vmem = (pl.BlockSpec(memory_space=pl.ANY), pl.BlockSpec(memory_space=pltpu.VMEM))
    bf16 = jnp.bfloat16
    return call(
        deal_kernel,
        [anywhere, anywhere, vmem],
        [anywhere],
        [(shape, bf16)],
        scratch=[
            pltpu.VMEM((4, rows, chan // 4), bf16),
            pltpu.VMEM((4, 2, rows, chan // 4), bf16),
            pltpu.VMEM(shape, bf16),
            pltpu.SemaphoreType.DMA((13,)),
        ],
        megabytes=32,
        moved=10 * rows * chan,
    )(filters, streams, taps)[0]


def first_tokens(ends, taps):
    count = ends.shape[0]

    def at(row):
        return ends[:, row].astype(jnp.float32)

    block = lax.broadcasted_iota(jnp.int32, (count, LANES), 0)

    def before(row):
        return jnp.where(block == 0, 0.0, pltpu.roll(at(row), 1, 0))

    values = [1.0, 1.0]
    for q in range(2):
        t0, t1, t2 = (taps[2 * m + q : 2 * m + q + 1] for m in range(3))
        one, two = (at(2 * q), at(2 * q + 1))
        far, near = (before(4 + 2 * q), before(5 + 2 * q))
        values[0] = values[0] * (t0 * one + t1 * near + t2 * far)
        values[1] = values[1] * (t0 * two + t1 * one + t2 * near)
    rest = jnp.zeros((LANES - 2 * count, LANES), jnp.float32)
    return jnp.concatenate(values + [rest], axis=0).T


def conv_kernel(split, place_ref, both_ref, head_ref, back_ref, skip_ref, taps_ref, o_ref, *scratch):
    head_buf, back_buf, spec_ref, factor_ref, low_ref, x_buf, fix_ref, sems = scratch
    count, _, part, rows = o_ref.shape
    tiles = rows // LANES
    high = min(part, 16)
    group = 2
    low = part * (split or 0)
    copies = [
        pltpu.make_async_copy(
            head_ref.at[:, pl.ds(t * 2 * LANES, 2 * LANES)], head_buf.at[t], sems.at[t]
        )
        for t in range(tiles)
    ]
    copies.append(pltpu.make_async_copy(back_ref, back_buf, sems.at[tiles]))
    for copy in copies:
        copy.start()
    height = count * part

    def arrived(kind):
        if split is None:
            return both_ref[:, kind * part : (kind + 1) * part].reshape(height, rows)
        first = (2 * split + kind) * tiles
        places = [(first + c) * part // 8 for c in range(tiles)]
        pieces = [both_ref[:, a : a + part // 8].reshape(height, LANES) for a in places]
        return jnp.concatenate(pieces, axis=1)

    x_buf[...] = arrived(1).reshape(count, part, rows)
    if split is not None:
        ends = both_ref[:, both_ref.shape[1] - 1]
        fix_ref[...] = first_tokens(ends, taps_ref[...])
        first = split * (LANES // 2) + place_ref[0] * part
        mine = fix_ref[pl.ds(pl.multiple_of(first, part), part), :]
        lane = lax.broadcasted_iota(jnp.int32, (part, LANES), 1)
        for block in range(count):
            one = pltpu.roll(mine, (LANES - block) % LANES, 1)
            two = pltpu.roll(mine, (LANES - block - count + 1) % LANES, 1)
            value = x_buf[block, :, :LANES].astype(jnp.float32)
            value = jnp.where(lane == 0, one, jnp.where(lane == 1, two, value))
            x_buf[block, :, :LANES] = value.astype(x_buf.dtype)
    filters = arrived(0)
    odd = lax.broadcasted_iota(jnp.int32, (height, 2 * LANES), 1) % 2 == 1
    lane = lax.broadcasted_iota(jnp.int32, (high, LANES), 1)

    lane0 = lax.broadcasted_iota(jnp.int32, (height, LANES), 1) == 0

    def spectra(t):
        value = jnp.dot(filters, head_buf[t], preferred_element_type=jnp.float32)
        earlier = jnp.concatenate([jnp.zeros_like(value[:part]), value[:-part]], axis=0)
        window = earlier + jnp.where(odd, -value, value)
        real, imag = (window[:, :LANES], window[:, LANES:])
        factor_ref[t, :, :LANES] = real
        less, more = (imag - real, real + imag)
        if t == 0:
            less, more = (jnp.where(lane0, real, less), jnp.where(lane0, imag, more))
        factor_ref[t, :, LANES : 2 * LANES] = less
        factor_ref[t, :, 2 * LANES :] = more
        spec_ref[t] = jnp.dot(
            x_buf[...].reshape(height, rows), head_buf[t], preferred_element_type=jnp.float32
        )

    def products(t, slab):
        base = slab * high
        if not isinstance(base, int):
            base = pl.multiple_of(base, high)
        for start in range(0, count, group):
            sums = [[None] * 3 for _ in range(group)]
            factors = {}
            for source in range(start + group):
                place = pl.ds(base + source * part, high)
                real, imag = (spec_ref[t, place, :LANES], spec_ref[t, place, LANES:])
                both = real + imag
                for g in range(group):
                    lag = start + g - source
                    if lag < 0:
                        continue
                    if lag not in factors:
                        place = pl.ds(base + lag * part, high)
                        factors[lag] = [
                            factor_ref[t, place, c * LANES : (c + 1) * LANES] for c in range(3)
                        ]
                    a, b, c = factors[lag]
                    terms = (both * a, real * b, imag * c)
                    before = sums[g]
                    sums[g] = [u if p is None else p + u for p, u in zip(before, terms)]
            for g in range(group):
                a, b, c = sums[g]
                place = pl.ds(base + (start + g) * part, high)
                re, im = (a - c, a + b)
                if t == 0:
                    re, im = (jnp.where(lane == 0, b, re), jnp.where(lane == 0, c, im))
                low_ref[place, t * 2 * LANES : t * 2 * LANES + LANES] = re.astype(low_ref.dtype)
                low_ref[place, t * 2 * LANES + LANES : (t + 1) * 2 * LANES] = im.astype(low_ref.dtype)

    for copy in copies:
        copy.wait()
    for t in range(tiles):
        spectra(t)
        if split is not None:
            for slab in range(part // high):
                products(t, slab)
        else:

            def one_slab(slab, carry, t=t):
                products(t, slab)
                return carry

            lax.fori_loop(0, part // high, one_slab, 0)
    back = jnp.dot(
        low_ref[...].astype(jnp.bfloat16), back_buf[...], preferred_element_type=jnp.float32
    )
    value = back.reshape(count, part, rows)
    skip = skip_ref[low : low + part, :1][None]
    value = value + skip * x_buf[...].astype(jnp.float32)
    for copy in range(o_ref.shape[1]):
        o_ref[:, copy] = value.astype(o_ref.dtype)


def long_conv(both, head, back, skip, taps, place, split, copies=1):
    count, rows = (both.shape[0], head.shape[0])
    own = skip.shape[0]
    part = own if split is None else own // 2
    height = count * part
    vmem, anywhere = (pl.BlockSpec(memory_space=pltpu.VMEM), pl.BlockSpec(memory_space=pl.ANY))
    return call(
        functools.partial(conv_kernel, split),
        [pl.BlockSpec(memory_space=pltpu.SMEM), vmem, anywhere, anywhere, vmem, vmem],
        [vmem],
        [((count, copies, part, rows), jnp.bfloat16)],
        scratch=[
            pltpu.VMEM((rows // LANES, rows, 2 * LANES), jnp.bfloat16),
            pltpu.VMEM(back.shape, jnp.bfloat16),
            pltpu.VMEM((rows // LANES, height, 2 * LANES), jnp.float32),
            pltpu.VMEM((rows // LANES, height, 3 * LANES), jnp.float32),
            pltpu.VMEM((height, 2 * rows), jnp.float32 if part % 16 else jnp.bfloat16),
            pltpu.VMEM((count, part, rows), jnp.bfloat16),
            pltpu.VMEM((LANES, LANES), jnp.float32),
            pltpu.SemaphoreType.DMA((rows // LANES + 1,)),
        ],
        megabytes=28,
        flops=12 * height * rows * rows,
        moved=height * rows * 8,
    )(place, both, head, back, skip, taps, free=(0, 1))[0]


def gated_part(long, outer, first):
    count, step, rows = long.shape
    value = long.reshape(count * step, rows).T.astype(jnp.float32)
    outer = outer.astype(jnp.float32)
    outer = jnp.concatenate([outer[:8] + first, outer[8:]], axis=0)
    return (outer * value).astype(jnp.bfloat16)


def gate_kernel(long_ref, outer_ref, first_ref, o_ref):
    o_ref[...] = gated_part(long_ref[...], outer_ref[...], first_ref[...])


def gate(long, outer, first):
    rows = outer.shape[0]
    width = long.shape[0] * long.shape[1]
    return call(
        gate_kernel,
        [
            pl.BlockSpec(long.shape, lambda n: (0, 0, 0)),
            pl.BlockSpec((rows, width), lambda n: (0, 0)),
            pl.BlockSpec((8, width), lambda n: (0, 0)),
        ],
        [pl.BlockSpec((rows, width), lambda n: (0, 0))],
        [((rows, width), jnp.bfloat16)],
        grid=(1,),
        moved=6 * rows * width,
    )(long, outer, first, free=(0,))[0]


def own_kernel(here_ref, gated_ref, weight_ref, o_ref):
    value = jnp.dot(gated_ref[...], weight_ref[...], preferred_element_type=jnp.float32)
    o_ref[...] = value.astype(o_ref.dtype)


def own_term(here, gated, out_weight, cols):
    rows, used = gated.shape
    wide = cols // 2
    return call(
        own_kernel,
        [
            pl.BlockSpec((rows, used), lambda n, h: (0, 0)),
            pl.BlockSpec((used, wide), lambda n, h: (0, h[0] * 2 + n)),
        ],
        [pl.BlockSpec((rows, wide), lambda n, h: (0, n))],
        [((rows, cols), jnp.bfloat16)],
        grid=(2,),
        flops=2 * rows * used * cols,
        moved=rows * cols * 2 + used * cols * 2,
        scalars=1,
    )(here, gated, out_weight)[0]


def last_kernel(
    place_ref, sent_ref, dealt_ref, first_ref, sum_ref, mine_ref, theirs_ref, *refs
):
    blocks, (weight_ref, o_ref, *scratch) = (refs[:4], refs[4:])
    outer_buf, weight_buf, block_buf, sum_buf, out_buf, gated_ref, sems = scratch
    here, quarter = (place_ref[0], place_ref[1])
    rows, used = outer_buf.shape[1:]
    wide = out_buf.shape[2]
    cols = 4 * wide
    pairs = [(mine_ref.at[:, pl.ds(used, used)], outer_buf.at[0]), (theirs_ref, outer_buf.at[1])]
    gates = [pltpu.make_async_copy(a, b, sems.at[g]) for g, (a, b) in enumerate(pairs)]
    for copy in gates:
        copy.start()
    places, inputs = ([], [])
    for k in range(4):
        column = pl.multiple_of((quarter ^ k) * wide, wide)
        places.append(pl.ds(column, wide))
        ours = pl.multiple_of(here * cols + column, wide)
        pairs = [
            (blocks[k], block_buf.at[k]),
            (weight_ref.at[pl.ds(used, used), pl.ds(ours, wide)], weight_buf.at[k]),
            (sum_ref.at[:, places[k]], sum_buf.at[k]),
        ]
        inputs.append(
            [pltpu.make_async_copy(a, b, sems.at[2 + 3 * k + i]) for i, (a, b) in enumerate(pairs)]
        )
        for copy in inputs[k]:
            copy.start()
    for g in range(2):
        gates[g].wait()
        long = dealt_ref[:, here if g == 0 else 1 - here]
        gated_ref[g] = gated_part(long, outer_buf[g], first_ref[g])
    outputs = []
    for k in range(4):
        for copy in inputs[k]:
            copy.wait()
        value = sum_buf[k].astype(jnp.float32)
        for left, right in (
            (sent_ref[...], block_buf[k, :used]),
            (gated_ref[1], block_buf[k, used:]),
            (gated_ref[0], weight_buf[k]),
        ):
            value = value + jnp.dot(left, right, preferred_element_type=jnp.float32)
        out_buf[k] = value.astype(out_buf.dtype)
        outputs.append(pltpu.make_async_copy(out_buf.at[k], o_ref.at[:, places[k]], sems.at[14 + k]))
        outputs[k].start()
    for copy in outputs:
        copy.wait()


def last_term(place, sent, dealt, first, total, mine, theirs, blocks, out_weight):
    rows, cols = total.shape
    chan = mine.shape[1]
    wide = cols // 4
    used = chan // 2
    vmem, anywhere = (pl.BlockSpec(memory_space=pltpu.VMEM), pl.BlockSpec(memory_space=pl.ANY))
    bf16 = jnp.bfloat16
    return call(
        last_kernel,
        [pl.BlockSpec(memory_space=pltpu.SMEM), vmem, vmem, vmem] + [anywhere] * 8,
        [anywhere],
        [((rows, cols), bf16)],
        scratch=[
            pltpu.VMEM((2, rows, used), bf16),
            pltpu.VMEM((4, used, wide), bf16),
            pltpu.VMEM((4, chan, wide), bf16),
            pltpu.VMEM((4, rows, wide), bf16),
            pltpu.VMEM((4, rows, wide), bf16),
            pltpu.VMEM((2, rows, used), bf16),
            pltpu.SemaphoreType.DMA((18,)),
        ],
        megabytes=32,
        flops=24 * rows * used * wide,
        moved=rows * wide * 16 + used * wide * 24,
    )(place, sent, dealt, first, total, mine, theirs, *blocks, out_weight, free=(0, 1, 2, 3))[0]


def exchanged(value):
    return lax.all_to_all(value, "ctx", 0, 0, tiled=True)


def to_groups(values):
    groups = lax.axis_size("ch")
    return [
        lax.ppermute(value, "ch", [(g, (g + s) % groups) for g in range(groups)])
        for s, value in enumerate(values, 1)
    ]


def any_groups(long, outer, out_weight):
    rows, chan = outer.shape
    groups = lax.axis_size("ch")
    here = lax.axis_index("ch")
    cols = out_weight.shape[1] // groups
    gated = gated_part(long, outer, jnp.zeros((8, chan), jnp.float32))
    total = jnp.zeros((rows, cols), jnp.float32)
    weights = [
        lax.dynamic_slice(out_weight, (0, (here + s) % groups * cols), (chan, cols))
        for s in range(groups)
    ]
    values = [gated] + to_groups([gated] * (groups - 1))
    for value, weight in zip(values, weights[:1] + to_groups(weights[1:])):
        total = total + jnp.dot(value, weight, preferred_element_type=jnp.float32)
    return total.astype(jnp.bfloat16)


def local(streams, short_taps, filters, skip_gain, out_weight):
    rows, _, chan = streams.shape
    count = lax.axis_size("ctx")
    groups = lax.axis_size("ch")
    own = chan // count
    step = own // 2
    fast = groups == 2 and count % 4 == 0 and own % 32 == 0 and count % 2 == 0 and LANES % (2 * step) == 0
    fast = fast and rows % LANES == 0 and 2 * count <= LANES and chan % (4 * LANES) == 0
    after = lax.optimization_barrier
    position, here = (lax.axis_index("ctx"), lax.axis_index("ch"))
    head = jnp.asarray(head_table(2 * rows))
    back = jnp.asarray(inverse_table(2 * rows))
    streams = streams.transpose(1, 0, 2)
    parts = 2 if fast else 1
    skip = skip_gain.reshape(parts, count, own // parts)
    skip = lax.dynamic_index_in_dim(skip, position, 1, False)
    skip = jnp.broadcast_to(skip.reshape(own, 1), (own, LANES))
    if not fast:
        both, tail = turned(filters, streams, count, parts)
        edges = passed_along(tail, "ctx", 1)
        both = exchanged(with_inner(both, streams, edges, short_taps, parts))
        both = both.reshape(count, 2 * own, rows)
        outer = outer_gate(streams, 2, edges[2:], short_taps[:, 2:], parts)
        none = jnp.zeros((8, LANES), jnp.float32)
        long = long_conv(both, head, back, skip, none, jnp.zeros((1,), jnp.int32), None)
        return any_groups(exchanged(long[:, 0]), outer, out_weight)
    per = LANES // step // 2
    place = (position % per)[None]
    taps = short_taps[:, :2].reshape(6, 2, chan // 2)
    taps = lax.dynamic_slice(taps, (0, 0, position // per * (LANES // 2)), (6, 2, LANES // 2))
    taps = jnp.pad(taps.reshape(6, LANES), ((0, 2), (0, 0)))
    both = exchanged(deal(filters, streams, short_taps, count))
    cols = out_weight.shape[1] // groups
    wide = cols // 4
    columns = (1 - here) * cols + position % 4 * wide
    near = lax.dynamic_slice(out_weight, (0, columns), (chan, wide))
    near, skip, taps = after((near, skip, taps))
    near = to_groups([near])[0]
    none = jnp.zeros((1, 2, chan), jnp.float32)
    none, near = after((none, near))
    outer = outer_gate(streams, 2, none, short_taps[:, 2:], 2)
    theirs = to_groups([outer[:, chan // 2 :]])[0]

    def swapped(value, bit):
        return lax.ppermute(value, "ctx", [(i, i ^ bit) for i in range(count)])

    across = swapped(near, 2)
    edges = passed_along(streams[2, rows - 2 :], "ctx", 1).astype(jnp.float32)
    both, outer, theirs, edges = after((both, outer, theirs, edges))
    early = long_conv(both, head, back, skip, taps, place, 0)[:, 0]
    first = jnp.stack(
        [short_taps[1, 2] * edges[1] + short_taps[2, 2] * edges[0], short_taps[2, 2] * edges[1]]
    )
    first = jnp.pad(first, ((0, 6), (0, 0)))
    other = to_groups([first[:, chan // 2 :]])[0]
    both, _ = after((both, early))
    late = long_conv(both, head, back, skip, taps, place, 1, copies=groups)
    late, across = after((late, across))
    blocks = [near, swapped(near, 1), across, swapped(across, 1)]
    early, late, other, first = after((exchanged(early), late, other, first))
    gated = gate(early, outer, first)
    sent = to_groups([gated])[0]
    dealt = lax.all_to_all(
        late.reshape(count * groups, step, rows), ("ctx", "ch"), 0, 0, tiled=True
    )
    dealt = dealt.reshape(count, groups, step, rows)
    total = own_term(here[None], gated, out_weight, cols)
    place = jnp.stack([here, position % 4])
    first = jnp.stack([first[:, chan // 2 :], other])
    return last_term(place, sent, dealt, first, total, outer, theirs, blocks, out_weight)


def solution(mesh):
    return jax.shard_map(
        local,
        mesh=mesh,
        in_specs=(
            P("ctx", None, "ch"),
            P(None, None, "ch"),
            P("ctx", "ch"),
            P("ch"),
            P("ch", None),
        ),
        out_specs=P("ctx", "ch"),
        check_vma=False,
    )
```

```python
import functools

import jax
import jax.numpy as jnp
import ml_dtypes
import numpy as np
from jax import lax
from jax.experimental import pallas as pl
from jax.experimental.pallas import tpu as pltpu
from jax.sharding import PartitionSpec as P

LANES = 128


def passed_along(value, axis, steps):
    count = lax.axis_size(axis)
    initial, last = (max(0, -steps), min(count, count - steps))
    return lax.ppermute(value, axis, [(source, source + steps) for source in range(initial, last)])


def paired_columns(half):
    order = np.arange(2 * half).reshape(2, half // LANES, LANES)
    return order.transpose(1, 0, 2).reshape(-1)


def head_table(size):
    half = size // 2
    rows = np.arange(half)[:, None]
    cols = np.arange(size)[None, :]
    freq = np.where(cols < half, cols, cols - half)
    angle = (rows * freq % size) * (2.0 * np.pi / size)
    nyquist = np.where(rows % 2 == 0, 1.0, -1.0)
    table = np.where(cols < half, np.cos(angle), np.where(cols == half, nyquist, -np.sin(angle)))
    return table[:, paired_columns(half)].astype(ml_dtypes.bfloat16)


def inverse_table(size):
    half = size // 2
    rows = np.arange(size)[:, None]
    places = half + np.arange(half)[None, :]
    freq = np.where(rows < half, rows, rows - half)
    angle = (places * freq % size) * (2.0 * np.pi / size)
    weight = np.where(freq == 0, 1.0, 2.0) / size
    nyquist = np.where(places % 2 == 0, 1.0, -1.0) / size
    table = np.where(
        rows < half, weight * np.cos(angle), np.where(rows == half, nyquist, -weight * np.sin(angle))
    )
    return table[paired_columns(half)].astype(ml_dtypes.bfloat16)


def call(kernel, in_specs, out_specs, outs, grid=(), scratch=(), megabytes=16, flops=0, moved=0, scalars=0, aliases=None):
    inner = pl.pallas_call(
        kernel,
        grid_spec=pltpu.PrefetchScalarGridSpec(
            num_scalar_prefetch=scalars,
            grid=grid,
            in_specs=in_specs,
            out_specs=out_specs,
            scratch_shapes=list(scratch),
        ),
        out_shape=[pltpu.HBM(shape, dtype) for shape, dtype in outs],
        input_output_aliases=aliases or {},
        compiler_params=pltpu.CompilerParams(vmem_limit_bytes=megabytes * 1024 * 1024),
        cost_estimate=pl.CostEstimate(flops=flops, bytes_accessed=moved, transcendentals=0),
    )

    def run(*args, free=()):
        pinned = [
            a if k < scalars or k in free else pltpu.with_memory_space_constraint(a, pltpu.HBM)
            for k, a in enumerate(args)
        ]
        return inner(*pinned)

    return run


def store_turned(value, o_ref):
    o_ref[...] = value.T.reshape(o_ref.shape).astype(o_ref.dtype)


def turn_kernel(x_ref, s_ref, o_ref, tail_ref):
    tail_ref[...] = s_ref[:, s_ref.shape[1] - 2 :]
    store_turned(x_ref[...].astype(jnp.float32), o_ref)


def turned(x, streams, count, parts):
    rows, chan = x.shape
    own = chan // count
    last = min(rows, 16)
    tile = chan // parts
    return call(
        turn_kernel,
        [
            pl.BlockSpec((rows, tile), lambda p: (0, p)),
            pl.BlockSpec((3, last, tile), lambda p: (0, rows // last - 1, p)),
        ],
        [
            pl.BlockSpec((count, 1, own // parts, rows), lambda p: (0, 0, p, 0)),
            pl.BlockSpec((3, 2, tile), lambda p: (0, 0, p)),
        ],
        [((count, 2, own, rows), x.dtype), ((3, 2, chan), streams.dtype)],
        grid=(parts,),
        moved=4 * rows * chan,
    )(x, streams)


def mixed(s_ref, e_ref, t_ref, q):
    rows, width = s_ref.shape[1:]
    place = lax.broadcasted_iota(jnp.int32, (8, width), 0)
    now = s_ref[q].astype(jnp.float32)
    edge = e_ref[q].astype(jnp.float32)
    one, two = (pltpu.roll(now, 1, 0), pltpu.roll(now, 2, 0))
    one_top = jnp.where(place == 0, edge[1:2], one[:8])
    two_top = jnp.where(place == 0, edge[0:1], jnp.where(place == 1, edge[1:2], two[:8]))
    one = jnp.concatenate([one_top, one[8:]], axis=0)
    two = jnp.concatenate([two_top, two[8:]], axis=0)
    return t_ref[0, q : q + 1] * now + t_ref[1, q : q + 1] * one + t_ref[2, q : q + 1] * two


def inner_kernel(s_ref, e_ref, t_ref, _, o_ref):
    store_turned(mixed(s_ref, e_ref, t_ref, 0) * mixed(s_ref, e_ref, t_ref, 1), o_ref)


def with_inner(both, streams, edges, taps, parts):
    count, _, own, rows = both.shape
    chan = count * own
    tile = chan // parts
    return call(
        inner_kernel,
        [
            pl.BlockSpec((2, rows, tile), lambda p: (0, 0, p)),
            pl.BlockSpec((3, 2, tile), lambda p: (0, 0, p)),
            pl.BlockSpec((3, 3, tile), lambda p: (0, 0, p)),
            pl.BlockSpec(memory_space=pl.ANY),
        ],
        [pl.BlockSpec((count, 1, own // parts, rows), lambda p: (0, 1, p, 0))],
        [(both.shape, both.dtype)],
        grid=(parts,),
        megabytes=32,
        moved=6 * rows * chan,
        aliases={3: 0},
    )(streams, edges, taps, both)[0]


def outer_kernel(s_ref, e_ref, t_ref, o_ref):
    o_ref[...] = mixed(s_ref, e_ref, t_ref, 0).astype(o_ref.dtype)


def outer_gate(streams, which, edges, taps, parts):
    _, rows, chan = streams.shape
    tile = chan // parts
    return call(
        outer_kernel,
        [
            pl.BlockSpec((1, rows, tile), lambda p: (which, 0, p)),
            pl.BlockSpec((1, 2, tile), lambda p: (0, 0, p)),
            pl.BlockSpec((3, 1, tile), lambda p: (0, 0, p)),
        ],
        [pl.BlockSpec((rows, tile), lambda p: (0, p))],
        [((rows, chan), jnp.bfloat16)],
        grid=(parts,),
        megabytes=32,
        moved=4 * rows * chan,
    )(streams, edges, taps)[0]


def deal_kernel(f_ref, s_ref, t_ref, o_ref, f_buf, s_buf, out_buf, sems):
    count, height, _, _ = out_buf.shape
    rows, chan = f_ref.shape
    step = chan // count // 2
    tile = chan // 4
    few = count // 2
    per = LANES // step // 2
    ins = []
    for q in range(4):
        lanes = pl.ds(q * tile, tile)
        ins.append(pltpu.make_async_copy(f_ref.at[:, lanes], f_buf.at[q], sems.at[2 * q]))
        ins.append(
            pltpu.make_async_copy(s_ref.at[pl.ds(0, 2), :, lanes], s_buf.at[q], sems.at[2 * q + 1])
        )
    for copy in ins:
        copy.start()
    outs, edges = ([], [])
    for q in range(4):
        p, owner = (q // 2, q % 2 * few)
        lanes = slice(q * tile, (q + 1) * tile)
        ins[2 * q].wait()
        values = [f_buf[q].astype(jnp.float32)]
        ins[2 * q + 1].wait()
        both = []
        for stream in range(2):
            now = s_buf[q, stream].astype(jnp.float32)
            value = t_ref[0, stream : stream + 1, lanes] * now
            value = value + t_ref[1, stream : stream + 1, lanes] * pltpu.roll(now, 1, 0)
            both.append(value + t_ref[2, stream : stream + 1, lanes] * pltpu.roll(now, 2, 0))
        values.append(both[0] * both[1])
        for k in range(2):
            value = values[k].astype(o_ref.dtype).T
            for c in range(rows // LANES):
                place = ((2 * p + k) * rows // LANES + c) * step // 8
                out_buf[owner : owner + few, place : place + step // 8] = value[
                    :, c * LANES : (c + 1) * LANES
                ].reshape(few, step // 8, 8, LANES)
        ends = [s_buf[q, k, a : a + 2].astype(jnp.float32) for a in (0, rows - 2) for k in range(2)]
        ends = jnp.concatenate(ends, axis=0)
        edges.append(ends)
        if p == 1:
            for g in range(few // per):
                lanes = slice(g * LANES // 2, (g + 1) * LANES // 2)
                value = jnp.concatenate([edges[q - 2][:, lanes], edges[q][:, lanes]], axis=1)
                first = owner + g * per
                out_buf[first : first + per, height - 1] = jnp.broadcast_to(
                    value[None].astype(o_ref.dtype), (per, 8, LANES)
                )
        some = (pl.ds(owner, few), pl.ds(p * (height // 2), height // 2))
        outs.append(pltpu.make_async_copy(out_buf.at[some], o_ref.at[some], sems.at[8 + q]))
        outs[q].start()
    some = pl.ds(height - 1, 1)
    outs.append(pltpu.make_async_copy(out_buf.at[:, some], o_ref.at[:, some], sems.at[12]))
    outs[4].start()
    for copy in outs:
        copy.wait()


def deal(filters, streams, taps, count):
    rows, chan = filters.shape
    shape = (count, chan // count * rows // LANES // 4 + 1, 8, LANES)
    anywhere, vmem = (pl.BlockSpec(memory_space=pl.ANY), pl.BlockSpec(memory_space=pltpu.VMEM))
    bf16 = jnp.bfloat16
    return call(
        deal_kernel,
        [anywhere, anywhere, vmem],
        [anywhere],
        [(shape, bf16)],
        scratch=[
            pltpu.VMEM((4, rows, chan // 4), bf16),
            pltpu.VMEM((4, 2, rows, chan // 4), bf16),
            pltpu.VMEM(shape, bf16),
            pltpu.SemaphoreType.DMA((13,)),
        ],
        megabytes=32,
        moved=10 * rows * chan,
    )(filters, streams, taps)[0]


def first_tokens(ends, taps):
    count = ends.shape[0]

    def at(row):
        return ends[:, row].astype(jnp.float32)

    block = lax.broadcasted_iota(jnp.int32, (count, LANES), 0)

    def before(row):
        return jnp.where(block == 0, 0.0, pltpu.roll(at(row), 1, 0))

    values = [1.0, 1.0]
    for q in range(2):
        t0, t1, t2 = (taps[2 * m + q : 2 * m + q + 1] for m in range(3))
        one, two = (at(2 * q), at(2 * q + 1))
        far, near = (before(4 + 2 * q), before(5 + 2 * q))
        values[0] = values[0] * (t0 * one + t1 * near + t2 * far)
        values[1] = values[1] * (t0 * two + t1 * one + t2 * near)
    rest = jnp.zeros((LANES - 2 * count, LANES), jnp.float32)
    return jnp.concatenate(values + [rest], axis=0).T


def conv_kernel(split, place_ref, both_ref, head_ref, back_ref, skip_ref, taps_ref, o_ref, *scratch):
    head_buf, back_buf, spec_ref, factor_ref, low_ref, x_buf, fix_ref, sems = scratch
    count, _, part, rows = o_ref.shape
    tiles = rows // LANES
    high = min(part, 16)
    group = 2
    low = part * (split or 0)
    copies = [
        pltpu.make_async_copy(
            head_ref.at[:, pl.ds(t * 2 * LANES, 2 * LANES)], head_buf.at[t], sems.at[t]
        )
        for t in range(tiles)
    ]
    copies.append(pltpu.make_async_copy(back_ref, back_buf, sems.at[tiles]))
    for copy in copies:
        copy.start()
    height = count * part

    def arrived(kind):
        if split is None:
            return both_ref[:, kind * part : (kind + 1) * part].reshape(height, rows)
        first = (2 * split + kind) * tiles
        places = [(first + c) * part // 8 for c in range(tiles)]
        pieces = [both_ref[:, a : a + part // 8].reshape(height, LANES) for a in places]
        return jnp.concatenate(pieces, axis=1)

    x_buf[...] = arrived(1).reshape(count, part, rows)
    if split is not None:
        ends = both_ref[:, both_ref.shape[1] - 1]
        fix_ref[...] = first_tokens(ends, taps_ref[...])
        first = split * (LANES // 2) + place_ref[0] * part
        mine = fix_ref[pl.ds(pl.multiple_of(first, part), part), :]
        lane = lax.broadcasted_iota(jnp.int32, (part, LANES), 1)
        for block in range(count):
            one = pltpu.roll(mine, (LANES - block) % LANES, 1)
            two = pltpu.roll(mine, (LANES - block - count + 1) % LANES, 1)
            value = x_buf[block, :, :LANES].astype(jnp.float32)
            value = jnp.where(lane == 0, one, jnp.where(lane == 1, two, value))
            x_buf[block, :, :LANES] = value.astype(x_buf.dtype)
    filters = arrived(0)
    odd = lax.broadcasted_iota(jnp.int32, (height, 2 * LANES), 1) % 2 == 1
    lane = lax.broadcasted_iota(jnp.int32, (high, LANES), 1)

    lane0 = lax.broadcasted_iota(jnp.int32, (height, LANES), 1) == 0

    def spectra(t):
        value = jnp.dot(filters, head_buf[t], preferred_element_type=jnp.float32)
        earlier = jnp.concatenate([jnp.zeros_like(value[:part]), value[:-part]], axis=0)
        window = earlier + jnp.where(odd, -value, value)
        real, imag = (window[:, :LANES], window[:, LANES:])
        factor_ref[t, :, :LANES] = real
        less, more = (imag - real, real + imag)
        if t == 0:
            less, more = (jnp.where(lane0, real, less), jnp.where(lane0, imag, more))
        factor_ref[t, :, LANES : 2 * LANES] = less
        factor_ref[t, :, 2 * LANES :] = more
        spec_ref[t] = jnp.dot(
            x_buf[...].reshape(height, rows), head_buf[t], preferred_element_type=jnp.float32
        )

    def products(t, slab):
        base = slab * high
        if not isinstance(base, int):
            base = pl.multiple_of(base, high)
        for start in range(0, count, group):
            sums = [[None] * 3 for _ in range(group)]
            factors = {}
            for source in range(start + group):
                place = pl.ds(base + source * part, high)
                real, imag = (spec_ref[t, place, :LANES], spec_ref[t, place, LANES:])
                both = real + imag
                for g in range(group):
                    lag = start + g - source
                    if lag < 0:
                        continue
                    if lag not in factors:
                        place = pl.ds(base + lag * part, high)
                        factors[lag] = [
                            factor_ref[t, place, c * LANES : (c + 1) * LANES] for c in range(3)
                        ]
                    a, b, c = factors[lag]
                    terms = (both * a, real * b, imag * c)
                    before = sums[g]
                    sums[g] = [u if p is None else p + u for p, u in zip(before, terms)]
            for g in range(group):
                a, b, c = sums[g]
                place = pl.ds(base + (start + g) * part, high)
                re, im = (a - c, a + b)
                if t == 0:
                    re, im = (jnp.where(lane == 0, b, re), jnp.where(lane == 0, c, im))
                low_ref[place, t * 2 * LANES : t * 2 * LANES + LANES] = re.astype(low_ref.dtype)
                low_ref[place, t * 2 * LANES + LANES : (t + 1) * 2 * LANES] = im.astype(low_ref.dtype)

    for copy in copies:
        copy.wait()
    for t in range(tiles):
        spectra(t)
        if split is not None:
            for slab in range(part // high):
                products(t, slab)
        else:

            def one_slab(slab, carry, t=t):
                products(t, slab)
                return carry

            lax.fori_loop(0, part // high, one_slab, 0)
    back = jnp.dot(
        low_ref[...].astype(jnp.bfloat16), back_buf[...], preferred_element_type=jnp.float32
    )
    value = back.reshape(count, part, rows)
    skip = skip_ref[low : low + part, :1][None]
    value = value + skip * x_buf[...].astype(jnp.float32)
    for copy in range(o_ref.shape[1]):
        o_ref[:, copy] = value.astype(o_ref.dtype)


def long_conv(both, head, back, skip, taps, place, split, copies=1):
    count, rows = (both.shape[0], head.shape[0])
    own = skip.shape[0]
    part = own if split is None else own // 2
    height = count * part
    vmem, anywhere = (pl.BlockSpec(memory_space=pltpu.VMEM), pl.BlockSpec(memory_space=pl.ANY))
    return call(
        functools.partial(conv_kernel, split),
        [pl.BlockSpec(memory_space=pltpu.SMEM), vmem, anywhere, anywhere, vmem, vmem],
        [vmem],
        [((count, copies, part, rows), jnp.bfloat16)],
        scratch=[
            pltpu.VMEM((rows // LANES, rows, 2 * LANES), jnp.bfloat16),
            pltpu.VMEM(back.shape, jnp.bfloat16),
            pltpu.VMEM((rows // LANES, height, 2 * LANES), jnp.float32),
            pltpu.VMEM((rows // LANES, height, 3 * LANES), jnp.float32),
            pltpu.VMEM((height, 2 * rows), jnp.float32 if part % 16 else jnp.bfloat16),
            pltpu.VMEM((count, part, rows), jnp.bfloat16),
            pltpu.VMEM((LANES, LANES), jnp.float32),
            pltpu.SemaphoreType.DMA((rows // LANES + 1,)),
        ],
        megabytes=28,
        flops=12 * height * rows * rows,
        moved=height * rows * 8,
    )(place, both, head, back, skip, taps, free=(0, 1))[0]


def gated_part(long, outer, first):
    count, step, rows = long.shape
    value = long.reshape(count * step, rows).T.astype(jnp.float32)
    outer = outer.astype(jnp.float32)
    outer = jnp.concatenate([outer[:8] + first, outer[8:]], axis=0)
    return (outer * value).astype(jnp.bfloat16)


def gate_kernel(long_ref, outer_ref, first_ref, o_ref):
    o_ref[...] = gated_part(long_ref[...], outer_ref[...], first_ref[...])


def gate(long, outer, first):
    rows = outer.shape[0]
    width = long.shape[0] * long.shape[1]
    return call(
        gate_kernel,
        [
            pl.BlockSpec(long.shape, lambda n: (0, 0, 0)),
            pl.BlockSpec((rows, width), lambda n: (0, 0)),
            pl.BlockSpec((8, width), lambda n: (0, 0)),
        ],
        [pl.BlockSpec((rows, width), lambda n: (0, 0))],
        [((rows, width), jnp.bfloat16)],
        grid=(1,),
        moved=6 * rows * width,
    )(long, outer, first, free=(0,))[0]


def own_kernel(here_ref, gated_ref, weight_ref, o_ref):
    value = jnp.dot(gated_ref[...], weight_ref[...], preferred_element_type=jnp.float32)
    o_ref[...] = value.astype(o_ref.dtype)


def own_term(here, gated, out_weight, cols):
    rows, used = gated.shape
    wide = cols // 2
    return call(
        own_kernel,
        [
            pl.BlockSpec((rows, used), lambda n, h: (0, 0)),
            pl.BlockSpec((used, wide), lambda n, h: (0, h[0] * 2 + n)),
        ],
        [pl.BlockSpec((rows, wide), lambda n, h: (0, n))],
        [((rows, cols), jnp.bfloat16)],
        grid=(2,),
        flops=2 * rows * used * cols,
        moved=rows * cols * 2 + used * cols * 2,
        scalars=1,
    )(here, gated, out_weight)[0]


def last_kernel(
    place_ref, sent_ref, dealt_ref, first_ref, sum_ref, mine_ref, theirs_ref, *refs
):
    blocks, (weight_ref, o_ref, *scratch) = (refs[:4], refs[4:])
    outer_buf, weight_buf, block_buf, sum_buf, out_buf, gated_ref, sems = scratch
    here, core = (place_ref[0], place_ref[1])
    rows, used = outer_buf.shape[1:]
    wide = out_buf.shape[2]
    cols = 4 * wide
    pairs = [(mine_ref.at[:, pl.ds(used, used)], outer_buf.at[0]), (theirs_ref, outer_buf.at[1])]
    gates = [pltpu.make_async_copy(a, b, sems.at[g]) for g, (a, b) in enumerate(pairs)]
    for copy in gates:
        copy.start()
    places, inputs = ([], [])
    for k in range(4):
        column = pl.multiple_of((2 * (core ^ k // 2) + k % 2) * wide, wide)
        places.append(pl.ds(column, wide))
        ours = pl.multiple_of(here * cols + column, wide)
        pairs = [
            (blocks[k], block_buf.at[k]),
            (weight_ref.at[pl.ds(used, used), pl.ds(ours, wide)], weight_buf.at[k]),
            (sum_ref.at[:, places[k]], sum_buf.at[k]),
        ]
        inputs.append(
            [pltpu.make_async_copy(a, b, sems.at[2 + 3 * k + i]) for i, (a, b) in enumerate(pairs)]
        )
        for copy in inputs[k]:
            copy.start()
    for g in range(2):
        gates[g].wait()
        long = dealt_ref[:, here if g == 0 else 1 - here]
        gated_ref[g] = gated_part(long, outer_buf[g], first_ref[g])
    outputs = []
    for k in range(4):
        for copy in inputs[k]:
            copy.wait()
        value = sum_buf[k].astype(jnp.float32)
        for left, right in (
            (sent_ref[...], block_buf[k, :used]),
            (gated_ref[1], block_buf[k, used:]),
            (gated_ref[0], weight_buf[k]),
        ):
            value = value + jnp.dot(left, right, preferred_element_type=jnp.float32)
        out_buf[k] = value.astype(out_buf.dtype)
        outputs.append(pltpu.make_async_copy(out_buf.at[k], o_ref.at[:, places[k]], sems.at[14 + k]))
        outputs[k].start()
    for copy in outputs:
        copy.wait()


def last_term(place, sent, dealt, first, total, mine, theirs, blocks, out_weight):
    rows, cols = total.shape
    chan = mine.shape[1]
    wide = cols // 4
    used = chan // 2
    vmem, anywhere = (pl.BlockSpec(memory_space=pltpu.VMEM), pl.BlockSpec(memory_space=pl.ANY))
    bf16 = jnp.bfloat16
    return call(
        last_kernel,
        [pl.BlockSpec(memory_space=pltpu.SMEM), vmem, vmem, vmem] + [anywhere] * 8,
        [anywhere],
        [((rows, cols), bf16)],
        scratch=[
            pltpu.VMEM((2, rows, used), bf16),
            pltpu.VMEM((4, used, wide), bf16),
            pltpu.VMEM((4, chan, wide), bf16),
            pltpu.VMEM((4, rows, wide), bf16),
            pltpu.VMEM((4, rows, wide), bf16),
            pltpu.VMEM((2, rows, used), bf16),
            pltpu.SemaphoreType.DMA((18,)),
        ],
        megabytes=32,
        flops=24 * rows * used * wide,
        moved=rows * wide * 16 + used * wide * 24,
    )(place, sent, dealt, first, total, mine, theirs, *blocks, out_weight, free=(0, 1, 2, 3))[0]


def exchanged(value):
    return lax.all_to_all(value, "ctx", 0, 0, tiled=True)


def to_groups(values):
    groups = lax.axis_size("ch")
    return [
        lax.ppermute(value, "ch", [(g, (g + s) % groups) for g in range(groups)])
        for s, value in enumerate(values, 1)
    ]


def any_groups(long, outer, out_weight):
    rows, chan = outer.shape
    groups = lax.axis_size("ch")
    here = lax.axis_index("ch")
    cols = out_weight.shape[1] // groups
    gated = gated_part(long, outer, jnp.zeros((8, chan), jnp.float32))
    total = jnp.zeros((rows, cols), jnp.float32)
    weights = [
        lax.dynamic_slice(out_weight, (0, (here + s) % groups * cols), (chan, cols))
        for s in range(groups)
    ]
    values = [gated] + to_groups([gated] * (groups - 1))
    for value, weight in zip(values, weights[:1] + to_groups(weights[1:])):
        total = total + jnp.dot(value, weight, preferred_element_type=jnp.float32)
    return total.astype(jnp.bfloat16)


def local(streams, short_taps, filters, skip_gain, out_weight):
    rows, _, chan = streams.shape
    count = lax.axis_size("ctx")
    groups = lax.axis_size("ch")
    own = chan // count
    step = own // 2
    fast = groups == 2 and count % 4 == 0 and own % 32 == 0 and count % 2 == 0 and LANES % (2 * step) == 0
    fast = fast and rows % LANES == 0 and 2 * count <= LANES and chan % (4 * LANES) == 0
    after = lax.optimization_barrier
    position, here = (lax.axis_index("ctx"), lax.axis_index("ch"))
    head = jnp.asarray(head_table(2 * rows))
    back = jnp.asarray(inverse_table(2 * rows))
    streams = streams.transpose(1, 0, 2)
    parts = 2 if fast else 1
    skip = skip_gain.reshape(parts, count, own // parts)
    skip = lax.dynamic_index_in_dim(skip, position, 1, False)
    skip = jnp.broadcast_to(skip.reshape(own, 1), (own, LANES))
    if not fast:
        both, tail = turned(filters, streams, count, parts)
        edges = passed_along(tail, "ctx", 1)
        both = exchanged(with_inner(both, streams, edges, short_taps, parts))
        both = both.reshape(count, 2 * own, rows)
        outer = outer_gate(streams, 2, edges[2:], short_taps[:, 2:], parts)
        none = jnp.zeros((8, LANES), jnp.float32)
        long = long_conv(both, head, back, skip, none, jnp.zeros((1,), jnp.int32), None)
        return any_groups(exchanged(long[:, 0]), outer, out_weight)
    per = LANES // step // 2
    place = (position % per)[None]
    taps = short_taps[:, :2].reshape(6, 2, chan // 2)
    taps = lax.dynamic_slice(taps, (0, 0, position // per * (LANES // 2)), (6, 2, LANES // 2))
    taps = jnp.pad(taps.reshape(6, LANES), ((0, 2), (0, 0)))
    both = exchanged(deal(filters, streams, short_taps, count))
    cols = out_weight.shape[1] // groups
    none = jnp.zeros((1, 2, chan), jnp.float32)
    outer = outer_gate(streams, 2, none, short_taps[:, 2:], 2)
    theirs = to_groups([outer[:, chan // 2 :]])[0]
    theirs, skip, taps, out_weight = after((theirs, skip, taps, out_weight))
    wide = cols // 4
    columns = [(1 - here) * cols + (position % 2 * 2 + k) * wide for k in range(2)]
    near = [lax.dynamic_slice(out_weight, (0, c), (chan, wide)) for c in columns]
    near, tail = after((near, streams[2, rows - 2 :]))
    near = [to_groups([n])[0] for n in near]

    def swapped(value, bit):
        return lax.ppermute(value, "ctx", [(i, i ^ bit) for i in range(count)])

    both, outer, theirs = after((both, outer, theirs))
    early = long_conv(both, head, back, skip, taps, place, 0)[:, 0]
    edges, early = after((passed_along(tail, "ctx", 1), early))
    edges = edges.astype(jnp.float32)
    first = jnp.stack(
        [short_taps[1, 2] * edges[1] + short_taps[2, 2] * edges[0], short_taps[2, 2] * edges[1]]
    )
    first = jnp.pad(first, ((0, 6), (0, 0)))
    other = to_groups([first[:, chan // 2 :]])[0]
    both, _ = after((both, early))
    late = long_conv(both, head, back, skip, taps, place, 1, copies=groups)
    late, near = after((late, near))
    blocks = near + [swapped(n, 1) for n in near]
    early, late, other, first = after((exchanged(early), late, other, first))
    gated = gate(early, outer, first)
    sent = to_groups([gated])[0]
    dealt = lax.all_to_all(
        late.reshape(count * groups, step, rows), ("ctx", "ch"), 0, 0, tiled=True
    )
    dealt = dealt.reshape(count, groups, step, rows)
    total = own_term(here[None], gated, out_weight, cols)
    place = jnp.stack([here, position % 2])
    first = jnp.stack([first[:, chan // 2 :], other])
    return last_term(place, sent, dealt, first, total, outer, theirs, blocks, out_weight)


def solution(mesh):
    return jax.shard_map(
        local,
        mesh=mesh,
        in_specs=(
            P("ctx", None, "ch"),
            P(None, None, "ch"),
            P("ctx", "ch"),
            P("ch"),
            P("ch", None),
        ),
        out_specs=P("ctx", "ch"),
        check_vma=False,
    )
```

```python
import functools

import jax
import jax.numpy as jnp
import ml_dtypes
import numpy as np
from jax import lax
from jax.experimental import pallas as pl
from jax.experimental.pallas import tpu as pltpu
from jax.sharding import PartitionSpec as P

LANES = 128


def passed_along(value, axis, steps):
    count = lax.axis_size(axis)
    initial, last = (max(0, -steps), min(count, count - steps))
    return lax.ppermute(value, axis, [(source, source + steps) for source in range(initial, last)])


def paired_columns(half):
    order = np.arange(2 * half).reshape(2, half // LANES, LANES)
    return order.transpose(1, 0, 2).reshape(-1)


def head_table(size):
    half = size // 2
    rows = np.arange(half)[:, None]
    cols = np.arange(size)[None, :]
    freq = np.where(cols < half, cols, cols - half)
    angle = (rows * freq % size) * (2.0 * np.pi / size)
    nyquist = np.where(rows % 2 == 0, 1.0, -1.0)
    table = np.where(cols < half, np.cos(angle), np.where(cols == half, nyquist, -np.sin(angle)))
    return table[:, paired_columns(half)].astype(ml_dtypes.bfloat16)


def inverse_table(size):
    half = size // 2
    rows = np.arange(size)[:, None]
    places = half + np.arange(half)[None, :]
    freq = np.where(rows < half, rows, rows - half)
    angle = (places * freq % size) * (2.0 * np.pi / size)
    weight = np.where(freq == 0, 1.0, 2.0) / size
    nyquist = np.where(places % 2 == 0, 1.0, -1.0) / size
    table = np.where(
        rows < half, weight * np.cos(angle), np.where(rows == half, nyquist, -weight * np.sin(angle))
    )
    return table[paired_columns(half)].astype(ml_dtypes.bfloat16)


def call(kernel, in_specs, out_specs, outs, grid=(), scratch=(), megabytes=16, flops=0, moved=0, scalars=0, aliases=None):
    inner = pl.pallas_call(
        kernel,
        grid_spec=pltpu.PrefetchScalarGridSpec(
            num_scalar_prefetch=scalars,
            grid=grid,
            in_specs=in_specs,
            out_specs=out_specs,
            scratch_shapes=list(scratch),
        ),
        out_shape=[pltpu.HBM(shape, dtype) for shape, dtype in outs],
        input_output_aliases=aliases or {},
        compiler_params=pltpu.CompilerParams(vmem_limit_bytes=megabytes * 1024 * 1024),
        cost_estimate=pl.CostEstimate(flops=flops, bytes_accessed=moved, transcendentals=0),
    )

    def run(*args, free=()):
        pinned = [
            a if k < scalars or k in free else pltpu.with_memory_space_constraint(a, pltpu.HBM)
            for k, a in enumerate(args)
        ]
        return inner(*pinned)

    return run


def store_turned(value, o_ref):
    o_ref[...] = value.T.reshape(o_ref.shape).astype(o_ref.dtype)


def turn_kernel(x_ref, s_ref, o_ref, tail_ref):
    tail_ref[...] = s_ref[:, s_ref.shape[1] - 2 :]
    store_turned(x_ref[...].astype(jnp.float32), o_ref)


def turned(x, streams, count, parts):
    rows, chan = x.shape
    own = chan // count
    last = min(rows, 16)
    tile = chan // parts
    return call(
        turn_kernel,
        [
            pl.BlockSpec((rows, tile), lambda p: (0, p)),
            pl.BlockSpec((3, last, tile), lambda p: (0, rows // last - 1, p)),
        ],
        [
            pl.BlockSpec((count, 1, own // parts, rows), lambda p: (0, 0, p, 0)),
            pl.BlockSpec((3, 2, tile), lambda p: (0, 0, p)),
        ],
        [((count, 2, own, rows), x.dtype), ((3, 2, chan), streams.dtype)],
        grid=(parts,),
        moved=4 * rows * chan,
    )(x, streams)


def mixed(s_ref, e_ref, t_ref, q):
    rows, width = s_ref.shape[1:]
    place = lax.broadcasted_iota(jnp.int32, (8, width), 0)
    now = s_ref[q].astype(jnp.float32)
    edge = e_ref[q].astype(jnp.float32)
    one, two = (pltpu.roll(now, 1, 0), pltpu.roll(now, 2, 0))
    one_top = jnp.where(place == 0, edge[1:2], one[:8])
    two_top = jnp.where(place == 0, edge[0:1], jnp.where(place == 1, edge[1:2], two[:8]))
    one = jnp.concatenate([one_top, one[8:]], axis=0)
    two = jnp.concatenate([two_top, two[8:]], axis=0)
    return t_ref[0, q : q + 1] * now + t_ref[1, q : q + 1] * one + t_ref[2, q : q + 1] * two


def inner_kernel(s_ref, e_ref, t_ref, _, o_ref):
    store_turned(mixed(s_ref, e_ref, t_ref, 0) * mixed(s_ref, e_ref, t_ref, 1), o_ref)


def with_inner(both, streams, edges, taps, parts):
    count, _, own, rows = both.shape
    chan = count * own
    tile = chan // parts
    return call(
        inner_kernel,
        [
            pl.BlockSpec((2, rows, tile), lambda p: (0, 0, p)),
            pl.BlockSpec((3, 2, tile), lambda p: (0, 0, p)),
            pl.BlockSpec((3, 3, tile), lambda p: (0, 0, p)),
            pl.BlockSpec(memory_space=pl.ANY),
        ],
        [pl.BlockSpec((count, 1, own // parts, rows), lambda p: (0, 1, p, 0))],
        [(both.shape, both.dtype)],
        grid=(parts,),
        megabytes=32,
        moved=6 * rows * chan,
        aliases={3: 0},
    )(streams, edges, taps, both)[0]


def outer_kernel(s_ref, e_ref, t_ref, o_ref):
    o_ref[...] = mixed(s_ref, e_ref, t_ref, 0).astype(o_ref.dtype)


def outer_gate(streams, which, edges, taps, parts):
    _, rows, chan = streams.shape
    tile = chan // parts
    return call(
        outer_kernel,
        [
            pl.BlockSpec((1, rows, tile), lambda p: (which, 0, p)),
            pl.BlockSpec((1, 2, tile), lambda p: (0, 0, p)),
            pl.BlockSpec((3, 1, tile), lambda p: (0, 0, p)),
        ],
        [pl.BlockSpec((rows, tile), lambda p: (0, p))],
        [((rows, chan), jnp.bfloat16)],
        grid=(parts,),
        megabytes=32,
        moved=4 * rows * chan,
    )(streams, edges, taps)[0]


def deal_kernel(f_ref, s_ref, t_ref, o_ref, f_buf, s_buf, out_buf, sems):
    count, height, _, _ = out_buf.shape
    rows, chan = f_ref.shape
    step = chan // count // 2
    tile = chan // 4
    few = count // 2
    per = LANES // step // 2
    ins = []
    for q in range(4):
        lanes = pl.ds(q * tile, tile)
        ins.append(pltpu.make_async_copy(f_ref.at[:, lanes], f_buf.at[q], sems.at[2 * q]))
        ins.append(
            pltpu.make_async_copy(s_ref.at[pl.ds(0, 2), :, lanes], s_buf.at[q], sems.at[2 * q + 1])
        )
    for copy in ins:
        copy.start()
    outs, edges = ([], [])
    for q in range(4):
        p, owner = (q // 2, q % 2 * few)
        lanes = slice(q * tile, (q + 1) * tile)
        ins[2 * q].wait()
        values = [f_buf[q].astype(jnp.float32)]
        ins[2 * q + 1].wait()
        both = []
        for stream in range(2):
            now = s_buf[q, stream].astype(jnp.float32)
            value = t_ref[0, stream : stream + 1, lanes] * now
            value = value + t_ref[1, stream : stream + 1, lanes] * pltpu.roll(now, 1, 0)
            both.append(value + t_ref[2, stream : stream + 1, lanes] * pltpu.roll(now, 2, 0))
        values.append(both[0] * both[1])
        for k in range(2):
            value = values[k].astype(o_ref.dtype).T
            for c in range(rows // LANES):
                place = ((2 * p + k) * rows // LANES + c) * step // 8
                out_buf[owner : owner + few, place : place + step // 8] = value[
                    :, c * LANES : (c + 1) * LANES
                ].reshape(few, step // 8, 8, LANES)
        ends = [s_buf[q, k, a : a + 2].astype(jnp.float32) for a in (0, rows - 2) for k in range(2)]
        ends = jnp.concatenate(ends, axis=0)
        edges.append(ends)
        if p == 1:
            for g in range(few // per):
                lanes = slice(g * LANES // 2, (g + 1) * LANES // 2)
                value = jnp.concatenate([edges[q - 2][:, lanes], edges[q][:, lanes]], axis=1)
                first = owner + g * per
                out_buf[first : first + per, height - 1] = jnp.broadcast_to(
                    value[None].astype(o_ref.dtype), (per, 8, LANES)
                )
        some = (pl.ds(owner, few), pl.ds(p * (height // 2), height // 2))
        outs.append(pltpu.make_async_copy(out_buf.at[some], o_ref.at[some], sems.at[8 + q]))
        outs[q].start()
    some = pl.ds(height - 1, 1)
    outs.append(pltpu.make_async_copy(out_buf.at[:, some], o_ref.at[:, some], sems.at[12]))
    outs[4].start()
    for copy in outs:
        copy.wait()


def deal(filters, streams, taps, count):
    rows, chan = filters.shape
    shape = (count, chan // count * rows // LANES // 4 + 1, 8, LANES)
    anywhere, vmem = (pl.BlockSpec(memory_space=pl.ANY), pl.BlockSpec(memory_space=pltpu.VMEM))
    bf16 = jnp.bfloat16
    return call(
        deal_kernel,
        [anywhere, anywhere, vmem],
        [anywhere],
        [(shape, bf16)],
        scratch=[
            pltpu.VMEM((4, rows, chan // 4), bf16),
            pltpu.VMEM((4, 2, rows, chan // 4), bf16),
            pltpu.VMEM(shape, bf16),
            pltpu.SemaphoreType.DMA((13,)),
        ],
        megabytes=32,
        moved=10 * rows * chan,
    )(filters, streams, taps)[0]


def first_tokens(ends, taps):
    count = ends.shape[0]

    def at(row):
        return ends[:, row].astype(jnp.float32)

    block = lax.broadcasted_iota(jnp.int32, (count, LANES), 0)

    def before(row):
        return jnp.where(block == 0, 0.0, pltpu.roll(at(row), 1, 0))

    values = [1.0, 1.0]
    for q in range(2):
        t0, t1, t2 = (taps[2 * m + q : 2 * m + q + 1] for m in range(3))
        one, two = (at(2 * q), at(2 * q + 1))
        far, near = (before(4 + 2 * q), before(5 + 2 * q))
        values[0] = values[0] * (t0 * one + t1 * near + t2 * far)
        values[1] = values[1] * (t0 * two + t1 * one + t2 * near)
    rest = jnp.zeros((LANES - 2 * count, LANES), jnp.float32)
    return jnp.concatenate(values + [rest], axis=0).T


def conv_kernel(split, place_ref, both_ref, head_ref, back_ref, skip_ref, taps_ref, o_ref, *scratch):
    head_buf, back_buf, spec_ref, factor_ref, low_ref, x_buf, fix_ref, sems = scratch
    count, _, part, rows = o_ref.shape
    tiles = rows // LANES
    high = min(part, 16)
    group = 2
    low = part * (split or 0)
    copies = [
        pltpu.make_async_copy(
            head_ref.at[:, pl.ds(t * 2 * LANES, 2 * LANES)], head_buf.at[t], sems.at[t]
        )
        for t in range(tiles)
    ]
    copies.append(pltpu.make_async_copy(back_ref, back_buf, sems.at[tiles]))
    for copy in copies:
        copy.start()
    height = count * part

    def arrived(kind):
        if split is None:
            return both_ref[:, kind * part : (kind + 1) * part].reshape(height, rows)
        first = (2 * split + kind) * tiles
        places = [(first + c) * part // 8 for c in range(tiles)]
        pieces = [both_ref[:, a : a + part // 8].reshape(height, LANES) for a in places]
        return jnp.concatenate(pieces, axis=1)

    x_buf[...] = arrived(1).reshape(count, part, rows)
    if split is not None:
        ends = both_ref[:, both_ref.shape[1] - 1]
        fix_ref[...] = first_tokens(ends, taps_ref[...])
        first = split * (LANES // 2) + place_ref[0] * part
        mine = fix_ref[pl.ds(pl.multiple_of(first, part), part), :]
        lane = lax.broadcasted_iota(jnp.int32, (part, LANES), 1)
        for block in range(count):
            one = pltpu.roll(mine, (LANES - block) % LANES, 1)
            two = pltpu.roll(mine, (LANES - block - count + 1) % LANES, 1)
            value = x_buf[block, :, :LANES].astype(jnp.float32)
            value = jnp.where(lane == 0, one, jnp.where(lane == 1, two, value))
            x_buf[block, :, :LANES] = value.astype(x_buf.dtype)
    filters = arrived(0)
    odd = lax.broadcasted_iota(jnp.int32, (height, 2 * LANES), 1) % 2 == 1
    lane = lax.broadcasted_iota(jnp.int32, (high, LANES), 1)

    lane0 = lax.broadcasted_iota(jnp.int32, (height, LANES), 1) == 0

    def spectra(t):
        value = jnp.dot(filters, head_buf[t], preferred_element_type=jnp.float32)
        earlier = jnp.concatenate([jnp.zeros_like(value[:part]), value[:-part]], axis=0)
        window = earlier + jnp.where(odd, -value, value)
        real, imag = (window[:, :LANES], window[:, LANES:])
        factor_ref[t, :, :LANES] = real
        less, more = (imag - real, real + imag)
        if t == 0:
            less, more = (jnp.where(lane0, real, less), jnp.where(lane0, imag, more))
        factor_ref[t, :, LANES : 2 * LANES] = less
        factor_ref[t, :, 2 * LANES :] = more
        spec_ref[t] = jnp.dot(
            x_buf[...].reshape(height, rows), head_buf[t], preferred_element_type=jnp.float32
        )

    def products(t, slab):
        base = slab * high
        if not isinstance(base, int):
            base = pl.multiple_of(base, high)
        for start in range(0, count, group):
            sums = [[None] * 3 for _ in range(group)]
            factors = {}
            for source in range(start + group):
                place = pl.ds(base + source * part, high)
                real, imag = (spec_ref[t, place, :LANES], spec_ref[t, place, LANES:])
                both = real + imag
                for g in range(group):
                    lag = start + g - source
                    if lag < 0:
                        continue
                    if lag not in factors:
                        place = pl.ds(base + lag * part, high)
                        factors[lag] = [
                            factor_ref[t, place, c * LANES : (c + 1) * LANES] for c in range(3)
                        ]
                    a, b, c = factors[lag]
                    terms = (both * a, real * b, imag * c)
                    before = sums[g]
                    sums[g] = [u if p is None else p + u for p, u in zip(before, terms)]
            for g in range(group):
                a, b, c = sums[g]
                place = pl.ds(base + (start + g) * part, high)
                re, im = (a - c, a + b)
                if t == 0:
                    re, im = (jnp.where(lane == 0, b, re), jnp.where(lane == 0, c, im))
                low_ref[place, t * 2 * LANES : t * 2 * LANES + LANES] = re.astype(low_ref.dtype)
                low_ref[place, t * 2 * LANES + LANES : (t + 1) * 2 * LANES] = im.astype(low_ref.dtype)

    for copy in copies:
        copy.wait()
    for t in range(tiles):
        spectra(t)
        if split is not None:
            for slab in range(part // high):
                products(t, slab)
        else:

            def one_slab(slab, carry, t=t):
                products(t, slab)
                return carry

            lax.fori_loop(0, part // high, one_slab, 0)
    back = jnp.dot(
        low_ref[...].astype(jnp.bfloat16), back_buf[...], preferred_element_type=jnp.float32
    )
    value = back.reshape(count, part, rows)
    skip = skip_ref[low : low + part, :1][None]
    value = value + skip * x_buf[...].astype(jnp.float32)
    for copy in range(o_ref.shape[1]):
        o_ref[:, copy] = value.astype(o_ref.dtype)


def long_conv(both, head, back, skip, taps, place, split, copies=1):
    count, rows = (both.shape[0], head.shape[0])
    own = skip.shape[0]
    part = own if split is None else own // 2
    height = count * part
    vmem, anywhere = (pl.BlockSpec(memory_space=pltpu.VMEM), pl.BlockSpec(memory_space=pl.ANY))
    return call(
        functools.partial(conv_kernel, split),
        [pl.BlockSpec(memory_space=pltpu.SMEM), vmem, anywhere, anywhere, vmem, vmem],
        [vmem],
        [((count, copies, part, rows), jnp.bfloat16)],
        scratch=[
            pltpu.VMEM((rows // LANES, rows, 2 * LANES), jnp.bfloat16),
            pltpu.VMEM(back.shape, jnp.bfloat16),
            pltpu.VMEM((rows // LANES, height, 2 * LANES), jnp.float32),
            pltpu.VMEM((rows // LANES, height, 3 * LANES), jnp.float32),
            pltpu.VMEM((height, 2 * rows), jnp.float32 if part % 16 else jnp.bfloat16),
            pltpu.VMEM((count, part, rows), jnp.bfloat16),
            pltpu.VMEM((LANES, LANES), jnp.float32),
            pltpu.SemaphoreType.DMA((rows // LANES + 1,)),
        ],
        megabytes=28,
        flops=12 * height * rows * rows,
        moved=height * rows * 8,
    )(place, both, head, back, skip, taps, free=(0, 1))[0]


def gated_part(long, outer, first):
    count, step, rows = long.shape
    value = long.reshape(count * step, rows).T.astype(jnp.float32)
    outer = outer.astype(jnp.float32)
    outer = jnp.concatenate([outer[:8] + first, outer[8:]], axis=0)
    return (outer * value).astype(jnp.bfloat16)


def gate_kernel(long_ref, outer_ref, first_ref, o_ref):
    o_ref[...] = gated_part(long_ref[...], outer_ref[...], first_ref[...])


def gate(long, outer, first):
    rows = outer.shape[0]
    width = long.shape[0] * long.shape[1]
    return call(
        gate_kernel,
        [
            pl.BlockSpec(long.shape, lambda n: (0, 0, 0)),
            pl.BlockSpec((rows, width), lambda n: (0, 0)),
            pl.BlockSpec((8, width), lambda n: (0, 0)),
        ],
        [pl.BlockSpec((rows, width), lambda n: (0, 0))],
        [((rows, width), jnp.bfloat16)],
        grid=(1,),
        moved=6 * rows * width,
    )(long, outer, first, free=(0,))[0]


def own_kernel(here_ref, gated_ref, weight_ref, o_ref):
    value = jnp.dot(gated_ref[...], weight_ref[...], preferred_element_type=jnp.float32)
    o_ref[...] = value.astype(o_ref.dtype)


def own_term(here, gated, out_weight, cols):
    rows, used = gated.shape
    wide = cols // 2
    return call(
        own_kernel,
        [
            pl.BlockSpec((rows, used), lambda n, h: (0, 0)),
            pl.BlockSpec((used, wide), lambda n, h: (0, h[0] * 2 + n)),
        ],
        [pl.BlockSpec((rows, wide), lambda n, h: (0, n))],
        [((rows, cols), jnp.bfloat16)],
        grid=(2,),
        flops=2 * rows * used * cols,
        moved=rows * cols * 2 + used * cols * 2,
        scalars=1,
    )(here, gated, out_weight)[0]


def last_kernel(
    place_ref, sent_ref, dealt_ref, first_ref, sum_ref, mine_ref, theirs_ref, *refs
):
    blocks, (weight_ref, o_ref, *scratch) = (refs[:4], refs[4:])
    outer_buf, weight_buf, block_buf, sum_buf, out_buf, gated_ref, sems = scratch
    here, core = (place_ref[0], place_ref[1])
    rows, used = outer_buf.shape[1:]
    wide = out_buf.shape[2]
    cols = 4 * wide
    pairs = [(mine_ref.at[:, pl.ds(used, used)], outer_buf.at[0]), (theirs_ref, outer_buf.at[1])]
    gates = [pltpu.make_async_copy(a, b, sems.at[g]) for g, (a, b) in enumerate(pairs)]
    for copy in gates:
        copy.start()
    places, inputs = ([], [])
    for k in range(4):
        column = pl.multiple_of((2 * (core ^ k // 2) + k % 2) * wide, wide)
        places.append(pl.ds(column, wide))
        ours = pl.multiple_of(here * cols + column, wide)
        pairs = [
            (blocks[k], block_buf.at[k]),
            (weight_ref.at[pl.ds(used, used), pl.ds(ours, wide)], weight_buf.at[k]),
            (sum_ref.at[:, places[k]], sum_buf.at[k]),
        ]
        inputs.append(
            [pltpu.make_async_copy(a, b, sems.at[2 + 3 * k + i]) for i, (a, b) in enumerate(pairs)]
        )
        for copy in inputs[k]:
            copy.start()
    for g in range(2):
        gates[g].wait()
        long = dealt_ref[:, here if g == 0 else 1 - here]
        gated_ref[g] = gated_part(long, outer_buf[g], first_ref[g])
    outputs = []
    for k in range(4):
        for copy in inputs[k]:
            copy.wait()
        value = sum_buf[k].astype(jnp.float32)
        for left, right in (
            (sent_ref[...], block_buf[k, :used]),
            (gated_ref[1], block_buf[k, used:]),
            (gated_ref[0], weight_buf[k]),
        ):
            value = value + jnp.dot(left, right, preferred_element_type=jnp.float32)
        out_buf[k] = value.astype(out_buf.dtype)
        outputs.append(pltpu.make_async_copy(out_buf.at[k], o_ref.at[:, places[k]], sems.at[14 + k]))
        outputs[k].start()
    for copy in outputs:
        copy.wait()


def last_term(place, sent, dealt, first, total, mine, theirs, blocks, out_weight):
    rows, cols = total.shape
    chan = mine.shape[1]
    wide = cols // 4
    used = chan // 2
    vmem, anywhere = (pl.BlockSpec(memory_space=pltpu.VMEM), pl.BlockSpec(memory_space=pl.ANY))
    bf16 = jnp.bfloat16
    return call(
        last_kernel,
        [pl.BlockSpec(memory_space=pltpu.SMEM), vmem, vmem, vmem] + [anywhere] * 8,
        [anywhere],
        [((rows, cols), bf16)],
        scratch=[
            pltpu.VMEM((2, rows, used), bf16),
            pltpu.VMEM((4, used, wide), bf16),
            pltpu.VMEM((4, chan, wide), bf16),
            pltpu.VMEM((4, rows, wide), bf16),
            pltpu.VMEM((4, rows, wide), bf16),
            pltpu.VMEM((2, rows, used), bf16),
            pltpu.SemaphoreType.DMA((18,)),
        ],
        megabytes=32,
        flops=24 * rows * used * wide,
        moved=rows * wide * 16 + used * wide * 24,
    )(place, sent, dealt, first, total, mine, theirs, *blocks, out_weight, free=(0, 1, 2, 3))[0]


def exchanged(value):
    return lax.all_to_all(value, "ctx", 0, 0, tiled=True)


def to_groups(values):
    groups = lax.axis_size("ch")
    return [
        lax.ppermute(value, "ch", [(g, (g + s) % groups) for g in range(groups)])
        for s, value in enumerate(values, 1)
    ]


def any_groups(long, outer, out_weight):
    rows, chan = outer.shape
    groups = lax.axis_size("ch")
    here = lax.axis_index("ch")
    cols = out_weight.shape[1] // groups
    gated = gated_part(long, outer, jnp.zeros((8, chan), jnp.float32))
    total = jnp.zeros((rows, cols), jnp.float32)
    weights = [
        lax.dynamic_slice(out_weight, (0, (here + s) % groups * cols), (chan, cols))
        for s in range(groups)
    ]
    values = [gated] + to_groups([gated] * (groups - 1))
    for value, weight in zip(values, weights[:1] + to_groups(weights[1:])):
        total = total + jnp.dot(value, weight, preferred_element_type=jnp.float32)
    return total.astype(jnp.bfloat16)


def local(streams, short_taps, filters, skip_gain, out_weight):
    rows, _, chan = streams.shape
    count = lax.axis_size("ctx")
    groups = lax.axis_size("ch")
    own = chan // count
    step = own // 2
    fast = groups == 2 and count % 4 == 0 and own % 32 == 0 and count % 2 == 0 and LANES % (2 * step) == 0
    fast = fast and rows % LANES == 0 and 2 * count <= LANES and chan % (4 * LANES) == 0
    after = lax.optimization_barrier
    position, here = (lax.axis_index("ctx"), lax.axis_index("ch"))
    head = jnp.asarray(head_table(2 * rows))
    back = jnp.asarray(inverse_table(2 * rows))
    streams = streams.transpose(1, 0, 2)
    parts = 2 if fast else 1
    skip = skip_gain.reshape(parts, count, own // parts)
    skip = lax.dynamic_index_in_dim(skip, position, 1, False)
    skip = jnp.broadcast_to(skip.reshape(own, 1), (own, LANES))
    if not fast:
        both, tail = turned(filters, streams, count, parts)
        edges = passed_along(tail, "ctx", 1)
        both = exchanged(with_inner(both, streams, edges, short_taps, parts))
        both = both.reshape(count, 2 * own, rows)
        outer = outer_gate(streams, 2, edges[2:], short_taps[:, 2:], parts)
        none = jnp.zeros((8, LANES), jnp.float32)
        long = long_conv(both, head, back, skip, none, jnp.zeros((1,), jnp.int32), None)
        return any_groups(exchanged(long[:, 0]), outer, out_weight)
    per = LANES // step // 2
    place = (position % per)[None]
    taps = short_taps[:, :2].reshape(6, 2, chan // 2)
    taps = lax.dynamic_slice(taps, (0, 0, position // per * (LANES // 2)), (6, 2, LANES // 2))
    taps = jnp.pad(taps.reshape(6, LANES), ((0, 2), (0, 0)))
    both = exchanged(deal(filters, streams, short_taps, count))
    cols = out_weight.shape[1] // groups
    wide = cols // 4
    columns = [(1 - here) * cols + (position % 2 * 2 + k) * wide for k in range(2)]
    near = [lax.dynamic_slice(out_weight, (0, c), (chan, wide)) for c in columns]
    near, none = after((near, jnp.zeros((1, 2, chan), jnp.float32)))
    outer = outer_gate(streams, 2, none, short_taps[:, 2:], 2)
    theirs = to_groups([outer[:, chan // 2 :]])[0]
    near, skip, taps = after((near, skip, taps))
    near, tail = after((near, streams[2, rows - 2 :]))
    near = [to_groups([n])[0] for n in near]

    def swapped(value, bit):
        return lax.ppermute(value, "ctx", [(i, i ^ bit) for i in range(count)])

    both, outer, theirs = after((both, outer, theirs))
    early = long_conv(both, head, back, skip, taps, place, 0)[:, 0]
    edges, early = after((passed_along(tail, "ctx", 1), early))
    edges = edges.astype(jnp.float32)
    first = jnp.stack(
        [short_taps[1, 2] * edges[1] + short_taps[2, 2] * edges[0], short_taps[2, 2] * edges[1]]
    )
    first = jnp.pad(first, ((0, 6), (0, 0)))
    other = to_groups([first[:, chan // 2 :]])[0]
    both, _ = after((both, early))
    late = long_conv(both, head, back, skip, taps, place, 1, copies=groups)
    late, near = after((late, near))
    blocks = near + [swapped(n, 1) for n in near]
    early, late, other, first = after((exchanged(early), late, other, first))
    gated = gate(early, outer, first)
    sent = to_groups([gated])[0]
    dealt = lax.all_to_all(
        late.reshape(count * groups, step, rows), ("ctx", "ch"), 0, 0, tiled=True
    )
    dealt = dealt.reshape(count, groups, step, rows)
    total = own_term(here[None], gated, out_weight, cols)
    place = jnp.stack([here, position % 2])
    first = jnp.stack([first[:, chan // 2 :], other])
    return last_term(place, sent, dealt, first, total, outer, theirs, blocks, out_weight)


def solution(mesh):
    return jax.shard_map(
        local,
        mesh=mesh,
        in_specs=(
            P("ctx", None, "ch"),
            P(None, None, "ch"),
            P("ctx", "ch"),
            P("ch"),
            P("ch", None),
        ),
        out_specs=P("ctx", "ch"),
        check_vma=False,
    )
```

```python
import functools

import jax
import jax.numpy as jnp
import ml_dtypes
import numpy as np
from jax import lax
from jax.experimental import pallas as pl
from jax.experimental.pallas import tpu as pltpu
from jax.sharding import PartitionSpec as P

LANES = 128


def passed_along(value, axis, steps):
    count = lax.axis_size(axis)
    initial, last = (max(0, -steps), min(count, count - steps))
    return lax.ppermute(value, axis, [(source, source + steps) for source in range(initial, last)])


def paired_columns(half):
    order = np.arange(2 * half).reshape(2, half // LANES, LANES)
    return order.transpose(1, 0, 2).reshape(-1)


def head_table(size):
    half = size // 2
    rows = np.arange(half)[:, None]
    cols = np.arange(size)[None, :]
    freq = np.where(cols < half, cols, cols - half)
    angle = (rows * freq % size) * (2.0 * np.pi / size)
    nyquist = np.where(rows % 2 == 0, 1.0, -1.0)
    table = np.where(cols < half, np.cos(angle), np.where(cols == half, nyquist, -np.sin(angle)))
    return table[:, paired_columns(half)].astype(ml_dtypes.bfloat16)


def inverse_table(size):
    half = size // 2
    rows = np.arange(size)[:, None]
    places = half + np.arange(half)[None, :]
    freq = np.where(rows < half, rows, rows - half)
    angle = (places * freq % size) * (2.0 * np.pi / size)
    weight = np.where(freq == 0, 1.0, 2.0) / size
    nyquist = np.where(places % 2 == 0, 1.0, -1.0) / size
    table = np.where(
        rows < half, weight * np.cos(angle), np.where(rows == half, nyquist, -weight * np.sin(angle))
    )
    return table[paired_columns(half)].astype(ml_dtypes.bfloat16)


def call(kernel, in_specs, out_specs, outs, grid=(), scratch=(), megabytes=16, flops=0, moved=0, scalars=0, aliases=None):
    inner = pl.pallas_call(
        kernel,
        grid_spec=pltpu.PrefetchScalarGridSpec(
            num_scalar_prefetch=scalars,
            grid=grid,
            in_specs=in_specs,
            out_specs=out_specs,
            scratch_shapes=list(scratch),
        ),
        out_shape=[pltpu.HBM(shape, dtype) for shape, dtype in outs],
        input_output_aliases=aliases or {},
        compiler_params=pltpu.CompilerParams(vmem_limit_bytes=megabytes * 1024 * 1024),
        cost_estimate=pl.CostEstimate(flops=flops, bytes_accessed=moved, transcendentals=0),
    )

    def run(*args, free=()):
        pinned = [
            a if k < scalars or k in free else pltpu.with_memory_space_constraint(a, pltpu.HBM)
            for k, a in enumerate(args)
        ]
        return inner(*pinned)

    return run


def store_turned(value, o_ref):
    o_ref[...] = value.T.reshape(o_ref.shape).astype(o_ref.dtype)


def turn_kernel(x_ref, s_ref, o_ref, tail_ref):
    tail_ref[...] = s_ref[:, s_ref.shape[1] - 2 :]
    store_turned(x_ref[...].astype(jnp.float32), o_ref)


def turned(x, streams, count, parts):
    rows, chan = x.shape
    own = chan // count
    last = min(rows, 16)
    tile = chan // parts
    return call(
        turn_kernel,
        [
            pl.BlockSpec((rows, tile), lambda p: (0, p)),
            pl.BlockSpec((3, last, tile), lambda p: (0, rows // last - 1, p)),
        ],
        [
            pl.BlockSpec((count, 1, own // parts, rows), lambda p: (0, 0, p, 0)),
            pl.BlockSpec((3, 2, tile), lambda p: (0, 0, p)),
        ],
        [((count, 2, own, rows), x.dtype), ((3, 2, chan), streams.dtype)],
        grid=(parts,),
        moved=4 * rows * chan,
    )(x, streams)


def mixed(s_ref, e_ref, t_ref, q):
    rows, width = s_ref.shape[1:]
    place = lax.broadcasted_iota(jnp.int32, (8, width), 0)
    now = s_ref[q].astype(jnp.float32)
    edge = e_ref[q].astype(jnp.float32)
    one, two = (pltpu.roll(now, 1, 0), pltpu.roll(now, 2, 0))
    one_top = jnp.where(place == 0, edge[1:2], one[:8])
    two_top = jnp.where(place == 0, edge[0:1], jnp.where(place == 1, edge[1:2], two[:8]))
    one = jnp.concatenate([one_top, one[8:]], axis=0)
    two = jnp.concatenate([two_top, two[8:]], axis=0)
    return t_ref[0, q : q + 1] * now + t_ref[1, q : q + 1] * one + t_ref[2, q : q + 1] * two


def inner_kernel(s_ref, e_ref, t_ref, _, o_ref):
    store_turned(mixed(s_ref, e_ref, t_ref, 0) * mixed(s_ref, e_ref, t_ref, 1), o_ref)


def with_inner(both, streams, edges, taps, parts):
    count, _, own, rows = both.shape
    chan = count * own
    tile = chan // parts
    return call(
        inner_kernel,
        [
            pl.BlockSpec((2, rows, tile), lambda p: (0, 0, p)),
            pl.BlockSpec((3, 2, tile), lambda p: (0, 0, p)),
            pl.BlockSpec((3, 3, tile), lambda p: (0, 0, p)),
            pl.BlockSpec(memory_space=pl.ANY),
        ],
        [pl.BlockSpec((count, 1, own // parts, rows), lambda p: (0, 1, p, 0))],
        [(both.shape, both.dtype)],
        grid=(parts,),
        megabytes=32,
        moved=6 * rows * chan,
        aliases={3: 0},
    )(streams, edges, taps, both)[0]


def outer_kernel(s_ref, e_ref, t_ref, o_ref):
    o_ref[...] = mixed(s_ref, e_ref, t_ref, 0).astype(o_ref.dtype)


def outer_gate(streams, which, edges, taps, parts):
    _, rows, chan = streams.shape
    tile = chan // parts
    return call(
        outer_kernel,
        [
            pl.BlockSpec((1, rows, tile), lambda p: (which, 0, p)),
            pl.BlockSpec((1, 2, tile), lambda p: (0, 0, p)),
            pl.BlockSpec((3, 1, tile), lambda p: (0, 0, p)),
        ],
        [pl.BlockSpec((rows, tile), lambda p: (0, p))],
        [((rows, chan), jnp.bfloat16)],
        grid=(parts,),
        megabytes=32,
        moved=4 * rows * chan,
    )(streams, edges, taps)[0]


def deal_kernel(f_ref, s_ref, t_ref, o_ref, f_buf, s_buf, out_buf, sems):
    count, height, _, _ = out_buf.shape
    rows, chan = f_ref.shape
    step = chan // count // 2
    tile = chan // 4
    few = count // 2
    per = LANES // step // 2
    ins = []
    for q in range(4):
        lanes = pl.ds(q * tile, tile)
        ins.append(pltpu.make_async_copy(f_ref.at[:, lanes], f_buf.at[q], sems.at[2 * q]))
        ins.append(
            pltpu.make_async_copy(s_ref.at[pl.ds(0, 2), :, lanes], s_buf.at[q], sems.at[2 * q + 1])
        )
    for copy in ins:
        copy.start()
    outs, edges = ([], [])
    for q in range(4):
        p, owner = (q // 2, q % 2 * few)
        lanes = slice(q * tile, (q + 1) * tile)
        ins[2 * q].wait()
        values = [f_buf[q].astype(jnp.float32)]
        ins[2 * q + 1].wait()
        both = []
        for stream in range(2):
            now = s_buf[q, stream].astype(jnp.float32)
            value = t_ref[0, stream : stream + 1, lanes] * now
            value = value + t_ref[1, stream : stream + 1, lanes] * pltpu.roll(now, 1, 0)
            both.append(value + t_ref[2, stream : stream + 1, lanes] * pltpu.roll(now, 2, 0))
        values.append(both[0] * both[1])
        for k in range(2):
            value = values[k].astype(o_ref.dtype).T
            for c in range(rows // LANES):
                place = ((2 * p + k) * rows // LANES + c) * step // 8
                out_buf[owner : owner + few, place : place + step // 8] = value[
                    :, c * LANES : (c + 1) * LANES
                ].reshape(few, step // 8, 8, LANES)
        ends = [s_buf[q, k, a : a + 2].astype(jnp.float32) for a in (0, rows - 2) for k in range(2)]
        ends = jnp.concatenate(ends, axis=0)
        edges.append(ends)
        if p == 1:
            for g in range(few // per):
                lanes = slice(g * LANES // 2, (g + 1) * LANES // 2)
                value = jnp.concatenate([edges[q - 2][:, lanes], edges[q][:, lanes]], axis=1)
                first = owner + g * per
                out_buf[first : first + per, height - 1] = jnp.broadcast_to(
                    value[None].astype(o_ref.dtype), (per, 8, LANES)
                )
        some = (pl.ds(owner, few), pl.ds(p * (height // 2), height // 2))
        outs.append(pltpu.make_async_copy(out_buf.at[some], o_ref.at[some], sems.at[8 + q]))
        outs[q].start()
    some = pl.ds(height - 1, 1)
    outs.append(pltpu.make_async_copy(out_buf.at[:, some], o_ref.at[:, some], sems.at[12]))
    outs[4].start()
    for copy in outs:
        copy.wait()


def deal(filters, streams, taps, count):
    rows, chan = filters.shape
    shape = (count, chan // count * rows // LANES // 4 + 1, 8, LANES)
    anywhere, vmem = (pl.BlockSpec(memory_space=pl.ANY), pl.BlockSpec(memory_space=pltpu.VMEM))
    bf16 = jnp.bfloat16
    return call(
        deal_kernel,
        [anywhere, anywhere, vmem],
        [anywhere],
        [(shape, bf16)],
        scratch=[
            pltpu.VMEM((4, rows, chan // 4), bf16),
            pltpu.VMEM((4, 2, rows, chan // 4), bf16),
            pltpu.VMEM(shape, bf16),
            pltpu.SemaphoreType.DMA((13,)),
        ],
        megabytes=32,
        moved=10 * rows * chan,
    )(filters, streams, taps)[0]


def first_tokens(ends, taps):
    count = ends.shape[0]

    def at(row):
        return ends[:, row].astype(jnp.float32)

    block = lax.broadcasted_iota(jnp.int32, (count, LANES), 0)

    def before(row):
        return jnp.where(block == 0, 0.0, pltpu.roll(at(row), 1, 0))

    values = [1.0, 1.0]
    for q in range(2):
        t0, t1, t2 = (taps[2 * m + q : 2 * m + q + 1] for m in range(3))
        one, two = (at(2 * q), at(2 * q + 1))
        far, near = (before(4 + 2 * q), before(5 + 2 * q))
        values[0] = values[0] * (t0 * one + t1 * near + t2 * far)
        values[1] = values[1] * (t0 * two + t1 * one + t2 * near)
    rest = jnp.zeros((LANES - 2 * count, LANES), jnp.float32)
    return jnp.concatenate(values + [rest], axis=0).T


def conv_kernel(split, place_ref, both_ref, head_ref, back_ref, skip_ref, taps_ref, o_ref, *scratch):
    head_buf, back_buf, spec_ref, factor_ref, low_ref, x_buf, fix_ref, sems = scratch
    count, _, part, rows = o_ref.shape
    tiles = rows // LANES
    high = min(part, 16)
    group = 2
    low = part * (split or 0)
    copies = [
        pltpu.make_async_copy(
            head_ref.at[:, pl.ds(t * 2 * LANES, 2 * LANES)], head_buf.at[t], sems.at[t]
        )
        for t in range(tiles)
    ]
    copies.append(pltpu.make_async_copy(back_ref, back_buf, sems.at[tiles]))
    for copy in copies:
        copy.start()
    height = count * part

    def arrived(kind):
        if split is None:
            return both_ref[:, kind * part : (kind + 1) * part].reshape(height, rows)
        first = (2 * split + kind) * tiles
        places = [(first + c) * part // 8 for c in range(tiles)]
        pieces = [both_ref[:, a : a + part // 8].reshape(height, LANES) for a in places]
        return jnp.concatenate(pieces, axis=1)

    x_buf[...] = arrived(1).reshape(count, part, rows)
    if split is not None:
        ends = both_ref[:, both_ref.shape[1] - 1]
        fix_ref[...] = first_tokens(ends, taps_ref[...])
        first = split * (LANES // 2) + place_ref[0] * part
        mine = fix_ref[pl.ds(pl.multiple_of(first, part), part), :]
        lane = lax.broadcasted_iota(jnp.int32, (part, LANES), 1)
        later = pltpu.roll(mine, LANES - count + 1, 1)
        for block in range(count):
            tokens = pltpu.roll(jnp.where(lane == block, mine, later), (LANES - block) % LANES, 1)
            value = x_buf[block, :, :LANES].astype(jnp.float32)
            value = jnp.where(lane < 2, tokens, value)
            x_buf[block, :, :LANES] = value.astype(x_buf.dtype)
    filters = arrived(0)
    odd = lax.broadcasted_iota(jnp.int32, (height, 2 * LANES), 1) % 2 == 1
    lane = lax.broadcasted_iota(jnp.int32, (high, LANES), 1)

    lane0 = lax.broadcasted_iota(jnp.int32, (height, LANES), 1) == 0

    def spectra(t):
        value = jnp.dot(filters, head_buf[t], preferred_element_type=jnp.float32)
        earlier = jnp.concatenate([jnp.zeros_like(value[:part]), value[:-part]], axis=0)
        window = earlier + jnp.where(odd, -value, value)
        real, imag = (window[:, :LANES], window[:, LANES:])
        factor_ref[t, :, :LANES] = real
        less, more = (imag - real, real + imag)
        if t == 0:
            less, more = (jnp.where(lane0, real, less), jnp.where(lane0, imag, more))
        factor_ref[t, :, LANES : 2 * LANES] = less
        factor_ref[t, :, 2 * LANES :] = more
        spec_ref[t] = jnp.dot(
            x_buf[...].reshape(height, rows), head_buf[t], preferred_element_type=jnp.float32
        )

    def products(t, slab):
        base = slab * high
        if not isinstance(base, int):
            base = pl.multiple_of(base, high)
        for start in range(0, count, group):
            sums = [[None] * 3 for _ in range(group)]
            factors = {}
            for source in range(start + group):
                place = pl.ds(base + source * part, high)
                real, imag = (spec_ref[t, place, :LANES], spec_ref[t, place, LANES:])
                both = real + imag
                for g in range(group):
                    lag = start + g - source
                    if lag < 0:
                        continue
                    if lag not in factors:
                        place = pl.ds(base + lag * part, high)
                        factors[lag] = [
                            factor_ref[t, place, c * LANES : (c + 1) * LANES] for c in range(3)
                        ]
                    a, b, c = factors[lag]
                    terms = (both * a, real * b, imag * c)
                    before = sums[g]
                    sums[g] = [u if p is None else p + u for p, u in zip(before, terms)]
            for g in range(group):
                a, b, c = sums[g]
                place = pl.ds(base + (start + g) * part, high)
                re, im = (a - c, a + b)
                if t == 0:
                    re, im = (jnp.where(lane == 0, b, re), jnp.where(lane == 0, c, im))
                low_ref[place, t * 2 * LANES : t * 2 * LANES + LANES] = re.astype(low_ref.dtype)
                low_ref[place, t * 2 * LANES + LANES : (t + 1) * 2 * LANES] = im.astype(low_ref.dtype)

    for copy in copies:
        copy.wait()
    for t in range(tiles):
        spectra(t)
        if split is not None:
            for slab in range(part // high):
                products(t, slab)
        else:

            def one_slab(slab, carry, t=t):
                products(t, slab)
                return carry

            lax.fori_loop(0, part // high, one_slab, 0)
    back = jnp.dot(
        low_ref[...].astype(jnp.bfloat16), back_buf[...], preferred_element_type=jnp.float32
    )
    value = back.reshape(count, part, rows)
    skip = skip_ref[low : low + part, :1][None]
    value = value + skip * x_buf[...].astype(jnp.float32)
    for copy in range(o_ref.shape[1]):
        o_ref[:, copy] = value.astype(o_ref.dtype)


def long_conv(both, head, back, skip, taps, place, split, copies=1):
    count, rows = (both.shape[0], head.shape[0])
    own = skip.shape[0]
    part = own if split is None else own // 2
    height = count * part
    vmem, anywhere = (pl.BlockSpec(memory_space=pltpu.VMEM), pl.BlockSpec(memory_space=pl.ANY))
    return call(
        functools.partial(conv_kernel, split),
        [pl.BlockSpec(memory_space=pltpu.SMEM), vmem, anywhere, anywhere, vmem, vmem],
        [vmem],
        [((count, copies, part, rows), jnp.bfloat16)],
        scratch=[
            pltpu.VMEM((rows // LANES, rows, 2 * LANES), jnp.bfloat16),
            pltpu.VMEM(back.shape, jnp.bfloat16),
            pltpu.VMEM((rows // LANES, height, 2 * LANES), jnp.float32),
            pltpu.VMEM((rows // LANES, height, 3 * LANES), jnp.float32),
            pltpu.VMEM((height, 2 * rows), jnp.float32 if part % 16 else jnp.bfloat16),
            pltpu.VMEM((count, part, rows), jnp.bfloat16),
            pltpu.VMEM((LANES, LANES), jnp.float32),
            pltpu.SemaphoreType.DMA((rows // LANES + 1,)),
        ],
        megabytes=28,
        flops=12 * height * rows * rows,
        moved=height * rows * 8,
    )(place, both, head, back, skip, taps, free=(0, 1))[0]


def gated_part(long, outer, first):
    count, step, rows = long.shape
    value = long.reshape(count * step, rows).T.astype(jnp.float32)
    outer = outer.astype(jnp.float32)
    outer = jnp.concatenate([outer[:8] + first, outer[8:]], axis=0)
    return (outer * value).astype(jnp.bfloat16)


def gate_kernel(long_ref, outer_ref, first_ref, o_ref):
    o_ref[...] = gated_part(long_ref[...], outer_ref[...], first_ref[...])


def gate(long, outer, first):
    rows = outer.shape[0]
    width = long.shape[0] * long.shape[1]
    return call(
        gate_kernel,
        [
            pl.BlockSpec(long.shape, lambda n: (0, 0, 0)),
            pl.BlockSpec((rows, width), lambda n: (0, 0)),
            pl.BlockSpec((8, width), lambda n: (0, 0)),
        ],
        [pl.BlockSpec((rows, width), lambda n: (0, 0))],
        [((rows, width), jnp.bfloat16)],
        grid=(1,),
        moved=6 * rows * width,
    )(long, outer, first, free=(0,))[0]


def own_kernel(here_ref, gated_ref, weight_ref, o_ref):
    value = jnp.dot(gated_ref[...], weight_ref[...], preferred_element_type=jnp.float32)
    o_ref[...] = value.astype(o_ref.dtype)


def own_term(here, gated, out_weight, cols):
    rows, used = gated.shape
    wide = cols // 2
    return call(
        own_kernel,
        [
            pl.BlockSpec((rows, used), lambda n, h: (0, 0)),
            pl.BlockSpec((used, wide), lambda n, h: (0, h[0] * 2 + n)),
        ],
        [pl.BlockSpec((rows, wide), lambda n, h: (0, n))],
        [((rows, cols), jnp.bfloat16)],
        grid=(2,),
        flops=2 * rows * used * cols,
        moved=rows * cols * 2 + used * cols * 2,
        scalars=1,
    )(here, gated, out_weight)[0]


def last_kernel(
    place_ref, sent_ref, dealt_ref, first_ref, sum_ref, mine_ref, theirs_ref, *refs
):
    blocks, (weight_ref, o_ref, *scratch) = (refs[:4], refs[4:])
    outer_buf, weight_buf, block_buf, sum_buf, out_buf, gated_ref, sems = scratch
    here, core = (place_ref[0], place_ref[1])
    rows, used = outer_buf.shape[1:]
    wide = out_buf.shape[2]
    cols = 4 * wide
    pairs = [(mine_ref.at[:, pl.ds(used, used)], outer_buf.at[0]), (theirs_ref, outer_buf.at[1])]
    gates = [pltpu.make_async_copy(a, b, sems.at[g]) for g, (a, b) in enumerate(pairs)]
    for copy in gates:
        copy.start()
    places, inputs = ([], [])
    for k in range(4):
        column = pl.multiple_of((2 * (core ^ k // 2) + k % 2) * wide, wide)
        places.append(pl.ds(column, wide))
        ours = pl.multiple_of(here * cols + column, wide)
        pairs = [
            (blocks[k], block_buf.at[k]),
            (weight_ref.at[pl.ds(used, used), pl.ds(ours, wide)], weight_buf.at[k]),
            (sum_ref.at[:, places[k]], sum_buf.at[k]),
        ]
        inputs.append(
            [pltpu.make_async_copy(a, b, sems.at[2 + 3 * k + i]) for i, (a, b) in enumerate(pairs)]
        )
        for copy in inputs[k]:
            copy.start()
    for g in range(2):
        gates[g].wait()
        long = dealt_ref[:, here if g == 0 else 1 - here]
        gated_ref[g] = gated_part(long, outer_buf[g], first_ref[g])
    outputs = []
    for k in range(4):
        if k < 3:
            for copy in inputs[k] + (inputs[3] if k == 2 else []):
                copy.wait()
        value = sum_buf[k].astype(jnp.float32)
        for left, right in (
            (sent_ref[...], block_buf[k, :used]),
            (gated_ref[1], block_buf[k, used:]),
            (gated_ref[0], weight_buf[k]),
        ):
            value = value + jnp.dot(left, right, preferred_element_type=jnp.float32)
        out_buf[k] = value.astype(out_buf.dtype)
        outputs.append(pltpu.make_async_copy(out_buf.at[k], o_ref.at[:, places[k]], sems.at[14 + k]))
        outputs[k].start()
    for copy in outputs:
        copy.wait()


def last_term(place, sent, dealt, first, total, mine, theirs, blocks, out_weight):
    rows, cols = total.shape
    chan = mine.shape[1]
    wide = cols // 4
    used = chan // 2
    vmem, anywhere = (pl.BlockSpec(memory_space=pltpu.VMEM), pl.BlockSpec(memory_space=pl.ANY))
    bf16 = jnp.bfloat16
    return call(
        last_kernel,
        [pl.BlockSpec(memory_space=pltpu.SMEM), vmem, vmem, vmem] + [anywhere] * 8,
        [anywhere],
        [((rows, cols), bf16)],
        scratch=[
            pltpu.VMEM((2, rows, used), bf16),
            pltpu.VMEM((4, used, wide), bf16),
            pltpu.VMEM((4, chan, wide), bf16),
            pltpu.VMEM((4, rows, wide), bf16),
            pltpu.VMEM((4, rows, wide), bf16),
            pltpu.VMEM((2, rows, used), bf16),
            pltpu.SemaphoreType.DMA((18,)),
        ],
        megabytes=32,
        flops=24 * rows * used * wide,
        moved=rows * wide * 16 + used * wide * 24,
    )(place, sent, dealt, first, total, mine, theirs, *blocks, out_weight, free=(0, 1, 2, 3))[0]


def exchanged(value):
    return lax.all_to_all(value, "ctx", 0, 0, tiled=True)


def to_groups(values):
    groups = lax.axis_size("ch")
    return [
        lax.ppermute(value, "ch", [(g, (g + s) % groups) for g in range(groups)])
        for s, value in enumerate(values, 1)
    ]


def any_groups(long, outer, out_weight):
    rows, chan = outer.shape
    groups = lax.axis_size("ch")
    here = lax.axis_index("ch")
    cols = out_weight.shape[1] // groups
    gated = gated_part(long, outer, jnp.zeros((8, chan), jnp.float32))
    total = jnp.zeros((rows, cols), jnp.float32)
    weights = [
        lax.dynamic_slice(out_weight, (0, (here + s) % groups * cols), (chan, cols))
        for s in range(groups)
    ]
    values = [gated] + to_groups([gated] * (groups - 1))
    for value, weight in zip(values, weights[:1] + to_groups(weights[1:])):
        total = total + jnp.dot(value, weight, preferred_element_type=jnp.float32)
    return total.astype(jnp.bfloat16)


def local(streams, short_taps, filters, skip_gain, out_weight):
    rows, _, chan = streams.shape
    count = lax.axis_size("ctx")
    groups = lax.axis_size("ch")
    own = chan // count
    step = own // 2
    fast = groups == 2 and count % 4 == 0 and own % 32 == 0 and count % 2 == 0 and LANES % (2 * step) == 0
    fast = fast and rows % LANES == 0 and 2 * count <= LANES and chan % (4 * LANES) == 0
    after = lax.optimization_barrier
    position, here = (lax.axis_index("ctx"), lax.axis_index("ch"))
    head = jnp.asarray(head_table(2 * rows))
    back = jnp.asarray(inverse_table(2 * rows))
    streams = streams.transpose(1, 0, 2)
    parts = 2 if fast else 1
    skip = skip_gain.reshape(parts, count, own // parts)
    skip = lax.dynamic_index_in_dim(skip, position, 1, False)
    skip = jnp.broadcast_to(skip.reshape(own, 1), (own, LANES))
    if not fast:
        both, tail = turned(filters, streams, count, parts)
        edges = passed_along(tail, "ctx", 1)
        both = exchanged(with_inner(both, streams, edges, short_taps, parts))
        both = both.reshape(count, 2 * own, rows)
        outer = outer_gate(streams, 2, edges[2:], short_taps[:, 2:], parts)
        none = jnp.zeros((8, LANES), jnp.float32)
        long = long_conv(both, head, back, skip, none, jnp.zeros((1,), jnp.int32), None)
        return any_groups(exchanged(long[:, 0]), outer, out_weight)
    per = LANES // step // 2
    place = (position % per)[None]
    taps = short_taps[:, :2].reshape(6, 2, chan // 2)
    taps = lax.dynamic_slice(taps, (0, 0, position // per * (LANES // 2)), (6, 2, LANES // 2))
    taps = jnp.pad(taps.reshape(6, LANES), ((0, 2), (0, 0)))
    both = exchanged(deal(filters, streams, short_taps, count))
    cols = out_weight.shape[1] // groups
    wide = cols // 4
    columns = [(1 - here) * cols + (position % 2 * 2 + k) * wide for k in range(2)]
    near = [lax.dynamic_slice(out_weight, (0, c), (chan, wide)) for c in columns]
    near, none = after((near, jnp.zeros((1, 2, chan), jnp.float32)))
    outer = outer_gate(streams, 2, none, short_taps[:, 2:], 2)
    theirs = to_groups([outer[:, chan // 2 :]])[0]
    near, skip, taps = after((near, skip, taps))
    near, tail = after((near, streams[2, rows - 2 :]))
    near = [to_groups([n])[0] for n in near]

    def swapped(value, bit):
        return lax.ppermute(value, "ctx", [(i, i ^ bit) for i in range(count)])

    both, outer, theirs = after((both, outer, theirs))
    early = long_conv(both, head, back, skip, taps, place, 0)[:, 0]
    edges, early = after((passed_along(tail, "ctx", 1), early))
    edges = edges.astype(jnp.float32)
    first = jnp.stack(
        [short_taps[1, 2] * edges[1] + short_taps[2, 2] * edges[0], short_taps[2, 2] * edges[1]]
    )
    first = jnp.pad(first, ((0, 6), (0, 0)))
    other = to_groups([first[:, chan // 2 :]])[0]
    both, _ = after((both, early))
    late = long_conv(both, head, back, skip, taps, place, 1, copies=groups)
    late, near = after((late, near))
    blocks = near + [swapped(n, 1) for n in near]
    early, late, other, first = after((exchanged(early), late, other, first))
    gated = gate(early, outer, first)
    sent = to_groups([gated])[0]
    dealt = lax.all_to_all(
        late.reshape(count * groups, step, rows), ("ctx", "ch"), 0, 0, tiled=True
    )
    dealt = dealt.reshape(count, groups, step, rows)
    total = own_term(here[None], gated, out_weight, cols)
    place = jnp.stack([here, position % 2])
    first = jnp.stack([first[:, chan // 2 :], other])
    return last_term(place, sent, dealt, first, total, outer, theirs, blocks, out_weight)


def solution(mesh):
    return jax.shard_map(
        local,
        mesh=mesh,
        in_specs=(
            P("ctx", None, "ch"),
            P(None, None, "ch"),
            P("ctx", "ch"),
            P("ch"),
            P("ch", None),
        ),
        out_specs=P("ctx", "ch"),
        check_vma=False,
    )
```

```python
import functools

import jax
import jax.numpy as jnp
import ml_dtypes
import numpy as np
from jax import lax
from jax.experimental import pallas as pl
from jax.experimental.pallas import tpu as pltpu
from jax.sharding import PartitionSpec as P

LANES = 128


def passed_along(value, axis, steps):
    count = lax.axis_size(axis)
    initial, last = (max(0, -steps), min(count, count - steps))
    return lax.ppermute(value, axis, [(source, source + steps) for source in range(initial, last)])


def paired_columns(half):
    order = np.arange(2 * half).reshape(2, half // LANES, LANES)
    return order.transpose(1, 0, 2).reshape(-1)


def head_table(size):
    half = size // 2
    rows = np.arange(half)[:, None]
    cols = np.arange(size)[None, :]
    freq = np.where(cols < half, cols, cols - half)
    angle = (rows * freq % size) * (2.0 * np.pi / size)
    nyquist = np.where(rows % 2 == 0, 1.0, -1.0)
    table = np.where(cols < half, np.cos(angle), np.where(cols == half, nyquist, -np.sin(angle)))
    return table[:, paired_columns(half)].astype(ml_dtypes.bfloat16)


def inverse_table(size):
    half = size // 2
    rows = np.arange(size)[:, None]
    places = half + np.arange(half)[None, :]
    freq = np.where(rows < half, rows, rows - half)
    angle = (places * freq % size) * (2.0 * np.pi / size)
    weight = np.where(freq == 0, 1.0, 2.0) / size
    nyquist = np.where(places % 2 == 0, 1.0, -1.0) / size
    table = np.where(
        rows < half, weight * np.cos(angle), np.where(rows == half, nyquist, -weight * np.sin(angle))
    )
    return table[paired_columns(half)].astype(ml_dtypes.bfloat16)


def call(kernel, in_specs, out_specs, outs, grid=(), scratch=(), megabytes=16, flops=0, moved=0, scalars=0, aliases=None):
    inner = pl.pallas_call(
        kernel,
        grid_spec=pltpu.PrefetchScalarGridSpec(
            num_scalar_prefetch=scalars,
            grid=grid,
            in_specs=in_specs,
            out_specs=out_specs,
            scratch_shapes=list(scratch),
        ),
        out_shape=[pltpu.HBM(shape, dtype) for shape, dtype in outs],
        input_output_aliases=aliases or {},
        compiler_params=pltpu.CompilerParams(vmem_limit_bytes=megabytes * 1024 * 1024),
        cost_estimate=pl.CostEstimate(flops=flops, bytes_accessed=moved, transcendentals=0),
    )

    def run(*args, free=()):
        pinned = [
            a if k < scalars or k in free else pltpu.with_memory_space_constraint(a, pltpu.HBM)
            for k, a in enumerate(args)
        ]
        return inner(*pinned)

    return run


def store_turned(value, o_ref):
    o_ref[...] = value.T.reshape(o_ref.shape).astype(o_ref.dtype)


def turn_kernel(x_ref, s_ref, o_ref, tail_ref):
    tail_ref[...] = s_ref[:, s_ref.shape[1] - 2 :]
    store_turned(x_ref[...].astype(jnp.float32), o_ref)


def turned(x, streams, count, parts):
    rows, chan = x.shape
    own = chan // count
    last = min(rows, 16)
    tile = chan // parts
    return call(
        turn_kernel,
        [
            pl.BlockSpec((rows, tile), lambda p: (0, p)),
            pl.BlockSpec((3, last, tile), lambda p: (0, rows // last - 1, p)),
        ],
        [
            pl.BlockSpec((count, 1, own // parts, rows), lambda p: (0, 0, p, 0)),
            pl.BlockSpec((3, 2, tile), lambda p: (0, 0, p)),
        ],
        [((count, 2, own, rows), x.dtype), ((3, 2, chan), streams.dtype)],
        grid=(parts,),
        moved=4 * rows * chan,
    )(x, streams)


def mixed(s_ref, e_ref, t_ref, q):
    rows, width = s_ref.shape[1:]
    place = lax.broadcasted_iota(jnp.int32, (8, width), 0)
    now = s_ref[q].astype(jnp.float32)
    edge = e_ref[q].astype(jnp.float32)
    one, two = (pltpu.roll(now, 1, 0), pltpu.roll(now, 2, 0))
    one_top = jnp.where(place == 0, edge[1:2], one[:8])
    two_top = jnp.where(place == 0, edge[0:1], jnp.where(place == 1, edge[1:2], two[:8]))
    one = jnp.concatenate([one_top, one[8:]], axis=0)
    two = jnp.concatenate([two_top, two[8:]], axis=0)
    return t_ref[0, q : q + 1] * now + t_ref[1, q : q + 1] * one + t_ref[2, q : q + 1] * two


def inner_kernel(s_ref, e_ref, t_ref, _, o_ref):
    store_turned(mixed(s_ref, e_ref, t_ref, 0) * mixed(s_ref, e_ref, t_ref, 1), o_ref)


def with_inner(both, streams, edges, taps, parts):
    count, _, own, rows = both.shape
    chan = count * own
    tile = chan // parts
    return call(
        inner_kernel,
        [
            pl.BlockSpec((2, rows, tile), lambda p: (0, 0, p)),
            pl.BlockSpec((3, 2, tile), lambda p: (0, 0, p)),
            pl.BlockSpec((3, 3, tile), lambda p: (0, 0, p)),
            pl.BlockSpec(memory_space=pl.ANY),
        ],
        [pl.BlockSpec((count, 1, own // parts, rows), lambda p: (0, 1, p, 0))],
        [(both.shape, both.dtype)],
        grid=(parts,),
        megabytes=32,
        moved=6 * rows * chan,
        aliases={3: 0},
    )(streams, edges, taps, both)[0]


def outer_kernel(s_ref, e_ref, t_ref, o_ref):
    o_ref[...] = mixed(s_ref, e_ref, t_ref, 0).astype(o_ref.dtype)


def outer_gate(streams, which, edges, taps, parts):
    _, rows, chan = streams.shape
    tile = chan // parts
    return call(
        outer_kernel,
        [
            pl.BlockSpec((1, rows, tile), lambda p: (which, 0, p)),
            pl.BlockSpec((1, 2, tile), lambda p: (0, 0, p)),
            pl.BlockSpec((3, 1, tile), lambda p: (0, 0, p)),
        ],
        [pl.BlockSpec((rows, tile), lambda p: (0, p))],
        [((rows, chan), jnp.bfloat16)],
        grid=(parts,),
        megabytes=32,
        moved=4 * rows * chan,
    )(streams, edges, taps)[0]


def deal_kernel(f_ref, s_ref, t_ref, o_ref, f_buf, s_buf, out_buf, sems):
    count, height, _, _ = out_buf.shape
    rows, chan = f_ref.shape
    step = chan // count // 2
    tile = chan // 4
    few = count // 2
    per = LANES // step // 2
    ins = []
    for q in range(4):
        lanes = pl.ds(q * tile, tile)
        ins.append(pltpu.make_async_copy(f_ref.at[:, lanes], f_buf.at[q], sems.at[2 * q]))
        ins.append(
            pltpu.make_async_copy(s_ref.at[pl.ds(0, 2), :, lanes], s_buf.at[q], sems.at[2 * q + 1])
        )
    for copy in ins:
        copy.start()
    outs, edges = ([], [])
    for q in range(4):
        p, owner = (q // 2, q % 2 * few)
        lanes = slice(q * tile, (q + 1) * tile)
        ins[2 * q].wait()
        values = [f_buf[q].astype(jnp.float32)]
        ins[2 * q + 1].wait()
        both = []
        for stream in range(2):
            now = s_buf[q, stream].astype(jnp.float32)
            value = t_ref[0, stream : stream + 1, lanes] * now
            value = value + t_ref[1, stream : stream + 1, lanes] * pltpu.roll(now, 1, 0)
            both.append(value + t_ref[2, stream : stream + 1, lanes] * pltpu.roll(now, 2, 0))
        values.append(both[0] * both[1])
        for k in range(2):
            value = values[k].astype(o_ref.dtype).T
            for c in range(rows // LANES):
                place = ((2 * p + k) * rows // LANES + c) * step // 8
                out_buf[owner : owner + few, place : place + step // 8] = value[
                    :, c * LANES : (c + 1) * LANES
                ].reshape(few, step // 8, 8, LANES)
        ends = [s_buf[q, k, a : a + 2].astype(jnp.float32) for a in (0, rows - 2) for k in range(2)]
        ends = jnp.concatenate(ends, axis=0)
        edges.append(ends)
        if p == 1:
            for g in range(few // per):
                lanes = slice(g * LANES // 2, (g + 1) * LANES // 2)
                value = jnp.concatenate([edges[q - 2][:, lanes], edges[q][:, lanes]], axis=1)
                first = owner + g * per
                out_buf[first : first + per, height - 1] = jnp.broadcast_to(
                    value[None].astype(o_ref.dtype), (per, 8, LANES)
                )
        some = (pl.ds(owner, few), pl.ds(p * (height // 2), height // 2))
        outs.append(pltpu.make_async_copy(out_buf.at[some], o_ref.at[some], sems.at[8 + q]))
        outs[q].start()
    some = pl.ds(height - 1, 1)
    outs.append(pltpu.make_async_copy(out_buf.at[:, some], o_ref.at[:, some], sems.at[12]))
    outs[4].start()
    for copy in outs:
        copy.wait()


def deal(filters, streams, taps, count):
    rows, chan = filters.shape
    shape = (count, chan // count * rows // LANES // 4 + 1, 8, LANES)
    anywhere, vmem = (pl.BlockSpec(memory_space=pl.ANY), pl.BlockSpec(memory_space=pltpu.VMEM))
    bf16 = jnp.bfloat16
    return call(
        deal_kernel,
        [anywhere, anywhere, vmem],
        [anywhere],
        [(shape, bf16)],
        scratch=[
            pltpu.VMEM((4, rows, chan // 4), bf16),
            pltpu.VMEM((4, 2, rows, chan // 4), bf16),
            pltpu.VMEM(shape, bf16),
            pltpu.SemaphoreType.DMA((13,)),
        ],
        megabytes=32,
        moved=10 * rows * chan,
    )(filters, streams, taps)[0]


def first_tokens(ends, taps):
    count = ends.shape[0]

    def at(row):
        return ends[:, row].astype(jnp.float32)

    block = lax.broadcasted_iota(jnp.int32, (count, LANES), 0)

    def before(row):
        return jnp.where(block == 0, 0.0, pltpu.roll(at(row), 1, 0))

    values = [1.0, 1.0]
    for q in range(2):
        t0, t1, t2 = (taps[2 * m + q : 2 * m + q + 1] for m in range(3))
        one, two = (at(2 * q), at(2 * q + 1))
        far, near = (before(4 + 2 * q), before(5 + 2 * q))
        values[0] = values[0] * (t0 * one + t1 * near + t2 * far)
        values[1] = values[1] * (t0 * two + t1 * one + t2 * near)
    rest = jnp.zeros((LANES - 2 * count, LANES), jnp.float32)
    return jnp.concatenate(values + [rest], axis=0).T


def conv_kernel(split, place_ref, both_ref, head_ref, back_ref, skip_ref, taps_ref, o_ref, *scratch):
    head_buf, back_buf, spec_ref, factor_ref, low_ref, x_buf, fix_ref, sems = scratch
    count, _, part, rows = o_ref.shape
    tiles = rows // LANES
    high = min(part, 16)
    group = 2
    low = part * (split or 0)
    copies = [
        pltpu.make_async_copy(
            head_ref.at[:, pl.ds(t * 2 * LANES, 2 * LANES)], head_buf.at[t], sems.at[t]
        )
        for t in range(tiles)
    ]
    copies.append(pltpu.make_async_copy(back_ref, back_buf, sems.at[tiles]))
    for copy in copies:
        copy.start()
    height = count * part

    def arrived(kind):
        if split is None:
            return both_ref[:, kind * part : (kind + 1) * part].reshape(height, rows)
        first = (2 * split + kind) * tiles
        places = [(first + c) * part // 8 for c in range(tiles)]
        pieces = [both_ref[:, a : a + part // 8].reshape(height, LANES) for a in places]
        return jnp.concatenate(pieces, axis=1)

    x_buf[...] = arrived(1).reshape(count, part, rows)
    if split is not None:
        ends = both_ref[:, both_ref.shape[1] - 1]
        fix_ref[...] = first_tokens(ends, taps_ref[...])
        first = split * (LANES // 2) + place_ref[0] * part
        mine = fix_ref[pl.ds(pl.multiple_of(first, part), part), :]
        lane = lax.broadcasted_iota(jnp.int32, (part, LANES), 1)
        for block in range(count):
            one = pltpu.roll(mine, (LANES - block) % LANES, 1)
            two = pltpu.roll(mine, (LANES - block - count + 1) % LANES, 1)
            value = x_buf[block, :, :LANES].astype(jnp.float32)
            value = jnp.where(lane == 0, one, jnp.where(lane == 1, two, value))
            x_buf[block, :, :LANES] = value.astype(x_buf.dtype)
    filters = arrived(0)
    odd = lax.broadcasted_iota(jnp.int32, (height, 2 * LANES), 1) % 2 == 1
    lane = lax.broadcasted_iota(jnp.int32, (high, LANES), 1)

    lane0 = lax.broadcasted_iota(jnp.int32, (height, LANES), 1) == 0

    def spectra(t):
        value = jnp.dot(filters, head_buf[t], preferred_element_type=jnp.float32)
        earlier = jnp.concatenate([jnp.zeros_like(value[:part]), value[:-part]], axis=0)
        window = earlier + jnp.where(odd, -value, value)
        real, imag = (window[:, :LANES], window[:, LANES:])
        factor_ref[t, :, :LANES] = real
        less, more = (imag - real, real + imag)
        if t == 0:
            less, more = (jnp.where(lane0, real, less), jnp.where(lane0, imag, more))
        factor_ref[t, :, LANES : 2 * LANES] = less
        factor_ref[t, :, 2 * LANES :] = more
        spec_ref[t] = jnp.dot(
            x_buf[...].reshape(height, rows), head_buf[t], preferred_element_type=jnp.float32
        )

    def products(t, slab):
        base = slab * high
        if not isinstance(base, int):
            base = pl.multiple_of(base, high)
        for start in range(0, count, group):
            sums = [[None] * 3 for _ in range(group)]
            factors = {}
            for source in range(start + group):
                place = pl.ds(base + source * part, high)
                real, imag = (spec_ref[t, place, :LANES], spec_ref[t, place, LANES:])
                both = real + imag
                for g in range(group):
                    lag = start + g - source
                    if lag < 0:
                        continue
                    if lag not in factors:
                        place = pl.ds(base + lag * part, high)
                        factors[lag] = [
                            factor_ref[t, place, c * LANES : (c + 1) * LANES] for c in range(3)
                        ]
                    a, b, c = factors[lag]
                    terms = (both * a, real * b, imag * c)
                    before = sums[g]
                    sums[g] = [u if p is None else p + u for p, u in zip(before, terms)]
            for g in range(group):
                a, b, c = sums[g]
                place = pl.ds(base + (start + g) * part, high)
                re, im = (a - c, a + b)
                if t == 0:
                    re, im = (jnp.where(lane == 0, b, re), jnp.where(lane == 0, c, im))
                low_ref[place, t * 2 * LANES : t * 2 * LANES + LANES] = re.astype(low_ref.dtype)
                low_ref[place, t * 2 * LANES + LANES : (t + 1) * 2 * LANES] = im.astype(low_ref.dtype)

    for copy in copies:
        copy.wait()
    for t in range(tiles):
        spectra(t)
        if split is not None:
            for slab in range(part // high):
                products(t, slab)
        else:

            def one_slab(slab, carry, t=t):
                products(t, slab)
                return carry

            lax.fori_loop(0, part // high, one_slab, 0)
    back = jnp.dot(
        low_ref[...].astype(jnp.bfloat16), back_buf[...], preferred_element_type=jnp.float32
    )
    value = back.reshape(count, part, rows)
    skip = skip_ref[low : low + part, :1][None]
    value = value + skip * x_buf[...].astype(jnp.float32)
    for copy in range(o_ref.shape[1]):
        o_ref[:, copy] = value.astype(o_ref.dtype)


def long_conv(both, head, back, skip, taps, place, split, copies=1):
    count, rows = (both.shape[0], head.shape[0])
    own = skip.shape[0]
    part = own if split is None else own // 2
    height = count * part
    vmem, anywhere = (pl.BlockSpec(memory_space=pltpu.VMEM), pl.BlockSpec(memory_space=pl.ANY))
    return call(
        functools.partial(conv_kernel, split),
        [pl.BlockSpec(memory_space=pltpu.SMEM), vmem, anywhere, anywhere, vmem, vmem],
        [vmem],
        [((count, copies, part, rows), jnp.bfloat16)],
        scratch=[
            pltpu.VMEM((rows // LANES, rows, 2 * LANES), jnp.bfloat16),
            pltpu.VMEM(back.shape, jnp.bfloat16),
            pltpu.VMEM((rows // LANES, height, 2 * LANES), jnp.float32),
            pltpu.VMEM((rows // LANES, height, 3 * LANES), jnp.float32),
            pltpu.VMEM((height, 2 * rows), jnp.float32 if part % 16 else jnp.bfloat16),
            pltpu.VMEM((count, part, rows), jnp.bfloat16),
            pltpu.VMEM((LANES, LANES), jnp.float32),
            pltpu.SemaphoreType.DMA((rows // LANES + 1,)),
        ],
        megabytes=28,
        flops=12 * height * rows * rows,
        moved=height * rows * 8,
    )(place, both, head, back, skip, taps, free=(0, 1))[0]


def gated_part(long, outer, first):
    count, step, rows = long.shape
    value = long.reshape(count * step, rows).T.astype(jnp.float32)
    outer = outer.astype(jnp.float32)
    outer = jnp.concatenate([outer[:8] + first, outer[8:]], axis=0)
    return (outer * value).astype(jnp.bfloat16)


def gate_kernel(long_ref, outer_ref, first_ref, o_ref):
    o_ref[...] = gated_part(long_ref[...], outer_ref[...], first_ref[...])


def gate(long, outer, first):
    rows = outer.shape[0]
    width = long.shape[0] * long.shape[1]
    return call(
        gate_kernel,
        [
            pl.BlockSpec(long.shape, lambda n: (0, 0, 0)),
            pl.BlockSpec((rows, width), lambda n: (0, 0)),
            pl.BlockSpec((8, width), lambda n: (0, 0)),
        ],
        [pl.BlockSpec((rows, width), lambda n: (0, 0))],
        [((rows, width), jnp.bfloat16)],
        grid=(1,),
        moved=6 * rows * width,
    )(long, outer, first, free=(0,))[0]


def own_kernel(here_ref, gated_ref, weight_ref, o_ref):
    value = jnp.dot(gated_ref[...], weight_ref[...], preferred_element_type=jnp.float32)
    o_ref[...] = value.astype(o_ref.dtype)


def own_term(here, gated, out_weight, cols):
    rows, used = gated.shape
    wide = cols // 2
    return call(
        own_kernel,
        [
            pl.BlockSpec((rows, used), lambda n, h: (0, 0)),
            pl.BlockSpec((used, wide), lambda n, h: (0, h[0] * 2 + n)),
        ],
        [pl.BlockSpec((rows, wide), lambda n, h: (0, n))],
        [((rows, cols), jnp.bfloat16)],
        grid=(2,),
        flops=2 * rows * used * cols,
        moved=rows * cols * 2 + used * cols * 2,
        scalars=1,
    )(here, gated, out_weight)[0]


def last_kernel(
    place_ref, sent_ref, dealt_ref, first_ref, sum_ref, mine_ref, theirs_ref, *refs
):
    blocks, (weight_ref, o_ref, *scratch) = (refs[:4], refs[4:])
    outer_buf, weight_buf, block_buf, sum_buf, out_buf, gated_ref, sems = scratch
    here, core = (place_ref[0], place_ref[1])
    rows, used = outer_buf.shape[1:]
    wide = out_buf.shape[2]
    cols = 4 * wide
    pairs = [(mine_ref.at[:, pl.ds(used, used)], outer_buf.at[0]), (theirs_ref, outer_buf.at[1])]
    gates = [pltpu.make_async_copy(a, b, sems.at[g]) for g, (a, b) in enumerate(pairs)]
    for copy in gates:
        copy.start()
    places, inputs = ([], [])
    for k in range(4):
        column = pl.multiple_of((2 * (core ^ k // 2) + k % 2) * wide, wide)
        places.append(pl.ds(column, wide))
        ours = pl.multiple_of(here * cols + column, wide)
        pairs = [
            (blocks[k], block_buf.at[k]),
            (weight_ref.at[pl.ds(used, used), pl.ds(ours, wide)], weight_buf.at[k]),
            (sum_ref.at[:, places[k]], sum_buf.at[k]),
        ]
        inputs.append(
            [pltpu.make_async_copy(a, b, sems.at[2 + 3 * k + i]) for i, (a, b) in enumerate(pairs)]
        )
        for copy in inputs[k]:
            copy.start()
    for g in range(2):
        gates[g].wait()
        long = dealt_ref[:, here if g == 0 else 1 - here]
        gated_ref[g] = gated_part(long, outer_buf[g], first_ref[g])
    outputs = []
    for k in range(4):
        if k < 3:
            for copy in inputs[k] + (inputs[3] if k == 2 else []):
                copy.wait()
        value = sum_buf[k].astype(jnp.float32)
        for left, right in (
            (sent_ref[...], block_buf[k, :used]),
            (gated_ref[1], block_buf[k, used:]),
            (gated_ref[0], weight_buf[k]),
        ):
            value = value + jnp.dot(left, right, preferred_element_type=jnp.float32)
        out_buf[k] = value.astype(out_buf.dtype)
        outputs.append(pltpu.make_async_copy(out_buf.at[k], o_ref.at[:, places[k]], sems.at[14 + k]))
        outputs[k].start()
    for copy in outputs:
        copy.wait()


def last_term(place, sent, dealt, first, total, mine, theirs, blocks, out_weight):
    rows, cols = total.shape
    chan = mine.shape[1]
    wide = cols // 4
    used = chan // 2
    vmem, anywhere = (pl.BlockSpec(memory_space=pltpu.VMEM), pl.BlockSpec(memory_space=pl.ANY))
    bf16 = jnp.bfloat16
    return call(
        last_kernel,
        [pl.BlockSpec(memory_space=pltpu.SMEM), vmem, vmem, vmem] + [anywhere] * 8,
        [anywhere],
        [((rows, cols), bf16)],
        scratch=[
            pltpu.VMEM((2, rows, used), bf16),
            pltpu.VMEM((4, used, wide), bf16),
            pltpu.VMEM((4, chan, wide), bf16),
            pltpu.VMEM((4, rows, wide), bf16),
            pltpu.VMEM((4, rows, wide), bf16),
            pltpu.VMEM((2, rows, used), bf16),
            pltpu.SemaphoreType.DMA((18,)),
        ],
        megabytes=32,
        flops=24 * rows * used * wide,
        moved=rows * wide * 16 + used * wide * 24,
    )(place, sent, dealt, first, total, mine, theirs, *blocks, out_weight, free=(0, 1, 2, 3))[0]


def exchanged(value):
    return lax.all_to_all(value, "ctx", 0, 0, tiled=True)


def to_groups(values):
    groups = lax.axis_size("ch")
    return [
        lax.ppermute(value, "ch", [(g, (g + s) % groups) for g in range(groups)])
        for s, value in enumerate(values, 1)
    ]


def any_groups(long, outer, out_weight):
    rows, chan = outer.shape
    groups = lax.axis_size("ch")
    here = lax.axis_index("ch")
    cols = out_weight.shape[1] // groups
    gated = gated_part(long, outer, jnp.zeros((8, chan), jnp.float32))
    total = jnp.zeros((rows, cols), jnp.float32)
    weights = [
        lax.dynamic_slice(out_weight, (0, (here + s) % groups * cols), (chan, cols))
        for s in range(groups)
    ]
    values = [gated] + to_groups([gated] * (groups - 1))
    for value, weight in zip(values, weights[:1] + to_groups(weights[1:])):
        total = total + jnp.dot(value, weight, preferred_element_type=jnp.float32)
    return total.astype(jnp.bfloat16)


def local(streams, short_taps, filters, skip_gain, out_weight):
    rows, _, chan = streams.shape
    count = lax.axis_size("ctx")
    groups = lax.axis_size("ch")
    own = chan // count
    step = own // 2
    fast = groups == 2 and count % 4 == 0 and own % 32 == 0 and count % 2 == 0 and LANES % (2 * step) == 0
    fast = fast and rows % LANES == 0 and 2 * count <= LANES and chan % (4 * LANES) == 0
    after = lax.optimization_barrier
    position, here = (lax.axis_index("ctx"), lax.axis_index("ch"))
    head = jnp.asarray(head_table(2 * rows))
    back = jnp.asarray(inverse_table(2 * rows))
    streams = streams.transpose(1, 0, 2)
    parts = 2 if fast else 1
    skip = skip_gain.reshape(parts, count, own // parts)
    skip = lax.dynamic_index_in_dim(skip, position, 1, False)
    skip = jnp.broadcast_to(skip.reshape(own, 1), (own, LANES))
    if not fast:
        both, tail = turned(filters, streams, count, parts)
        edges = passed_along(tail, "ctx", 1)
        both = exchanged(with_inner(both, streams, edges, short_taps, parts))
        both = both.reshape(count, 2 * own, rows)
        outer = outer_gate(streams, 2, edges[2:], short_taps[:, 2:], parts)
        none = jnp.zeros((8, LANES), jnp.float32)
        long = long_conv(both, head, back, skip, none, jnp.zeros((1,), jnp.int32), None)
        return any_groups(exchanged(long[:, 0]), outer, out_weight)
    per = LANES // step // 2
    place = (position % per)[None]
    taps = short_taps[:, :2].reshape(6, 2, chan // 2)
    taps = lax.dynamic_slice(taps, (0, 0, position // per * (LANES // 2)), (6, 2, LANES // 2))
    taps = jnp.pad(taps.reshape(6, LANES), ((0, 2), (0, 0)))
    both = exchanged(deal(filters, streams, short_taps, count))
    cols = out_weight.shape[1] // groups
    wide = cols // 4
    columns = [(1 - here) * cols + (position % 2 * 2 + k) * wide for k in range(2)]
    near = [lax.dynamic_slice(out_weight, (0, c), (chan, wide)) for c in columns]
    near, none = after((near, jnp.zeros((1, 2, chan), jnp.float32)))
    outer = outer_gate(streams, 2, none, short_taps[:, 2:], 2)
    theirs = to_groups([outer[:, chan // 2 :]])[0]
    near, skip, taps = after((near, skip, taps))
    near, tail = after((near, streams[2, rows - 2 :]))
    near = [to_groups([n])[0] for n in near]

    def swapped(value, bit):
        return lax.ppermute(value, "ctx", [(i, i ^ bit) for i in range(count)])

    both, outer, theirs = after((both, outer, theirs))
    early = long_conv(both, head, back, skip, taps, place, 0)[:, 0]
    edges, early = after((passed_along(tail, "ctx", 1), early))
    edges = edges.astype(jnp.float32)
    first = jnp.stack(
        [short_taps[1, 2] * edges[1] + short_taps[2, 2] * edges[0], short_taps[2, 2] * edges[1]]
    )
    first = jnp.pad(first, ((0, 6), (0, 0)))
    other = to_groups([first[:, chan // 2 :]])[0]
    both, _ = after((both, early))
    late = long_conv(both, head, back, skip, taps, place, 1, copies=groups)
    late, near = after((late, near))
    blocks = near + [swapped(n, 1) for n in near]
    early, late, other, first = after((exchanged(early), late, other, first))
    gated = gate(early, outer, first)
    sent = to_groups([gated])[0]
    dealt = lax.all_to_all(
        late.reshape(count * groups, step, rows), ("ctx", "ch"), 0, 0, tiled=True
    )
    dealt = dealt.reshape(count, groups, step, rows)
    total = own_term(here[None], gated, out_weight, cols)
    place = jnp.stack([here, position % 2])
    first = jnp.stack([first[:, chan // 2 :], other])
    return last_term(place, sent, dealt, first, total, outer, theirs, blocks, out_weight)


def solution(mesh):
    return jax.shard_map(
        local,
        mesh=mesh,
        in_specs=(
            P("ctx", None, "ch"),
            P(None, None, "ch"),
            P("ctx", "ch"),
            P("ch"),
            P("ch", None),
        ),
        out_specs=P("ctx", "ch"),
        check_vma=False,
    )
```
